32 devices in a mesh: ctx: 4 (over z), head: 2 (over y), seq: 4 (over x, core).
Axes of the slice: x: 2, y: 2, z: 4, core: 2. Of those that a mesh axis runs over, the one named last changes fastest.
Arguments:
- x_heads: bfloat16 [4, 16, 1024, 128], P('seq', 'head', 'ctx'), may hold values from -6 to 6
- target: bfloat16 [4, 16, 1024, 128], P('seq', 'head', 'ctx'), may hold values from -6 to 6
- b_proj: bfloat16 [4, 1024, 128], P('seq', 'ctx'), may hold values from -6 to 6
- c_proj: bfloat16 [4, 1024, 128], P('seq', 'ctx'), may hold values from -0.5 to 0.5
- dt_raw: float32 [4, 16, 1024], P('seq', 'head', 'ctx'), may hold values from -1.2 to 1.2
- a_log: float32 [16], P('head'), as said below
- skip_gain: float32 [16], P('head'), may hold values from 0.5 to 1.5
- dt_bias: float32 [16], P('head'), may hold values from -4.5 to -3.5
Outputs:
- grad_x: bfloat16 [4, 16, 1024, 128], P('seq', 'head', 'ctx')
- grad_b: float32 [4, 1024, 128], P('seq', ('ctx', 'head'))
- grad_c: float32 [4, 1024, 128], P('seq', ('ctx', 'head'))
- grad_dt_raw: float32 [4, 16, 1024], P('seq', 'head', 'ctx')
- grad_a_log: float32 [16], P('head')
- grad_skip: float32 [16], P('head')
- grad_dt_bias: float32 [16], P('head')
The draws below stay inside these ranges and needn't reach their ends.
Inputs may be any that keep to these rules, and one draw needn't show every extreme that they name: exp(a_log) lies between 16 / 1024 and 3.
All inputs are finite; a program needn't handle non-finite values.
Results may differ from the reference program's by a relative error of at most 0.0054.
Values sent between devices are 32-bit elements; how exact they have to be, the bound alone decides.
No kernel may reach another device: no remote copies, remote signals or barrier semaphores. Data moves between devices by JAX's collectives and lax.ppermute only.
A program may use at most 64 MiB of HBM per device.

```python
import math
from functools import partial
import jax
import jax.numpy as jnp
from jax import lax

P_SIZE = 128
N = 128
GROUP = 256
HEADS = 16
SEQUENCE_LENGTH = 1024
SEQS = 4


def draw_a_log(key, part):
    pick_key, slow_key, fast_key = jax.random.split(jax.random.fold_in(key, 11), 3)
    slow_heads = jax.random.bernoulli(pick_key, 0.5, (HEADS,))
    slow_values = jax.random.uniform(slow_key, (HEADS,), jnp.float32, math.log(16.0) - math.log(SEQUENCE_LENGTH), math.log(48.0) - math.log(SEQUENCE_LENGTH))
    fast_values = jax.random.uniform(fast_key, (HEADS,), jnp.float32, math.log(0.5), math.log(3.0))
    return jnp.where(slow_heads, slow_values, fast_values)


def draw_dt_raw(key, part):
    baseline_random_key, jitter_random_key = jax.random.split(jax.random.fold_in(key, 23), 2)
    complete_shape = (SEQS, HEADS, SEQUENCE_LENGTH)
    baseline_values = jax.random.uniform(baseline_random_key, (SEQS, HEADS, SEQUENCE_LENGTH // GROUP, 1), jnp.float32, -0.7, 0.7)
    baseline_values = jnp.broadcast_to(baseline_values, (SEQS, HEADS, SEQUENCE_LENGTH // GROUP, GROUP)).reshape(complete_shape)
    jitter_component = jnp.clip(0.4 * jax.random.normal(jitter_random_key, complete_shape, jnp.float32), -0.8, 0.8)
    return jnp.clip(baseline_values + jitter_component, -1.2, 1.2)


def levels(stream_key, dims, shards, smallest, high):
    factor_of = 1.0
    for axis_at, shards_of in shards:
        heights = jax.random.uniform(jax.random.fold_in(jax.random.fold_in(stream_key, 6), axis_at), (shards_of,), jnp.float32, smallest / len(shards), high / len(shards))
        factor_of = factor_of * jnp.repeat(jnp.exp(heights), dims[axis_at] // shards_of).reshape((-1,) + (1,) * (len(dims) - 1 - axis_at))
    return factor_of


def gaussian(own_key, extent, spread, limit, shards=(), held_as=jnp.bfloat16):
    level = levels(own_key, extent, shards, -0.22, 0.18) if shards else 1.0
    entries = jax.random.normal(own_key, extent, jnp.float32) * spread * level
    return jnp.minimum(jnp.maximum(entries, -limit), limit).astype(held_as)


def setup_inputs(seed: int = 0) -> dict:
    arg_keys = jax.random.split(jax.random.key(seed), 9)
    x_heads = gaussian(arg_keys[0], (SEQS, HEADS, SEQUENCE_LENGTH, P_SIZE), 1.0, 6.0, ((0, 4), (1, 2), (2, 4)))
    target = gaussian(arg_keys[1], (SEQS, HEADS, SEQUENCE_LENGTH, P_SIZE), 1.0, 6.0, ((0, 4), (1, 2), (2, 4)))
    b_proj = gaussian(arg_keys[2], (SEQS, SEQUENCE_LENGTH, N), 1.0, 6.0, ((0, 4), (1, 4)))
    c_proj = gaussian(arg_keys[3], (SEQS, SEQUENCE_LENGTH, N), N ** -0.5, 0.5, ((0, 4), (1, 4)))
    dt_raw = draw_dt_raw(jax.random.fold_in(arg_keys[8], 71), 0)
    a_log = draw_a_log(jax.random.fold_in(arg_keys[8], 71), 0)
    skip_gain = jnp.clip(0.5 + 1.0 * jax.random.uniform(arg_keys[6], (HEADS,), jnp.float32) ** levels(arg_keys[6], (HEADS,), ((0, 2),), -0.2, 0.2), 0.5, 1.5)
    dt_bias = jnp.clip(-4.5 + 1.0 * jax.random.uniform(arg_keys[7], (HEADS,), jnp.float32) ** levels(arg_keys[7], (HEADS,), ((0, 2),), -0.2, 0.2), -4.5, -3.5)
    return dict(x_heads=x_heads, target=target, b_proj=b_proj, c_proj=c_proj, dt_raw=dt_raw, a_log=a_log, skip_gain=skip_gain, dt_bias=dt_bias)


highest = lax.Precision.HIGHEST


def block_logs(dt_block, decay_rate):
    return jnp.cumsum(-decay_rate[:, None] * dt_block, axis=-1)


def state_part(x_block, b_block, dt_block, log_decay):
    weights = jnp.exp(log_decay[:, -1:] - log_decay) * dt_block
    scaled = (x_block.astype(jnp.float32) * weights[:, :, None]).astype(jnp.bfloat16)
    contrib = jnp.einsum("hjp,jn->hpn", scaled, b_block, preferred_element_type=jnp.float32)
    return weights, scaled, contrib, jnp.exp(log_decay[:, -1])


def intra_parts(b_block, c_block, dt_block, log_decay):
    block_size = log_decay.shape[-1]
    row_ids = lax.broadcasted_iota(jnp.int32, (block_size, block_size), 0)
    column_ids = lax.broadcasted_iota(jnp.int32, (block_size, block_size), 1)
    causal = (row_ids >= column_ids)[None]
    log_gaps = log_decay[:, :, None] - log_decay[:, None, :]
    decays = jnp.where(causal, jnp.exp(jnp.where(causal, log_gaps, 0.0)), 0.0)
    scores = jnp.einsum("in,jn->ij", c_block, b_block, preferred_element_type=jnp.float32)
    mixing = (scores[None] * decays * dt_block[:, None, :]).astype(jnp.bfloat16)
    return decays, scores, mixing


def forward_block(x_block, t_block, c_block, log_decay, skip_gain, start_state, mixing):
    inner = jnp.einsum("hij,hjp->hip", mixing, x_block, preferred_element_type=jnp.float32)
    state_low = start_state.astype(jnp.bfloat16)
    growth = jnp.exp(log_decay)[:, :, None]
    carried = jnp.einsum("in,hpn->hip", c_block, state_low, preferred_element_type=jnp.float32) * growth
    out_error = inner + carried + skip_gain[:, None, None] * x_block.astype(jnp.float32) - t_block.astype(jnp.float32)
    error_weighted = (out_error * growth).astype(jnp.bfloat16)
    pulled = jnp.einsum("hip,in->hpn", error_weighted, c_block, preferred_element_type=jnp.float32)
    return out_error, carried, error_weighted, state_low, pulled


def backward_local(x_block, b_block, c_block, dt_block, skip_gain, out_error, carried, error_weighted, state_low, decays, scores, mixing):
    error_low = out_error.astype(jnp.bfloat16)
    grad_mixing = jnp.einsum("hip,hjp->hij", error_low, x_block, preferred_element_type=jnp.float32)
    grad_in = jnp.einsum("hij,hip->hjp", mixing, error_low, preferred_element_type=jnp.float32) + skip_gain[:, None, None] * out_error
    masked = grad_mixing * decays
    grad_score = (masked * dt_block[:, None, :]).astype(jnp.bfloat16)
    grad_c = jnp.einsum("hij,jn->in", grad_score, b_block, preferred_element_type=jnp.float32)
    grad_c = grad_c + jnp.einsum("hip,hpn->in", error_weighted, state_low, preferred_element_type=jnp.float32)
    grad_b = jnp.einsum("hij,in->jn", grad_score, c_block, preferred_element_type=jnp.float32)
    product = masked * scores[None]
    column_sum = jnp.sum(product, axis=1)
    row_sum = jnp.einsum("hij,hj->hi", product, dt_block, precision=highest)
    grad_logs = row_sum - column_sum * dt_block + jnp.sum(out_error * carried, axis=-1)
    grad_skip = jnp.sum(out_error * x_block.astype(jnp.float32), axis=(1, 2))
    return grad_in, grad_c, grad_b, column_sum, grad_logs, grad_skip


def backward_state(x_block, b_block, log_decay, weights, scaled, start_state, end_adjoint):
    adjoint_low = end_adjoint.astype(jnp.bfloat16)
    grad_b = jnp.einsum("hjp,hpn->jn", scaled, adjoint_low, preferred_element_type=jnp.float32)
    grad_scaled = jnp.einsum("jn,hpn->hjp", b_block, adjoint_low, preferred_element_type=jnp.float32)
    grad_in = grad_scaled * weights[:, :, None]
    grad_weight = jnp.sum(grad_scaled * x_block.astype(jnp.float32), axis=-1)
    grad_step = grad_weight * jnp.exp(log_decay[:, -1:] - log_decay)
    grad_logs = -grad_weight * weights
    grad_final = jnp.sum(grad_weight * weights, axis=-1) + jnp.exp(log_decay[:, -1]) * jnp.sum(end_adjoint * start_state, axis=(1, 2))
    return grad_in, grad_b, grad_step, grad_logs, grad_final


def finish_block(column_sum, grad_logs_a, grad_step_b, grad_logs_b, grad_final, dt_block, decay_rate):
    grad_logs = grad_logs_a + grad_logs_b
    grad_logs = grad_logs.at[:, -1].add(grad_final)
    grad_log_rate = jnp.flip(jnp.cumsum(jnp.flip(grad_logs, axis=-1), axis=-1), axis=-1)
    grad_step = column_sum + grad_step_b - decay_rate[:, None] * grad_log_rate
    grad_alog = -decay_rate * jnp.sum(grad_log_rate * dt_block, axis=-1)
    return grad_step, grad_alog


def one_sequence(decay_rate, skip_gain, dt_bias, seq_items):
    x_seq, t_seq, b_seq, c_seq, raw_seq = seq_items
    head_count, positions, head_size = x_seq.shape
    state_size = b_seq.shape[-1]
    block_count = positions // GROUP
    step_sizes = jax.nn.softplus(raw_seq + dt_bias[:, None])
    x_blocks = jnp.swapaxes(x_seq.reshape(head_count, block_count, GROUP, head_size), 0, 1)
    t_blocks = jnp.swapaxes(t_seq.reshape(head_count, block_count, GROUP, head_size), 0, 1)
    b_blocks = b_seq.reshape(block_count, GROUP, state_size)
    c_blocks = c_seq.reshape(block_count, GROUP, state_size)
    dt_blocks = jnp.swapaxes(step_sizes.reshape(head_count, block_count, GROUP), 0, 1)
    zero_state = jnp.zeros((head_count, head_size, state_size), jnp.float32)

    def forward(carry_state, block_items):
        x_block, t_block, b_block, c_block, dt_block = block_items
        log_decay = block_logs(dt_block, decay_rate)
        weights, scaled, contrib, decay_total = state_part(x_block, b_block, dt_block, log_decay)
        decays, scores, mixing = intra_parts(b_block, c_block, dt_block, log_decay)
        outputs = forward_block(x_block, t_block, c_block, log_decay, skip_gain, carry_state, mixing)
        return decay_total[:, None, None] * carry_state + contrib, (carry_state, outputs[4], decay_total)

    final_state, (start_states, pulled_all, decay_totals) = lax.scan(forward, zero_state, (x_blocks, t_blocks, b_blocks, c_blocks, dt_blocks))

    def reverse_chain(adjoint, chain_items):
        decay_total, pulled = chain_items
        return decay_total[:, None, None] * adjoint + pulled, adjoint

    first_adjoint, end_adjoints = lax.scan(reverse_chain, zero_state, (decay_totals, pulled_all), reverse=True)

    def gradients(block_items):
        x_block, t_block, b_block, c_block, dt_block, start_state, end_adjoint = block_items
        log_decay = block_logs(dt_block, decay_rate)
        weights, scaled, contrib, decay_total = state_part(x_block, b_block, dt_block, log_decay)
        decays, scores, mixing = intra_parts(b_block, c_block, dt_block, log_decay)
        out_error, carried, error_weighted, state_low, pulled = forward_block(x_block, t_block, c_block, log_decay, skip_gain, start_state, mixing)
        grad_in_a, grad_c, grad_b_a, column_sum, grad_logs_a, grad_skip = backward_local(x_block, b_block, c_block, dt_block, skip_gain, out_error, carried, error_weighted, state_low, decays, scores, mixing)
        grad_in_b, grad_b_b, grad_step_b, grad_logs_b, grad_final = backward_state(x_block, b_block, log_decay, weights, scaled, start_state, end_adjoint)
        grad_step, grad_alog = finish_block(column_sum, grad_logs_a, grad_step_b, grad_logs_b, grad_final, dt_block, decay_rate)
        return (grad_in_a + grad_in_b).astype(jnp.bfloat16), grad_b_a + grad_b_b, grad_c, grad_step, grad_alog, grad_skip

    results = lax.map(gradients, (x_blocks, t_blocks, b_blocks, c_blocks, dt_blocks, start_states, end_adjoints))
    grad_x = jnp.swapaxes(results[0], 0, 1).reshape(head_count, positions, head_size)
    grad_b = results[1].reshape(positions, state_size)
    grad_c = results[2].reshape(positions, state_size)
    grad_step = jnp.swapaxes(results[3], 0, 1).reshape(head_count, positions)
    grad_raw = grad_step * jax.nn.sigmoid(raw_seq + dt_bias[:, None])
    return grad_x, grad_b, grad_c, grad_raw, jnp.sum(results[4], axis=0), jnp.sum(results[5], axis=0), jnp.sum(grad_raw, axis=1)


def reference(x_heads, target, b_proj, c_proj, dt_raw, a_log, skip_gain, dt_bias):
    decay_rate = jnp.exp(a_log)
    results = lax.map(partial(one_sequence, decay_rate, skip_gain, dt_bias), (x_heads, target, b_proj, c_proj, dt_raw))
    token_total = x_heads.shape[0] * x_heads.shape[2]
    grad_a_log = jnp.sum(results[4], axis=0) / token_total
    grad_skip = jnp.sum(results[5], axis=0) / (token_total * x_heads.shape[3])
    grad_dt_bias = jnp.sum(results[6], axis=0) / token_total
    return results[0], results[1], results[2], results[3], grad_a_log, grad_skip, grad_dt_bias
```

```python
import functools
import jax
import jax.numpy as jnp
from jax import lax
from jax.experimental import pallas as pl
from jax.experimental.pallas import tpu as pltpu
from jax.sharding import PartitionSpec as P

CHUNKS = 2
f32, bf16 = jnp.float32, jnp.bfloat16
highest = lax.Precision.HIGHEST
VMEM = pl.BlockSpec(memory_space=pltpu.VMEM)
SMEM = pl.BlockSpec(memory_space=pltpu.SMEM)
LIMIT = 48 * 1024 * 1024


def dot(a, b):
    return jnp.dot(a, b, preferred_element_type=f32)


def dot_nt(a, b):
    return lax.dot_general(a, b, (((1,), (1,)), ((), ())), preferred_element_type=f32)


def call(body, outs, *args, flops=0):
    return pl.pallas_call(
        body,
        out_shape=outs,
        in_specs=[SMEM if a.ndim == 1 else VMEM for a in args],
        out_specs=jax.tree.map(lambda _: VMEM, outs),
        compiler_params=pltpu.CompilerParams(vmem_limit_bytes=LIMIT),
        cost_estimate=pl.CostEstimate(flops=flops, bytes_accessed=1 << 20, transcendentals=0),
    )(*args)


def head_row(values, width):
    lanes = lax.broadcasted_iota(jnp.int32, (1, width), 1)
    row = jnp.zeros((1, width), f32)
    for h in range(values.shape[0]):
        row = jnp.where(lanes == h, values[h], row)
    return row


def steps_of(raw, bias, rate, width):
    heads, size = raw.shape
    columns = jnp.concatenate([raw, jnp.zeros((width - heads, size), f32)], axis=0).T
    shifted = columns + bias
    dt = jnp.maximum(shifted, 0.0) + jnp.log1p(jnp.exp(-jnp.abs(shifted)))
    rows = lax.broadcasted_iota(jnp.int32, (size, size), 0)
    cols = lax.broadcasted_iota(jnp.int32, (size, size), 1)
    lower = jnp.where(rows >= cols, 1.0, 0.0).astype(f32)
    logs = jnp.dot(lower, -rate * dt, precision=highest, preferred_element_type=f32)
    return shifted, dt, logs, 0.5 * logs[size - 1 : size, :]


def masked_scores(b, c):
    size = b.shape[0]
    rows = lax.broadcasted_iota(jnp.int32, (size, size), 0)
    cols = lax.broadcasted_iota(jnp.int32, (size, size), 1)
    low = jnp.where(rows >= cols, dot_nt(c, b), 0.0).astype(bf16)
    low_t = jnp.where(cols >= rows, dot_nt(b, c), 0.0).astype(bf16)
    return low, low_t


def first_body(heads, width, x, t, b, c, raw, a_log, skip, dt_bias, f_out, p_out, pay_out, a_out):
    rate = head_row(a_log, width)
    rate = jnp.where(lax.broadcasted_iota(jnp.int32, rate.shape, 1) < a_log.shape[0], jnp.exp(rate), 0.0)
    _, dt, logs, mid = steps_of(raw[...], head_row(dt_bias, width), rate, width)
    grow = jnp.exp(logs - mid)
    shrink = dt * jnp.exp(mid - logs)
    half = jnp.exp(mid)
    low, _ = masked_scores(b[...], c[...])
    b_t, c_t = b[...].T, c[...].T
    first = lax.axis_index("ctx") == 0
    for k, h in enumerate(heads):
        xs = x[h].astype(f32)
        g, scale = grow[:, h : h + 1], half[:, h : h + 1]
        xr = (xs * shrink[:, h : h + 1]).astype(bf16)
        err = g * dot(low, xr) + skip[h] * xs - t[h].astype(f32)
        ew = (err * g).astype(bf16)
        contrib = scale * dot(b_t, xr)
        pulled = scale * dot(c_t, ew)
        f_out[k] = contrib
        p_out[k] = pulled
        pay_out[k] = jnp.where(first, contrib, pulled)
        a_out[k] = jnp.broadcast_to(scale * scale, a_out.shape[1:])


def maps_body(heads, width, reach, *refs):
    c, raw, a_log, dt_bias = refs[:4]
    later, (m_out, mc_out) = refs[4 : 4 + reach], refs[4 + reach :]
    rate = head_row(a_log, width)
    rate = jnp.where(lax.broadcasted_iota(jnp.int32, rate.shape, 1) < a_log.shape[0], jnp.exp(rate), 0.0)
    bias = head_row(dt_bias, width)
    size = c.shape[0]

    def squares(c_low, raw_rows):
        _, _, logs, mid = steps_of(raw_rows, bias, rate, width)
        return c_low, c_low.T.astype(f32), jnp.exp(2.0 * logs).T, jnp.exp(2.0 * mid)

    own = squares(c[...], raw[...])
    rest = []
    for ref in later:
        rows = ref[size:, :]
        per = size // rows.shape[1]
        raw_rows = jnp.concatenate(
            [rows[per * h : per * h + per, :].reshape(1, size) if per == 1 else
             jnp.concatenate([rows[per * h + s : per * h + s + 1, :] for s in range(per)], axis=1)
             for h in range(raw.shape[0])], axis=0)
        rest.append(squares(ref[:size, :].astype(bf16), raw_rows))
    for k, h in enumerate(heads):

        def one(item):
            c_low, c_t, grow2, _ = item
            return dot((c_t * grow2[h : h + 1, :]).astype(bf16), c_low)

        m_out[k] = one(own)
        total = jnp.zeros(mc_out.shape[1:], f32)
        factor = jnp.ones((1, 1), f32)
        for item in rest:
            total = total + factor * one(item)
            factor = factor * item[3][:, h : h + 1] * item[3][:, h : h + 1]
        mc_out[k] = total


def times(m, s):
    high = m.astype(bf16)
    low = (m - high.astype(f32)).astype(bf16)
    s_low = s.astype(bf16)
    return dot(high, s_low) + dot(low, s_low)


def round_body(n, r, f, p, m, mc, a, got, s_in, d_in, pay_out, s_out, d_out):
    place = lax.axis_index("ctx")
    came_up, came_down = place == r - 1, place == n - r
    for k in range(f.shape[0]):
        s = jnp.where(came_up, got[k], s_in[k])
        d = jnp.where(came_down, got[k], d_in[k])
        s_out[k] = s
        d_out[k] = d
        after = a[k] * s + f[k]
        full = p[k] + times(m[k], s) + a[k] * (d + times(mc[k], after))
        pay_out[k] = jnp.where(place == r - 1, after, full)


def last_body(heads, width, final, scales, *refs):
    (x, t, b, c, raw, a_log, skip, dt_bias, f, mc, a, got, s_in, d_in) = refs[:14]
    refs = refs[14:]
    if not final:
        gx_out, cols_out, gb_out, gc_out, sums_out, ew_s, xr_s, s_s, a_s = refs
        before = None
    else:
        before = refs[:5]
        gx_out, raw_out, keep_out, send_out, sums_out, ew_s, xr_s, s_s, a_s = refs[5:]
    n = lax.axis_size("ctx")
    place = lax.axis_index("ctx")
    count = a_log.shape[0]
    lanes = lax.broadcasted_iota(jnp.int32, (1, width), 1)
    rate = jnp.where(lanes < count, jnp.exp(head_row(a_log, width)), 0.0)
    shifted, dt, logs, mid = steps_of(raw[...], head_row(dt_bias, width), rate, width)
    grow = jnp.exp(logs - mid)
    shrink = dt * jnp.exp(mid - logs)
    half = jnp.exp(mid)
    low, low_t = masked_scores(b[...], c[...])
    size, state = b.shape
    channels = x.shape[2]
    if final:
        v_all, w_all = before[1][0], before[1][1]
        ends, skips = before[4][0:1, :], before[4][1:2, :]
        for h in range(heads[0]):
            gx_out[h] = before[0][h]
    else:
        v_all = w_all = jnp.zeros((size, width), f32)
        ends = skips = jnp.zeros((1, width), f32)
    for k, h in enumerate(heads):
        xs = x[h].astype(f32)
        g, r, scale = grow[:, h : h + 1], shrink[:, h : h + 1], half[:, h : h + 1]
        s = jnp.where(place == n - 1, got[k], s_in[k]) if n > 1 else s_in[k]
        d = jnp.where(place == 0, got[k], d_in[k]) if n > 1 else d_in[k]
        after = a[k] * s + f[k]
        adjoint = d + times(mc[k], after)
        s_low = (scale * s).astype(bf16)
        a_low = (scale * adjoint).astype(bf16)
        xr = (xs * r).astype(bf16)
        y = dot(low, xr) + dot(c[...], s_low)
        err = g * y + skip[h] * xs - t[h].astype(f32)
        ew = (err * g).astype(bf16)
        z = dot(low_t, ew) + dot(b[...], a_low)
        gx_out[h if final else k] = (r * z + skip[h] * err).astype(bf16)
        here = lanes == h
        v_all = jnp.where(here, jnp.sum(ew.astype(f32) * y, axis=1, keepdims=True), v_all)
        w_all = jnp.where(here, jnp.sum(xr.astype(f32) * z, axis=1, keepdims=True), w_all)
        ends = jnp.where(here, jnp.sum(adjoint * after, keepdims=True).reshape(1, 1), ends)
        skips = jnp.where(here, jnp.sum(err * xs, keepdims=True).reshape(1, 1), skips)
        span = pl.ds(k * channels, channels)
        ew_s[:, span] = ew
        xr_s[:, span] = xr
        s_s[:, span] = s_low
        a_s[:, span] = a_low
    rows = lax.broadcasted_iota(jnp.int32, (size, size), 0)
    cols = lax.broadcasted_iota(jnp.int32, (size, size), 1)
    score = jnp.where(rows >= cols, dot_nt(ew_s[...], xr_s[...]), 0.0).astype(bf16)
    score_t = jnp.where(cols >= rows, dot_nt(xr_s[...], ew_s[...]), 0.0).astype(bf16)
    grad_c = dot(score, b[...]) + dot_nt(ew_s[...], s_s[...])
    grad_b = dot(score_t, c[...]) + dot_nt(xr_s[...], a_s[...])
    if not final:
        cols_out[0] = v_all
        cols_out[1] = w_all
        gb_out[...] = grad_b
        gc_out[...] = grad_c
        sums_out[...] = jnp.concatenate([ends, skips, jnp.zeros((6, width), f32)], axis=0)
        return
    grad_b = grad_b + before[2][...]
    grad_c = grad_c + before[3][...]
    parts = lax.axis_size("head")
    if parts == 1:
        keep_out[0], keep_out[1] = grad_b, grad_c
        send_out[0], send_out[1] = grad_b, grad_c
    else:
        cut = size // 2
        upper = lax.axis_index("head") >= parts // 2
        for i, grad in enumerate((grad_b, grad_c)):
            keep_out[i] = jnp.where(upper, grad[cut:, :], grad[:cut, :])
            send_out[i] = jnp.where(upper, grad[:cut, :], grad[cut:, :])
    last = lax.broadcasted_iota(jnp.int32, (size, width), 0) == size - 1
    grad_logs = v_all - w_all + jnp.where(last, ends, 0.0)
    upper_ones = jnp.where(cols >= rows, 1.0, 0.0).astype(f32)
    log_rate = jnp.dot(upper_ones, grad_logs, precision=highest, preferred_element_type=f32)
    grad_raw = (w_all / dt - rate * log_rate) / (1.0 + jnp.exp(-shifted))
    raw_out[...] = grad_raw.T[:count, :]
    alog = -rate * jnp.sum(log_rate * dt, axis=0, keepdims=True)
    bias = jnp.sum(grad_raw, axis=0, keepdims=True)
    sums_out[...] = jnp.concatenate(
        [alog * scales[0], skips * scales[1], bias * scales[0], jnp.zeros((5, width), f32)], axis=0
    )


def on_device(x_heads, target, b_proj, c_proj, dt_raw, a_log, skip_gain, dt_bias):
    x, t, b, c, raw = x_heads[0], target[0], b_proj[0], c_proj[0], dt_raw[0]
    heads, size, channels = x.shape
    state = b.shape[1]
    width = state
    n, place = lax.axis_size("ctx"), lax.axis_index("ctx")
    shape = jax.ShapeDtypeStruct

    own = jnp.concatenate([c.astype(f32), raw.reshape(-1, state)], axis=0)
    lowest = max(n // 2 - 1, 0)
    later = [
        lax.ppermute(own, "ctx", [(i + s, i) for i in range(lowest, n - s)]) for s in range(1, n - lowest)
    ]

    chunks = CHUNKS if heads % CHUNKS == 0 else 1
    per = heads // chunks
    groups = [tuple(range(i * per, (i + 1) * per)) for i in range(chunks)]
    states = shape((per, channels, state), f32)
    held = []
    for group in groups:
        f, p, pay, a = call(
            functools.partial(first_body, group, width),
            (states, states, states, shape((per, 1, state), f32)),
            x, t, b, c, raw, a_log, skip_gain, dt_bias, flops=4 * 10**8,
        )
        held.append(dict(f=f, p=p, pay=pay, a=a, s=jnp.zeros(states.shape, f32), d=jnp.zeros(states.shape, f32)))
    for group, h in zip(groups, held):
        h["m"], h["mc"] = call(
            functools.partial(maps_body, group, width, len(later)), (states, states),
            c, raw, a_log, dt_bias, *later, flops=10**8,
        )

    def swap(r):
        pairs = [(r - 1, r), (r, r - 1)]
        other = [(n - r, n - 1 - r), (n - 1 - r, n - r)]
        return pairs if r - 1 == n - 1 - r else pairs + other

    for stage in range(1, n - 1 + chunks):
        for i, h in enumerate(held):
            r = stage - i
            if not 1 <= r <= n - 1:
                continue
            if r > 1:
                h["pay"], h["s"], h["d"] = call(
                    functools.partial(round_body, n, r), (states, states, states),
                    h["f"], h["p"], h["m"], h["mc"], h["a"], h["got"], h["s"], h["d"], flops=10**8,
                )
            h["got"] = lax.ppermute(h["pay"], "ctx", swap(r))

    tokens = size * n * x_heads.shape[0] * lax.axis_size("seq")
    scales = (1.0 / tokens, 1.0 / (tokens * channels))
    sums = shape((8, width), f32)
    before = ()
    for i, (group, h) in enumerate(zip(groups, held)):
        final = i == chunks - 1
        got = h.get("got", h["s"])
        grads = shape((size, state), f32)
        cut = size if lax.axis_size("head") == 1 else size // 2
        if final:
            outs = (shape(x.shape, bf16), shape(raw.shape, f32), shape((2, cut, state), f32), shape((2, cut, state), f32), sums)
        else:
            outs = (shape((heads // chunks * (i + 1), size, channels), bf16), shape((2, size, width), f32), grads, grads, sums)
        args = (x, t, b, c, raw, a_log, skip_gain, dt_bias, h["f"], h["mc"], h["a"], got, h["s"], h["d"]) + before
        before = pl.pallas_call(
            functools.partial(last_body, group, width, final, scales),
            out_shape=outs,
            in_specs=[SMEM if v.ndim == 1 else VMEM for v in args],
            out_specs=[VMEM] * len(outs),
            scratch_shapes=[pltpu.VMEM((size, per * channels), bf16)] * 2 + [pltpu.VMEM((state, per * channels), bf16)] * 2,
            compiler_params=pltpu.CompilerParams(vmem_limit_bytes=LIMIT),
            cost_estimate=pl.CostEstimate(flops=4 * 10**8, bytes_accessed=1 << 20, transcendentals=0),
        )(*args)
    grad_x, grad_raw, keep, send, total = before

    parts = lax.axis_size("head")
    step = parts // 2
    while step >= 1:
        keep = keep + lax.ppermute(send, "head", [(i, i ^ step) for i in range(parts)])
        step //= 2
        if step >= 1:
            cut = keep.shape[1] // 2
            upper = (lax.axis_index("head") // step) % 2 == 1
            keep, send = (
                jnp.where(upper, keep[:, cut:], keep[:, :cut]),
                jnp.where(upper, keep[:, :cut], keep[:, cut:]),
            )
    for axis in ("seq", "ctx"):
        step = 1
        while step < lax.axis_size(axis):
            total = total + lax.ppermute(total, axis, [(i, i ^ step) for i in range(lax.axis_size(axis))])
            step *= 2
    return (
        grad_x[None], keep[0][None], keep[1][None], grad_raw[None],
        total[0, :heads], total[1, :heads], total[2, :heads],
    )


def solution(mesh):
    return jax.shard_map(
        on_device,
        mesh=mesh,
        in_specs=(
            P("seq", "head", "ctx", None),
            P("seq", "head", "ctx", None),
            P("seq", "ctx", None),
            P("seq", "ctx", None),
            P("seq", "head", "ctx"),
            P("head"),
            P("head"),
            P("head"),
        ),
        out_specs=(
            P("seq", "head", "ctx", None),
            P("seq", ("ctx", "head"), None),
            P("seq", ("ctx", "head"), None),
            P("seq", "head", "ctx"),
            P("head"),
            P("head"),
            P("head"),
        ),
        check_vma=False,
    )
```

```python
import functools
import jax
import jax.numpy as jnp
from jax import lax
from jax.experimental import pallas as pl
from jax.experimental.pallas import tpu as pltpu
from jax.sharding import PartitionSpec as P

CHUNKS = 2
f32, bf16 = jnp.float32, jnp.bfloat16
highest = lax.Precision.HIGHEST
VMEM = pl.BlockSpec(memory_space=pltpu.VMEM)
SMEM = pl.BlockSpec(memory_space=pltpu.SMEM)
HBM = pl.BlockSpec(memory_space=pltpu.HBM)
LIMIT = 48 * 1024 * 1024
shape = jax.ShapeDtypeStruct


def dot(a, b):
    return jnp.dot(a, b, preferred_element_type=f32)


def dot_nt(a, b):
    return lax.dot_general(a, b, (((1,), (1,)), ((), ())), preferred_element_type=f32)


def call(body, outs, *args, flops=10**8, ins=None, out_specs=None, scratch=()):
    return pl.pallas_call(
        body,
        out_shape=outs,
        in_specs=ins or [SMEM if a.ndim == 1 else VMEM for a in args],
        out_specs=out_specs or [VMEM] * len(outs),
        scratch_shapes=scratch,
        compiler_params=pltpu.CompilerParams(vmem_limit_bytes=LIMIT),
        cost_estimate=pl.CostEstimate(flops=flops // 10**5, bytes_accessed=1 << 8, transcendentals=0),
    )(*args)


def triangle(size, lower):
    rows = lax.broadcasted_iota(jnp.int32, (size, size), 0)
    cols = lax.broadcasted_iota(jnp.int32, (size, size), 1)
    return rows >= cols if lower else cols >= rows


def head_row(values, width):
    lanes = lax.broadcasted_iota(jnp.int32, (1, width), 1)
    row = jnp.zeros((1, width), f32)
    for h in range(values.shape[0]):
        row = jnp.where(lanes == h, values[h], row)
    return row


def steps_of(raw, bias, rate, width):
    heads, size = raw.shape
    columns = jnp.concatenate([raw, jnp.zeros((width - heads, size), f32)], axis=0).T
    shifted = columns + bias
    dt = jnp.maximum(shifted, 0.0) + jnp.log1p(jnp.exp(-jnp.abs(shifted)))
    lower = jnp.where(triangle(size, True), 1.0, 0.0).astype(f32)
    return shifted, dt, jnp.dot(lower, -rate * dt, precision=highest, preferred_element_type=f32)


def load_body(x, t, b, c, raw, xv, tv, bv, cv, rawv, own, sems):
    copies = [
        pltpu.make_async_copy(src, dst, sems.at[i])
        for i, (src, dst) in enumerate(((c, cv), (raw, rawv), (b, bv), (x, xv), (t, tv)))
    ]
    for copy in copies:
        copy.start()
    copies[0].wait()
    copies[1].wait()
    size, state = c.shape
    heads = raw.shape[0]
    own[:size, :] = cv[...].astype(f32)
    for s in range(size // state):
        own[size + s * heads : size + (s + 1) * heads, :] = rawv[:, s * state : (s + 1) * state]
    for copy in copies[2:]:
        copy.wait()


def prepare_body(b, c, raw, a_log, skip, dt_bias, cols_out, low_out, low_t_out, b_t_out, c_t_out, sq_out, rows_out):
    size, width = b.shape
    lanes = lax.broadcasted_iota(jnp.int32, (1, width), 1)
    rate = jnp.where(lanes < a_log.shape[0], jnp.exp(head_row(a_log, width)), 0.0)
    bias = head_row(dt_bias, width)
    shifted, dt, logs = steps_of(raw[...], bias, rate, width)
    mid = 0.5 * logs[size - 1 : size, :]
    cols_out[0] = jnp.exp(logs - mid)
    cols_out[1] = dt * jnp.exp(mid - logs)
    cols_out[2] = dt
    cols_out[3] = shifted
    half = jnp.exp(mid)
    rows_out[...] = jnp.concatenate([half, half * half, rate, head_row(skip, width), bias, jnp.zeros((3, width), f32)], axis=0)
    sq_out[...] = jnp.exp(2.0 * logs).T
    low_out[...] = jnp.where(triangle(size, True), dot_nt(c[...], b[...]), 0.0).astype(bf16)
    low_t_out[...] = jnp.where(triangle(size, False), dot_nt(b[...], c[...]), 0.0).astype(bf16)
    b_t_out[...] = b[...].T
    c_t_out[...] = c[...].T


def first_body(heads, x, t, cols, low, b_t, c_t, rows, f_out, p_out, xr_out, y_out, err_out):
    for k, h in enumerate(heads):
        xs = x[h].astype(f32)
        g, scale, skip = cols[0, :, h : h + 1], rows[0:1, h : h + 1], rows[3:4, h : h + 1]
        xr = (xs * cols[1, :, h : h + 1]).astype(bf16)
        y = dot(low[...], xr)
        err = g * y + skip * xs - t[h].astype(f32)
        ew = (err * g).astype(bf16)
        xr_out[k] = xr
        y_out[k] = y
        err_out[k] = err
        f_out[k] = scale * dot(b_t[...], xr)
        p_out[k] = scale * dot(c_t[...], ew)


def send_body(f, p, *refs):
    got, (pay_out, *low_outs) = refs[:-3], refs[-3:] if len(refs) == 4 else refs
    pay_out[...] = jnp.where(lax.axis_index("ctx") == 0, f[...], p[...])
    if got:
        c = got[0][: low_outs[0].shape[0], :].astype(bf16)
        low_outs[0][...] = c
        low_outs[1][...] = c.T


def own_map_body(c, c_t, sq, m_out):
    wide = c_t[...].astype(f32)
    for h in range(m_out.shape[0]):
        m_out[h] = dot((wide * sq[h : h + 1, :]).astype(bf16), c[...])


def later_maps_body(reach, rows, c_first, c_t_first, *refs):
    later, outs = refs[:reach], refs[reach:]
    heads, width = outs[0].shape[0], outs[0].shape[2]
    size = c_first.shape[0]
    factor = jnp.ones((1, width), f32)
    for i, (got, out) in enumerate(zip(later, outs)):
        raw = jnp.concatenate([got[size + s * heads : size + (s + 1) * heads, :] for s in range(size // width)], axis=1)
        _, _, logs = steps_of(raw, rows[4:5, :], rows[2:3, :], width)
        c = got[:size, :].astype(bf16) if i else c_first[...]
        c_t = (c.T if i else c_t_first[...]).astype(f32)
        sq = jnp.exp(2.0 * logs).T
        for h in range(heads):
            added = factor[:, h : h + 1] * dot((c_t * sq[h : h + 1, :]).astype(bf16), c)
            out[h] = outs[i - 1][h] + added if i else added
        factor = factor * jnp.exp(2.0 * logs[size - 1 : size, :])


def times(m, s):
    high = m.astype(bf16)
    low = (m - high.astype(f32)).astype(bf16)
    s_low = s.astype(bf16)
    return dot(high, s_low) + dot(low, s_low)


def round_body(heads, n, r, f, p, m, mc, rows, got, s_in, d_in, pay_out, s_out, d_out):
    place = lax.axis_index("ctx")
    came_up, came_down = place == r - 1, place == n - r
    for k, h in enumerate(heads):
        s = jnp.where(came_up, got[k], s_in[k])
        d = jnp.where(came_down, got[k], d_in[k])
        s_out[k] = s
        d_out[k] = d
        total = rows[1:2, h : h + 1]
        after = total * s + f[k]
        full = p[k] + times(m[h], s) + total * (d + times(mc[h], after))
        pay_out[k] = jnp.where(place == r - 1, after, full)


def last_body(heads, scales, *refs):
    (x, cols, low, low_t, b, c, rows, xr, y_in, err_in, f, mc, got, s_in, d_in, v_in, sums_in) = refs[:17]
    gx_out, ew_out, s_low_out, a_low_out, v_out, sums_out = refs[17:23]
    n = lax.axis_size("ctx")
    place = lax.axis_index("ctx")
    size, width = b.shape
    channels = x.shape[2]
    lanes = lax.broadcasted_iota(jnp.int32, (1, width), 1)
    v_all, w_all = v_in[0], v_in[1]
    ends, skips = sums_in[0:1, :], sums_in[1:2, :]
    for k, h in enumerate(heads):
        g, r = cols[0, :, h : h + 1], cols[1, :, h : h + 1]
        scale, total, skip = rows[0:1, h : h + 1], rows[1:2, h : h + 1], rows[3:4, h : h + 1]
        s = jnp.where(place == n - 1, got[k], s_in[k]) if n > 1 else s_in[k]
        d = jnp.where(place == 0, got[k], d_in[k]) if n > 1 else d_in[k]
        after = total * s + f[k]
        adjoint = d + times(mc[h], after)
        s_low = (scale * s).astype(bf16)
        a_low = (scale * adjoint).astype(bf16)
        carried = dot(c[...], s_low)
        y = y_in[k] + carried
        err = err_in[k] + g * carried
        ew = (err * g).astype(bf16)
        z = dot(low_t[...], ew) + dot(b[...], a_low)
        gx_out[k] = (r * z + skip * err).astype(bf16)
        here = lanes == h
        v_all = jnp.where(here, jnp.sum(ew.astype(f32) * y, axis=1, keepdims=True), v_all)
        w_all = jnp.where(here, jnp.sum(xr[k].astype(f32) * z, axis=1, keepdims=True), w_all)
        ends = jnp.where(here, jnp.sum(jnp.sum(adjoint * after, axis=0, keepdims=True), axis=1, keepdims=True), ends)
        skips = jnp.where(here, jnp.sum(jnp.sum(err * x[h].astype(f32), axis=0, keepdims=True), axis=1, keepdims=True), skips)
        span = slice(k * channels, (k + 1) * channels)
        ew_out[:, span] = ew
        s_low_out[:, span] = s_low
        a_low_out[:, span] = a_low
    if scales is None:
        v_out[0] = v_all
        v_out[1] = w_all
        sums_out[...] = jnp.concatenate([ends, skips, jnp.zeros((6, width), f32)], axis=0)
        return
    count = v_out.shape[0]
    rate, dt = rows[2:3, :], cols[2]
    last = lax.broadcasted_iota(jnp.int32, (size, width), 0) == size - 1
    grad_logs = v_all - w_all + jnp.where(last, ends, 0.0)
    upper = jnp.where(triangle(size, False), 1.0, 0.0).astype(f32)
    log_rate = jnp.dot(upper, grad_logs, precision=highest, preferred_element_type=f32)
    grad_raw = (w_all / dt - rate * log_rate) / (1.0 + jnp.exp(-cols[3]))
    v_out[...] = grad_raw.T[:count, :]
    alog = -rate * jnp.sum(log_rate * dt, axis=0, keepdims=True)
    bias = jnp.sum(grad_raw, axis=0, keepdims=True)
    sums_out[...] = jnp.concatenate(
        [alog * scales[0], skips * scales[1], bias * scales[0], jnp.zeros((5, width), f32)], axis=0
    )


def project_body(b, c, xr, ew, s_low, a_low, grads_in, grads_out):
    size = b.shape[0]
    wide = jnp.concatenate([xr[k] for k in range(xr.shape[0])], axis=1)
    score = jnp.where(triangle(size, True), dot_nt(ew[...], wide), 0.0).astype(bf16)
    score_t = jnp.where(triangle(size, False), dot_nt(wide, ew[...]), 0.0).astype(bf16)
    grads_out[0] = grads_in[0] + dot(score_t, c[...]) + dot_nt(wide, a_low[...])
    grads_out[1] = grads_in[1] + dot(score, b[...]) + dot_nt(ew[...], s_low[...])


def output_body(chunks, *refs):
    parts = refs[:chunks]
    sums, sums_got = refs[chunks + 7 : chunks + 9]
    keep_out, send_out, gx_out, sums_out, grads, sems = refs[chunks + 9 :]
    sums_out[...] = sums[...] + sums_got[...]
    per = parts[0].shape[0]
    copies = [pltpu.make_async_copy(part, gx_out.at[pl.ds(i * per, per)], sems.at[i]) for i, part in enumerate(parts)]
    for copy in copies:
        copy.start()
    project_body(*refs[chunks : chunks + 7], grads)
    cut, size = keep_out.shape[1], grads.shape[1]
    upper = lax.axis_index("head") >= lax.axis_size("head") // 2
    for i in range(2):
        grad = grads[i]
        keep_out[i] = jnp.where(upper, grad[size - cut :, :], grad[:cut, :])
        send_out[i] = jnp.where(upper, grad[:cut, :], grad[size - cut :, :])
    for copy in copies:
        copy.wait()


def add_body(a, b, c, d, first_out, second_out):
    first_out[...] = a[...] + b[...]
    second_out[...] = c[...] + d[...]


def on_device(x_heads, target, b_proj, c_proj, dt_raw, a_log, skip_gain, dt_bias):
    heads, size, channels = x_heads.shape[1:]
    width = b_proj.shape[2]
    n = lax.axis_size("ctx")
    parts = lax.axis_size("head")
    chunks = CHUNKS if heads % CHUNKS == 0 else 1
    per = heads // chunks
    groups = [tuple(range(i * per, (i + 1) * per)) for i in range(chunks)]
    square, states, all_states = shape((size, size), bf16), shape((per, width, channels), f32), shape((heads, width, width), f32)
    flat = shape((width, size), bf16)
    panel = shape((per, size, channels), f32)

    x, t, b, c, raw, own = call(
        load_body,
        [shape(a.shape[1:], a.dtype) for a in (x_heads, target, b_proj, c_proj, dt_raw)]
        + [shape((size + heads * size // width, width), f32)],
        *[pltpu.with_memory_space_constraint(a[0], pltpu.HBM) for a in (x_heads, target, b_proj, c_proj, dt_raw)],
        ins=[HBM] * 5, scratch=[pltpu.SemaphoreType.DMA((5,))], flops=10**6,
    )
    lowest = max(n // 2 - 1, 0)
    later = []
    for s in range(1, n - lowest):
        own = lax.ppermute(own, "ctx", [(i + 1, i) for i in range(lowest, n - s)])
        later.append(own)
    cols, low, low_t, b_t, c_t, sq, rows = call(
        prepare_body,
        [shape((4, size, width), f32), square, square, flat, flat, shape((width, size), f32), shape((8, width), f32)],
        b, c, raw, a_log, skip_gain, dt_bias,
    )
    held = []
    maps = [jnp.zeros(all_states.shape, f32)]
    for i, group in enumerate(groups):
        f, p, xr, y, err = call(
            functools.partial(first_body, group),
            [states, states, shape(panel.shape, bf16), panel, panel],
            x, t, cols, low, b_t, c_t, rows, flops=4 * 10**8,
        )
        if i == 0 and later:
            pay, *lows = call(send_body, [states, shape((size, width), bf16), flat], f, p, later[0])
        else:
            (pay,) = call(send_body, [states], f, p)
        zero = jnp.zeros(states.shape, f32)
        held.append(dict(f=f, p=p, pay=pay, xr=xr, y=y, err=err, s=zero, d=zero))
    (m,) = call(own_map_body, [all_states], c, c_t, sq)
    if later:
        maps += call(functools.partial(later_maps_body, len(later)), [all_states] * len(later), rows, *lows, *later)

    def swap(r):
        pairs = [(r - 1, r), (r, r - 1)]
        other = [(n - r, n - 1 - r), (n - 1 - r, n - r)]
        return pairs if r - 1 == n - 1 - r else pairs + other

    for stage in range(1, n - 1 + chunks):
        for i, h in enumerate(held):
            r = stage - i
            if not 1 <= r <= n - 1:
                continue
            if r > 1:
                h["pay"], h["s"], h["d"] = call(
                    functools.partial(round_body, groups[i], n, r), [states, states, states],
                    h["f"], h["p"], m, maps[min(r - 1, len(later))], rows, h["got"], h["s"], h["d"],
                )
            h["got"] = lax.ppermute(h["pay"], "ctx", swap(r))

    tokens = size * n * x_heads.shape[0] * lax.axis_size("seq")
    scales = (1.0 / tokens, 1.0 / (tokens * channels))
    cut = size if parts == 1 else size // 2
    v, total = jnp.zeros((2, size, width), f32), jnp.zeros((8, width), f32)
    grads = jnp.zeros((2, size, width), f32)
    grad_x = []
    for i, h in enumerate(held):
        final = i == chunks - 1
        gx, ew, s_low, a_low, v, total = call(
            functools.partial(last_body, groups[i], scales if final else None),
            [shape(panel.shape, bf16), shape((size, per * channels), bf16)] + [shape((width, per * channels), bf16)] * 2
            + [shape(raw.shape if final else v.shape, f32), shape((8, width), f32)],
            x, cols, low, low_t, b, c, rows, h["xr"], h["y"], h["err"], h["f"], maps[-1],
            h.get("got", h["s"]), h["s"], h["d"], v, total, flops=4 * 10**8,
        )
        grad_x.append(gx)
        args = (b, c, h["xr"], ew, s_low, a_low, grads)
        if not final:
            (grads,) = call(project_body, [shape(grads.shape, f32)], *args, flops=2 * 10**8)
    swaps = [(axis, 1 << k) for axis in ("seq", "ctx") for k in reversed(range(lax.axis_size(axis).bit_length() - 1))]
    if ("seq", 1) in swaps:
        swaps.remove(("seq", 1))
        got = lax.ppermute(total, "seq", [(i, i ^ 1) for i in range(lax.axis_size("seq"))])
    else:
        got = jnp.zeros(total.shape, f32)
    halves = shape((2, cut, width), f32)
    keep, send, grad_x, total = call(
        functools.partial(output_body, chunks),
        [halves, halves, shape((heads, size, channels), bf16), shape(total.shape, f32)],
        *grad_x, *args, total, got, out_specs=[VMEM, VMEM, HBM, VMEM], flops=2 * 10**8,
        scratch=[pltpu.VMEM(grads.shape, f32), pltpu.SemaphoreType.DMA((chunks,))],
    )
    step = parts // 2
    while step >= 1:
        received = lax.ppermute(send, "head", [(i, i ^ step) for i in range(parts)])
        if swaps:
            axis, by = swaps.pop()
            got = lax.ppermute(total, axis, [(i, i ^ by) for i in range(lax.axis_size(axis))])
            keep, total = call(add_body, [shape(keep.shape, f32), shape(total.shape, f32)], keep, received, total, got)
        else:
            keep = keep + received
        step //= 2
        if step >= 1:
            cut = keep.shape[1] // 2
            upper = (lax.axis_index("head") // step) % 2 == 1
            keep, send = (
                jnp.where(upper, keep[:, cut:], keep[:, :cut]),
                jnp.where(upper, keep[:, :cut], keep[:, cut:]),
            )
    while swaps:
        axis, by = swaps.pop()
        total = total + lax.ppermute(total, axis, [(i, i ^ by) for i in range(lax.axis_size(axis))])
    return (
        grad_x[None], keep[0][None], keep[1][None], v[None],
        total[0, :heads], total[1, :heads], total[2, :heads],
    )


def solution(mesh):
    return jax.shard_map(
        on_device,
        mesh=mesh,
        in_specs=(
            P("seq", "head", "ctx", None),
            P("seq", "head", "ctx", None),
            P("seq", "ctx", None),
            P("seq", "ctx", None),
            P("seq", "head", "ctx"),
            P("head"),
            P("head"),
            P("head"),
        ),
        out_specs=(
            P("seq", "head", "ctx", None),
            P("seq", ("ctx", "head"), None),
            P("seq", ("ctx", "head"), None),
            P("seq", "head", "ctx"),
            P("head"),
            P("head"),
            P("head"),
        ),
        check_vma=False,
    )
```

```python
import functools
import jax
import jax.numpy as jnp
from jax import lax
from jax.experimental import pallas as pl
from jax.experimental.pallas import tpu as pltpu
from jax.sharding import PartitionSpec as P

CHUNKS = 2
f32, bf16 = jnp.float32, jnp.bfloat16
highest = lax.Precision.HIGHEST
VMEM = pl.BlockSpec(memory_space=pltpu.VMEM)
HBM = pl.BlockSpec(memory_space=pltpu.HBM)
LIMIT = 48 * 1024 * 1024
shape = jax.ShapeDtypeStruct


def dot(a, b):
    return jnp.dot(a, b, preferred_element_type=f32)


def dot_nt(a, b):
    return lax.dot_general(a, b, (((1,), (1,)), ((), ())), preferred_element_type=f32)


def call(body, outs, *args, flops=10**8, ins=None, out_specs=None, scratch=()):
    return pl.pallas_call(
        body,
        out_shape=outs,
        in_specs=ins or [VMEM] * len(args),
        out_specs=out_specs or [VMEM] * len(outs),
        scratch_shapes=scratch,
        compiler_params=pltpu.CompilerParams(vmem_limit_bytes=LIMIT),
        cost_estimate=pl.CostEstimate(flops=flops // 10**5, bytes_accessed=1 << 8, transcendentals=0),
    )(*args)


def triangle(size, lower):
    rows = lax.broadcasted_iota(jnp.int32, (size, size), 0)
    cols = lax.broadcasted_iota(jnp.int32, (size, size), 1)
    return rows >= cols if lower else cols >= rows


def head_row(values, width):
    heads = values.shape[1]
    rows = lax.broadcasted_iota(jnp.int32, (heads, width), 0)
    cols = lax.broadcasted_iota(jnp.int32, (heads, width), 1)
    spread = jnp.where(rows == cols, 1.0, 0.0).astype(f32)
    return jnp.dot(values, spread, precision=highest, preferred_element_type=f32)


def steps_of(raw, bias, rate, width):
    heads, size = raw.shape
    columns = jnp.concatenate([raw, jnp.zeros((width - heads, size), f32)], axis=0).T
    shifted = columns + bias
    dt = jnp.maximum(shifted, 0.0) + jnp.log1p(jnp.exp(-jnp.abs(shifted)))
    lower = jnp.where(triangle(size, True), 1.0, 0.0).astype(f32)
    return shifted, dt, jnp.dot(lower, -rate * dt, precision=highest, preferred_element_type=f32)


def fetch(pairs, sems):
    copies = [pltpu.make_async_copy(src, dst, sems.at[i]) for i, (src, dst) in enumerate(pairs)]
    for copy in copies:
        copy.start()
    return copies


def own_body(c, raw, cv, rawv, own, sems):
    for copy in fetch(((c, cv), (raw, rawv)), sems):
        copy.wait()
    size, state = c.shape
    heads = raw.shape[0]
    own[:size, :] = cv[...].astype(f32)
    for s in range(size // state):
        own[size + s * heads : size + (s + 1) * heads, :] = rawv[:, s * state : (s + 1) * state]


def load_body(*refs):
    count = len(refs) // 2
    for copy in fetch(zip(refs[:count], refs[count : 2 * count]), refs[-1]):
        copy.wait()


def prepare_body(b, c, raw, a_log, skip, dt_bias, cols_out, low_out, low_t_out, b_t_out, c_t_out, sq_out, rows_out):
    size, width = b.shape
    lanes = lax.broadcasted_iota(jnp.int32, (1, width), 1)
    rate = jnp.where(lanes < a_log.shape[1], jnp.exp(head_row(a_log[...], width)), 0.0)
    bias = head_row(dt_bias[...], width)
    shifted, dt, logs = steps_of(raw[...], bias, rate, width)
    mid = 0.5 * logs[size - 1 : size, :]
    cols_out[0] = jnp.exp(logs - mid)
    cols_out[1] = dt * jnp.exp(mid - logs)
    cols_out[2] = dt
    half = jnp.exp(mid)
    rows_out[...] = jnp.concatenate([half, half * half, rate, head_row(skip[...], width), bias, jnp.zeros((3, width), f32)], axis=0)
    sigma = 1.0 / (1.0 + jnp.exp(-shifted))
    cols_out[3] = sigma
    cols_out[4] = logs
    lower = jnp.where(triangle(size, True), 1.0, 0.0).astype(f32)
    cols_out[5] = jnp.dot(lower, rate * sigma, precision=highest, preferred_element_type=f32)
    sq_out[...] = jnp.exp(2.0 * logs).T
    low_out[...] = jnp.where(triangle(size, True), dot_nt(c[...], b[...]), 0.0).astype(bf16)
    low_t_out[...] = jnp.where(triangle(size, False), dot_nt(b[...], c[...]), 0.0).astype(bf16)
    b_t_out[...] = b[...].T
    c_t_out[...] = c[...].T


def first_body(heads, x, t, cols, low, b_t, c_t, rows, f_out, p_out, xr_out, y_out, err_out):
    for k, h in enumerate(heads):
        xs = x[h].astype(f32)
        g, scale, skip = cols[0, :, h : h + 1], rows[0:1, h : h + 1], rows[3:4, h : h + 1]
        xr = (xs * cols[1, :, h : h + 1]).astype(bf16)
        y = dot(low[...], xr)
        err = g * y + skip * xs - t[h].astype(f32)
        ew = (err * g).astype(bf16)
        xr_out[k] = xr
        y_out[k] = y
        err_out[k] = err
        f_out[k] = scale * dot(b_t[...], xr)
        p_out[k] = scale * dot(c_t[...], ew)


def send_body(chunks, *refs):
    got, refs = refs[0], refs[1:]
    first = lax.axis_index("ctx") == 0
    for f, p, pay in zip(refs[:chunks], refs[chunks : 2 * chunks], refs[2 * chunks :]):
        pay[...] = jnp.where(first, f[...], p[...])
    refs[-1][...] = got[...]


def own_map_body(c, c_t, sq, m_out):
    wide = c_t[...].astype(f32)
    for h in range(m_out.shape[0]):
        m_out[h] = dot((wide * sq[h : h + 1, :]).astype(bf16), c[...])


def later_map_body(rows, got, *refs):
    before, (mc_out, factor_out) = refs[:-2], refs[-2:]
    heads, width = mc_out.shape[0], mc_out.shape[2]
    size = got.shape[0] * width // (width + heads)
    raw = jnp.concatenate([got[size + s * heads : size + (s + 1) * heads, :] for s in range(size // width)], axis=1)
    _, _, logs = steps_of(raw, rows[4:5, :], rows[2:3, :], width)
    c = got[:size, :].astype(bf16)
    c_t = c.T.astype(f32)
    sq = jnp.exp(2.0 * logs).T
    factor = before[1][...] if before else jnp.ones((1, width), f32)
    for h in range(heads):
        added = factor[:, h : h + 1] * dot((c_t * sq[h : h + 1, :]).astype(bf16), c)
        mc_out[h] = before[0][h] + added if before else added
    factor_out[...] = factor * jnp.exp(2.0 * logs[size - 1 : size, :])


def times(m, s):
    high = m.astype(bf16)
    low = (m - high.astype(f32)).astype(bf16)
    s_low = s.astype(bf16)
    return dot(high, s_low) + dot(low, s_low)


def round_body(heads, n, r, f, p, m, mc, rows, got, s_in, d_in, pay_out, s_out, d_out):
    place = lax.axis_index("ctx")
    came_up, came_down = place == r - 1, place == n - r
    for k, h in enumerate(heads):
        s = jnp.where(came_up, got[k], s_in[k])
        d = jnp.where(came_down, got[k], d_in[k])
        s_out[k] = s
        d_out[k] = d
        total = rows[1:2, h : h + 1]
        after = total * s + f[k]
        full = p[k] + times(m[h], s) + total * (d + times(mc[h], after))
        pay_out[k] = jnp.where(place == r - 1, after, full)


def last_body(heads, scales, *refs):
    (x, cols, low, low_t, b, c, rows, xr, y_in, err_in, f, mc, got, s_in, d_in, v_in, sums_in) = refs[:17]
    gx_out, ew_out, s_low_out, a_low_out, v_out, sums_out = refs[17:23]
    n = lax.axis_size("ctx")
    place = lax.axis_index("ctx")
    size, width = b.shape
    channels = x.shape[2]
    lanes = lax.broadcasted_iota(jnp.int32, (1, width), 1)
    v_all, w_all = v_in[0], v_in[1]
    ends, skips = sums_in[0:1, :], sums_in[1:2, :]
    for k, h in enumerate(heads):
        g, r = cols[0, :, h : h + 1], cols[1, :, h : h + 1]
        scale, total, skip = rows[0:1, h : h + 1], rows[1:2, h : h + 1], rows[3:4, h : h + 1]
        s = jnp.where(place == n - 1, got[k], s_in[k]) if n > 1 else s_in[k]
        d = jnp.where(place == 0, got[k], d_in[k]) if n > 1 else d_in[k]
        after = total * s + f[k]
        adjoint = d + times(mc[h], after)
        s_low = (scale * s).astype(bf16)
        a_low = (scale * adjoint).astype(bf16)
        carried = dot(c[...], s_low)
        y = y_in[k] + carried
        err = err_in[k] + g * carried
        ew = (err * g).astype(bf16)
        z = dot(low_t[...], ew) + dot(b[...], a_low)
        gx_out[k] = (r * z + skip * err).astype(bf16)
        here = lanes == h
        v_all = jnp.where(here, jnp.sum(ew.astype(f32) * y, axis=1, keepdims=True), v_all)
        w_all = jnp.where(here, jnp.sum(xr[k].astype(f32) * z, axis=1, keepdims=True), w_all)
        ends = jnp.where(here, jnp.sum(jnp.sum(adjoint * after, axis=0, keepdims=True), axis=1, keepdims=True), ends)
        skips = jnp.where(here, jnp.sum(jnp.sum(err * x[h].astype(f32), axis=0, keepdims=True), axis=1, keepdims=True), skips)
        span = slice(k * channels, (k + 1) * channels)
        ew_out[:, span] = ew
        s_low_out[:, span] = s_low
        a_low_out[:, span] = a_low
    if scales is None:
        v_out[0] = v_all
        v_out[1] = w_all
        sums_out[...] = jnp.concatenate([ends, skips, jnp.zeros((6, width), f32)], axis=0)
        return
    last = lax.broadcasted_iota(jnp.int32, (size, width), 0) == size - 1
    grad_logs = v_all - w_all + jnp.where(last, ends, 0.0)
    by_step = w_all / cols[2]
    v_out[0] = grad_logs
    v_out[1] = by_step
    alog = jnp.sum(grad_logs * cols[4], axis=0, keepdims=True)
    bias = jnp.sum(by_step * cols[3] - grad_logs * cols[5], axis=0, keepdims=True)
    sums_out[...] = jnp.concatenate(
        [alog * scales[0], skips * scales[1], bias * scales[0], jnp.zeros((5, width), f32)], axis=0
    )


def project_body(b, c, xr, ew, s_low, a_low, grads_in, grads_out):
    size = b.shape[0]
    wide = jnp.concatenate([xr[k] for k in range(xr.shape[0])], axis=1)
    score = jnp.where(triangle(size, True), dot_nt(ew[...], wide), 0.0).astype(bf16)
    score_t = jnp.where(triangle(size, False), dot_nt(wide, ew[...]), 0.0).astype(bf16)
    grads_out[0] = grads_in[0] + dot(score_t, c[...]) + dot_nt(wide, a_low[...])
    grads_out[1] = grads_in[1] + dot(score, b[...]) + dot_nt(ew[...], s_low[...])


def cut_body(grads, *refs):
    *sums, keep_out, send_out, sums_out = refs
    cut, size = keep_out.shape[1], grads.shape[1]
    upper = lax.axis_index("head") >= lax.axis_size("head") // 2
    for i in range(2):
        grad = grads[i]
        keep_out[i] = jnp.where(upper, grad[size - cut :, :], grad[:cut, :])
        send_out[i] = jnp.where(upper, grad[:cut, :], grad[size - cut :, :])
    sums_out[...] = sums[0][...] + sums[1][...] if len(sums) > 1 else sums[0][...]


def output_body(chunks, *refs):
    parts, (cols, rows, v), (gx_out, raw_out, sems) = refs[:chunks], refs[chunks : chunks + 3], refs[chunks + 3 :]
    per, size = parts[0].shape[0], v.shape[1]
    copies = fetch([(part, gx_out.at[pl.ds(i * per, per)]) for i, part in enumerate(parts)], sems)
    later = jnp.where(triangle(size, False), 1.0, 0.0).astype(f32)
    log_rate = jnp.dot(later, v[0], precision=highest, preferred_element_type=f32)
    raw_out[...] = ((v[1] - rows[2:3, :] * log_rate) * cols[3]).T[: raw_out.shape[0], :]
    for copy in copies:
        copy.wait()


def add_body(*refs):
    count = len(refs) // 3
    for a, b, out in zip(refs[:count], refs[count : 2 * count], refs[2 * count :]):
        out[...] = a[...] + b[...]


def on_device(x_heads, target, b_proj, c_proj, dt_raw, a_log, skip_gain, dt_bias):
    heads, size, channels = x_heads.shape[1:]
    width = b_proj.shape[2]
    n = lax.axis_size("ctx")
    parts = lax.axis_size("head")
    chunks = CHUNKS if heads % CHUNKS == 0 else 1
    per = heads // chunks
    groups = [tuple(range(i * per, (i + 1) * per)) for i in range(chunks)]
    square, states, all_states = shape((size, size), bf16), shape((per, width, channels), f32), shape((heads, width, width), f32)
    flat = shape((width, size), bf16)
    panel = shape((per, size, channels), f32)

    def held_in_hbm(*arrays):
        return [pltpu.with_memory_space_constraint(a, pltpu.HBM) for a in arrays]

    def like(*arrays):
        return [shape(a.shape, a.dtype) for a in arrays]

    shared = held_in_hbm(c_proj[0], dt_raw[0])
    c, raw, own = call(
        own_body, like(*shared) + [shape((size + heads * size // width, width), f32)], *shared,
        ins=[HBM] * 2, scratch=[pltpu.SemaphoreType.DMA((2,))], flops=10**6,
    )
    rest = held_in_hbm(a_log[None], skip_gain[None], dt_bias[None], b_proj[0], x_heads[0], target[0])
    a_log, skip_gain, dt_bias, b, x, t = call(
        load_body, like(*rest), *rest, ins=[HBM] * 6, scratch=[pltpu.SemaphoreType.DMA((6,))], flops=10**6
    )
    lowest = max(n // 2 - 1, 0)

    def down(step, value):
        return lax.ppermute(value, "ctx", [(i + 1, i) for i in range(lowest, n - step)])

    later = down(1, own)
    cols, low, low_t, b_t, c_t, sq, rows = call(
        prepare_body,
        [shape((6, size, width), f32), square, square, flat, flat, shape((width, size), f32), shape((8, width), f32)],
        b, c, raw, a_log, skip_gain, dt_bias,
    )
    held = []
    for group in groups:
        f, p, xr, y, err = call(
            functools.partial(first_body, group),
            [states, states, shape(panel.shape, bf16), panel, panel],
            x, t, cols, low, b_t, c_t, rows, flops=4 * 10**8,
        )
        zero = jnp.zeros(states.shape, f32)
        held.append(dict(f=f, p=p, xr=xr, y=y, err=err, s=zero, d=zero))
    *pays, later = call(
        functools.partial(send_body, chunks), [states] * chunks + [shape(own.shape, f32)],
        later, *[h["f"] for h in held], *[h["p"] for h in held],
    )
    for h, pay in zip(held, pays):
        h["pay"] = pay
    (m,) = call(own_map_body, [all_states], c, c_t, sq)
    mc, before = jnp.zeros(all_states.shape, f32), ()
    for step in range(1, n - lowest):
        if step > 1:
            later = down(step, later)
        mc, factor = before = call(later_map_body, [all_states, shape((1, width), f32)], rows, later, *before)

    def swap(r):
        pairs = [(r - 1, r), (r, r - 1)]
        other = [(n - r, n - 1 - r), (n - 1 - r, n - r)]
        return pairs if r - 1 == n - 1 - r else pairs + other

    for stage in range(1, n - 1 + chunks):
        for i, h in enumerate(held):
            r = stage - i
            if not 1 <= r <= n - 1:
                continue
            if r > 1:
                h["pay"], h["s"], h["d"] = call(
                    functools.partial(round_body, groups[i], n, r), [states, states, states],
                    h["f"], h["p"], m, mc, rows, h["got"], h["s"], h["d"],
                )
            h["got"] = lax.ppermute(h["pay"], "ctx", swap(r))

    tokens = size * n * x_heads.shape[0] * lax.axis_size("seq")
    scales = (1.0 / tokens, 1.0 / (tokens * channels))
    cut = size if parts == 1 else size // 2
    v, total = jnp.zeros((2, size, width), f32), jnp.zeros((8, width), f32)
    grads = jnp.zeros((2, size, width), f32)
    grad_x = []
    for i, h in enumerate(held):
        final = i == chunks - 1
        gx, ew, s_low, a_low, v, total = call(
            functools.partial(last_body, groups[i], scales if final else None),
            [shape(panel.shape, bf16), shape((size, per * channels), bf16)] + [shape((width, per * channels), bf16)] * 2
            + [shape(v.shape, f32), shape((8, width), f32)],
            x, cols, low, low_t, b, c, rows, h["xr"], h["y"], h["err"], h["f"], mc,
            h.get("got", h["s"]), h["s"], h["d"], v, total, flops=4 * 10**8,
        )
        grad_x.append(gx)
        args = (b, c, h["xr"], ew, s_low, a_low, grads)
        (grads,) = call(project_body, [shape(grads.shape, f32)], *args, flops=2 * 10**8)
    spans = {axis: lax.axis_size(axis) for axis in ("seq", "ctx")}
    swaps = [(axis, 1 << k) for axis in ("seq", "ctx") for k in range(spans[axis].bit_length() - 1)]

    def swapped(value, axis, by):
        return lax.ppermute(value, axis, [(i, i ^ by) for i in range(spans[axis])])

    halves, sums = shape((2, cut, width), f32), shape(total.shape, f32)
    firsts = [total]
    if ("seq", 1) in swaps:
        swaps.remove(("seq", 1))
        firsts.append(swapped(total, "seq", 1))
    keep, send, total = call(cut_body, [halves, halves, sums], grads, *firsts)
    grad_x, grad_raw = call(
        functools.partial(output_body, chunks), [shape((heads, size, channels), bf16), shape(raw.shape, f32)],
        *grad_x, cols, rows, v, out_specs=[HBM, VMEM], scratch=[pltpu.SemaphoreType.DMA((chunks,))],
    )
    step = parts // 2
    while step >= 1:
        received = lax.ppermute(send, "head", [(i, i ^ step) for i in range(parts)])
        if swaps:
            got = swapped(total, *swaps.pop())
            keep, total = call(add_body, [shape(keep.shape, f32), sums], keep, total, received, got)
        else:
            keep = keep + received
        step //= 2
        if step >= 1:
            cut = keep.shape[1] // 2
            upper = (lax.axis_index("head") // step) % 2 == 1
            keep, send = (
                jnp.where(upper, keep[:, cut:], keep[:, :cut]),
                jnp.where(upper, keep[:, :cut], keep[:, cut:]),
            )
    while swaps:
        total = total + swapped(total, *swaps.pop())
    return (
        grad_x[None], keep[0][None], keep[1][None], grad_raw[None],
        total[0, :heads], total[1, :heads], total[2, :heads],
    )


def solution(mesh):
    return jax.shard_map(
        on_device,
        mesh=mesh,
        in_specs=(
            P("seq", "head", "ctx", None),
            P("seq", "head", "ctx", None),
            P("seq", "ctx", None),
            P("seq", "ctx", None),
            P("seq", "head", "ctx"),
            P("head"),
            P("head"),
            P("head"),
        ),
        out_specs=(
            P("seq", "head", "ctx", None),
            P("seq", ("ctx", "head"), None),
            P("seq", ("ctx", "head"), None),
            P("seq", "head", "ctx"),
            P("head"),
            P("head"),
            P("head"),
        ),
        check_vma=False,
    )
```

```python
import functools
import jax
import jax.numpy as jnp
from jax import lax
from jax.experimental import pallas as pl
from jax.experimental.pallas import tpu as pltpu
from jax.sharding import PartitionSpec as P

CHUNKS = 2
f32, bf16 = jnp.float32, jnp.bfloat16
highest = lax.Precision.HIGHEST
VMEM = pl.BlockSpec(memory_space=pltpu.VMEM)
HBM = pl.BlockSpec(memory_space=pltpu.HBM)
LIMIT = 48 * 1024 * 1024
shape = jax.ShapeDtypeStruct


def dot(a, b):
    return jnp.dot(a, b, preferred_element_type=f32)


def dot_nt(a, b):
    return lax.dot_general(a, b, (((1,), (1,)), ((), ())), preferred_element_type=f32)


def call(body, outs, *args, flops=10**8, ins=None, out_specs=None, scratch=()):
    return pl.pallas_call(
        body,
        out_shape=outs,
        in_specs=ins or [VMEM] * len(args),
        out_specs=out_specs or [VMEM] * len(outs),
        scratch_shapes=scratch,
        compiler_params=pltpu.CompilerParams(vmem_limit_bytes=LIMIT),
        cost_estimate=pl.CostEstimate(flops=flops // 10**5, bytes_accessed=1 << 8, transcendentals=0),
    )(*args)


def triangle(size, lower):
    rows = lax.broadcasted_iota(jnp.int32, (size, size), 0)
    cols = lax.broadcasted_iota(jnp.int32, (size, size), 1)
    return rows >= cols if lower else cols >= rows


def head_row(values, width):
    heads = values.shape[1]
    rows = lax.broadcasted_iota(jnp.int32, (heads, width), 0)
    cols = lax.broadcasted_iota(jnp.int32, (heads, width), 1)
    spread = jnp.where(rows == cols, 1.0, 0.0).astype(f32)
    return jnp.dot(values, spread, precision=highest, preferred_element_type=f32)


def steps_of(raw, bias, rate, width):
    heads, size = raw.shape
    columns = jnp.concatenate([raw, jnp.zeros((width - heads, size), f32)], axis=0).T
    shifted = columns + bias
    dt = jnp.maximum(shifted, 0.0) + jnp.log1p(jnp.exp(-jnp.abs(shifted)))
    lower = jnp.where(triangle(size, True), 1.0, 0.0).astype(f32)
    return shifted, dt, jnp.dot(lower, -rate * dt, precision=highest, preferred_element_type=f32)


def fetch(pairs, sems):
    copies = [pltpu.make_async_copy(src, dst, sems.at[i]) for i, (src, dst) in enumerate(pairs)]
    for copy in copies:
        copy.start()
    return copies


def own_body(c, raw, cv, rawv, own, sems):
    for copy in fetch(((c, cv), (raw, rawv)), sems):
        copy.wait()
    size, state = c.shape
    heads = raw.shape[0]
    own[:size, :] = cv[...].astype(f32)
    for s in range(size // state):
        own[size + s * heads : size + (s + 1) * heads, :] = rawv[:, s * state : (s + 1) * state]


def load_body(*refs):
    count = len(refs) // 2
    for copy in fetch(zip(refs[:count], refs[count : 2 * count]), refs[-1]):
        copy.wait()


def prepare_body(b, c, raw, a_log, skip, dt_bias, cols_out, low_out, low_t_out, b_t_out, c_t_out, sq_out, rows_out):
    size, width = b.shape
    lanes = lax.broadcasted_iota(jnp.int32, (1, width), 1)
    rate = jnp.where(lanes < a_log.shape[1], jnp.exp(head_row(a_log[...], width)), 0.0)
    bias = head_row(dt_bias[...], width)
    shifted, dt, logs = steps_of(raw[...], bias, rate, width)
    mid = 0.5 * logs[size - 1 : size, :]
    cols_out[0] = jnp.exp(logs - mid)
    cols_out[1] = dt * jnp.exp(mid - logs)
    cols_out[2] = dt
    half = jnp.exp(mid)
    rows_out[...] = jnp.concatenate([half, half * half, rate, head_row(skip[...], width), bias, jnp.zeros((3, width), f32)], axis=0)
    sigma = 1.0 / (1.0 + jnp.exp(-shifted))
    cols_out[3] = sigma
    cols_out[4] = logs
    lower = jnp.where(triangle(size, True), 1.0, 0.0).astype(f32)
    cols_out[5] = jnp.dot(lower, rate * sigma, precision=highest, preferred_element_type=f32)
    sq_out[...] = jnp.exp(2.0 * logs).T
    low_out[...] = jnp.where(triangle(size, True), dot_nt(c[...], b[...]), 0.0).astype(bf16)
    low_t_out[...] = jnp.where(triangle(size, False), dot_nt(b[...], c[...]), 0.0).astype(bf16)
    b_t_out[...] = b[...].T
    c_t_out[...] = c[...].T


def first_body(heads, x, t, cols, low, b_t, c_t, rows, f_out, p_out, xr_out, y_out, err_out):
    for k, h in enumerate(heads):
        xs = x[h].astype(f32)
        g, scale, skip = cols[0, :, h : h + 1], rows[0:1, h : h + 1], rows[3:4, h : h + 1]
        xr = (xs * cols[1, :, h : h + 1]).astype(bf16)
        y = dot(low[...], xr)
        err = g * y + skip * xs - t[h].astype(f32)
        ew = (err * g).astype(bf16)
        xr_out[k] = xr
        y_out[k] = y
        err_out[k] = err
        f_out[k] = scale * dot(b_t[...], xr)
        p_out[k] = scale * dot(c_t[...], ew)


def send_body(chunks, *refs):
    got, refs = refs[0], refs[1:]
    first = lax.axis_index("ctx") == 0
    for f, p, pay in zip(refs[:chunks], refs[chunks : 2 * chunks], refs[2 * chunks :]):
        pay[...] = jnp.where(first, f[...], p[...])
    refs[-1][...] = got[...]


def own_map_body(c, c_t, sq, m_out):
    wide = c_t[...].astype(f32)
    for h in range(m_out.shape[0]):
        m_out[h] = dot((wide * sq[h : h + 1, :]).astype(bf16), c[...])


def later_map_body(step, lowest, rows, got, *refs):
    before, (mc_out, factor_out) = refs[:-2], refs[-2:]
    heads, width = mc_out.shape[0], mc_out.shape[2]
    size = got.shape[0] * width // (width + heads)
    n, place = lax.axis_size("ctx"), lax.axis_index("ctx")
    needed = (place >= lowest) & (place < n - step)
    raw = jnp.concatenate([got[size + s * heads : size + (s + 1) * heads, :] for s in range(size // width)], axis=1)
    _, _, logs = steps_of(raw, rows[4:5, :], rows[2:3, :], width)
    c = jnp.where(needed, got[:size, :], 0.0).astype(bf16)
    c_t = c.T.astype(f32)
    sq = jnp.exp(2.0 * logs).T
    factor = before[1][...] if before else jnp.ones((1, width), f32)
    for h in range(heads):
        added = factor[:, h : h + 1] * dot((c_t * sq[h : h + 1, :]).astype(bf16), c)
        mc_out[h] = before[0][h] + added if before else added
    factor_out[...] = factor * jnp.exp(2.0 * logs[size - 1 : size, :])


def times(m, s):
    high = m.astype(bf16)
    low = (m - high.astype(f32)).astype(bf16)
    s_low = s.astype(bf16)
    return dot(high, s_low) + dot(low, s_low)


def round_body(heads, n, r, f, p, m, mc, rows, got, s_in, d_in, pay_out, s_out, d_out):
    place = lax.axis_index("ctx")
    came_up, came_down = place == r - 1, place == n - r
    for k, h in enumerate(heads):
        s = jnp.where(came_up, got[k], s_in[k])
        d = jnp.where(came_down, got[k], d_in[k])
        s_out[k] = s
        d_out[k] = d
        total = rows[1:2, h : h + 1]
        after = total * s + f[k]
        full = p[k] + times(m[h], s) + total * (d + times(mc[h], after))
        pay_out[k] = jnp.where(place == r - 1, after, full)


def last_body(heads, scales, *refs):
    (x, cols, low, low_t, b, c, rows, xr, y_in, err_in, f, mc, got, s_in, d_in, v_in, sums_in) = refs[:17]
    gx_out, ew_out, s_low_out, a_low_out, v_out, sums_out = refs[17:23]
    n = lax.axis_size("ctx")
    place = lax.axis_index("ctx")
    size, width = b.shape
    channels = x.shape[2]
    lanes = lax.broadcasted_iota(jnp.int32, (1, width), 1)
    v_all, w_all = v_in[0], v_in[1]
    ends, skips = sums_in[0:1, :], sums_in[1:2, :]
    for k, h in enumerate(heads):
        g, r = cols[0, :, h : h + 1], cols[1, :, h : h + 1]
        scale, total, skip = rows[0:1, h : h + 1], rows[1:2, h : h + 1], rows[3:4, h : h + 1]
        s = jnp.where(place == n - 1, got[k], s_in[k]) if n > 1 else s_in[k]
        d = jnp.where(place == 0, got[k], d_in[k]) if n > 1 else d_in[k]
        after = total * s + f[k]
        adjoint = d + times(mc[h], after)
        s_low = (scale * s).astype(bf16)
        a_low = (scale * adjoint).astype(bf16)
        carried = dot(c[...], s_low)
        y = y_in[k] + carried
        err = err_in[k] + g * carried
        ew = (err * g).astype(bf16)
        z = dot(low_t[...], ew) + dot(b[...], a_low)
        gx_out[k] = (r * z + skip * err).astype(bf16)
        here = lanes == h
        v_all = jnp.where(here, jnp.sum(ew.astype(f32) * y, axis=1, keepdims=True), v_all)
        w_all = jnp.where(here, jnp.sum(xr[k].astype(f32) * z, axis=1, keepdims=True), w_all)
        ends = jnp.where(here, jnp.sum(jnp.sum(adjoint * after, axis=0, keepdims=True), axis=1, keepdims=True), ends)
        skips = jnp.where(here, jnp.sum(jnp.sum(err * x[h].astype(f32), axis=0, keepdims=True), axis=1, keepdims=True), skips)
        span = slice(k * channels, (k + 1) * channels)
        ew_out[:, span] = ew
        s_low_out[:, span] = s_low
        a_low_out[:, span] = a_low
    if scales is None:
        v_out[0] = v_all
        v_out[1] = w_all
        sums_out[...] = jnp.concatenate([ends, skips, jnp.zeros((6, width), f32)], axis=0)
        return
    last = lax.broadcasted_iota(jnp.int32, (size, width), 0) == size - 1
    grad_logs = v_all - w_all + jnp.where(last, ends, 0.0)
    by_step = w_all / cols[2]
    v_out[0] = grad_logs
    v_out[1] = by_step
    alog = jnp.sum(grad_logs * cols[4], axis=0, keepdims=True)
    bias = jnp.sum(by_step * cols[3] - grad_logs * cols[5], axis=0, keepdims=True)
    sums_out[...] = jnp.concatenate(
        [alog * scales[0], skips * scales[1], bias * scales[0], jnp.zeros((5, width), f32)], axis=0
    )


def project_body(b, c, xr, ew, s_low, a_low, grads_in, grads_out):
    size = b.shape[0]
    wide = jnp.concatenate([xr[k] for k in range(xr.shape[0])], axis=1)
    score = jnp.where(triangle(size, True), dot_nt(ew[...], wide), 0.0).astype(bf16)
    score_t = jnp.where(triangle(size, False), dot_nt(wide, ew[...]), 0.0).astype(bf16)
    grads_out[0] = grads_in[0] + dot(score_t, c[...]) + dot_nt(wide, a_low[...])
    grads_out[1] = grads_in[1] + dot(score, b[...]) + dot_nt(ew[...], s_low[...])


def cut_body(grads, *refs):
    *sums, keep_out, send_out, sums_out = refs
    cut, size = keep_out.shape[1], grads.shape[1]
    upper = lax.axis_index("head") >= lax.axis_size("head") // 2
    for i in range(2):
        grad = grads[i]
        keep_out[i] = jnp.where(upper, grad[size - cut :, :], grad[:cut, :])
        send_out[i] = jnp.where(upper, grad[:cut, :], grad[size - cut :, :])
    sums_out[...] = sums[0][...] + sums[1][...] if len(sums) > 1 else sums[0][...]


def output_body(chunks, *refs):
    parts, (cols, rows, v), (gx_out, raw_out, sems) = refs[:chunks], refs[chunks : chunks + 3], refs[chunks + 3 :]
    per, size = parts[0].shape[0], v.shape[1]
    copies = fetch([(part, gx_out.at[pl.ds(i * per, per)]) for i, part in enumerate(parts)], sems)
    later = jnp.where(triangle(size, False), 1.0, 0.0).astype(f32)
    log_rate = jnp.dot(later, v[0], precision=highest, preferred_element_type=f32)
    raw_out[...] = ((v[1] - rows[2:3, :] * log_rate) * cols[3]).T[: raw_out.shape[0], :]
    for copy in copies:
        copy.wait()


def add_body(*refs):
    count = len(refs) // 3
    for a, b, out in zip(refs[:count], refs[count : 2 * count], refs[2 * count :]):
        out[...] = a[...] + b[...]


def on_device(x_heads, target, b_proj, c_proj, dt_raw, a_log, skip_gain, dt_bias):
    heads, size, channels = x_heads.shape[1:]
    width = b_proj.shape[2]
    n = lax.axis_size("ctx")
    parts = lax.axis_size("head")
    chunks = CHUNKS if heads % CHUNKS == 0 else 1
    per = heads // chunks
    groups = [tuple(range(i * per, (i + 1) * per)) for i in range(chunks)]
    square, states, all_states = shape((size, size), bf16), shape((per, width, channels), f32), shape((heads, width, width), f32)
    flat = shape((width, size), bf16)
    panel = shape((per, size, channels), f32)

    def held_in_hbm(*arrays):
        return [pltpu.with_memory_space_constraint(a, pltpu.HBM) for a in arrays]

    def like(*arrays):
        return [shape(a.shape, a.dtype) for a in arrays]

    shared = held_in_hbm(c_proj[0], dt_raw[0])
    c, raw, own = call(
        own_body, like(*shared) + [shape((size + heads * size // width, width), f32)], *shared,
        ins=[HBM] * 2, scratch=[pltpu.SemaphoreType.DMA((2,))], flops=10**6,
    )
    rest = held_in_hbm(a_log[None], skip_gain[None], dt_bias[None], b_proj[0], x_heads[0], target[0])
    a_log, skip_gain, dt_bias, b, x, t = call(
        load_body, like(*rest), *rest, ins=[HBM] * 6, scratch=[pltpu.SemaphoreType.DMA((6,))], flops=10**6
    )
    lowest = max(n // 2 - 1, 0)

    def exchange(value, links):
        to, width = dict(links), lax.axis_size("seq")
        if width % 2:
            return lax.ppermute(value, "ctx", links)
        places = [(i, j) for i in range(n) for j in range(width)]
        pairs = [(i * width + j, to[i] * width + j if i in to else i * width + (j ^ 1)) for i, j in places]
        return lax.ppermute(value, ("ctx", "seq"), pairs)

    def down(step, value):
        return exchange(value, [(i + 1, i) for i in range(lowest, n - step)] + [(lowest, n - step)])

    later = down(1, own) if n > 1 else own
    cols, low, low_t, b_t, c_t, sq, rows = call(
        prepare_body,
        [shape((6, size, width), f32), square, square, flat, flat, shape((width, size), f32), shape((8, width), f32)],
        b, c, raw, a_log, skip_gain, dt_bias,
    )
    held = []
    for group in groups:
        f, p, xr, y, err = call(
            functools.partial(first_body, group),
            [states, states, shape(panel.shape, bf16), panel, panel],
            x, t, cols, low, b_t, c_t, rows, flops=4 * 10**8,
        )
        zero = jnp.zeros(states.shape, f32)
        held.append(dict(f=f, p=p, xr=xr, y=y, err=err, s=zero, d=zero))
    *pays, later = call(
        functools.partial(send_body, chunks), [states] * chunks + [shape(own.shape, f32)],
        later, *[h["f"] for h in held], *[h["p"] for h in held],
    )
    for h, pay in zip(held, pays):
        h["pay"] = pay
    (m,) = call(own_map_body, [all_states], c, c_t, sq)
    mc, before = jnp.zeros(all_states.shape, f32), ()
    for step in range(1, n - lowest):
        if step > 1:
            later = down(step, later)
        mc, factor = before = call(functools.partial(later_map_body, step, lowest), [all_states, shape((1, width), f32)], rows, later, *before)

    def swap(r):
        pairs = [(r - 1, r), (r, r - 1)]
        other = [(n - r, n - 1 - r), (n - 1 - r, n - r)]
        return pairs if r - 1 == n - 1 - r else pairs + other

    for stage in range(1, n - 1 + chunks):
        for i, h in enumerate(held):
            r = stage - i
            if not 1 <= r <= n - 1:
                continue
            if r > 1:
                h["pay"], h["s"], h["d"] = call(
                    functools.partial(round_body, groups[i], n, r), [states, states, states],
                    h["f"], h["p"], m, mc, rows, h["got"], h["s"], h["d"],
                )
            h["got"] = exchange(h["pay"], swap(r))

    tokens = size * n * x_heads.shape[0] * lax.axis_size("seq")
    scales = (1.0 / tokens, 1.0 / (tokens * channels))
    cut = size if parts == 1 else size // 2
    v, total = jnp.zeros((2, size, width), f32), jnp.zeros((8, width), f32)
    grads = jnp.zeros((2, size, width), f32)
    grad_x = []
    for i, h in enumerate(held):
        final = i == chunks - 1
        gx, ew, s_low, a_low, v, total = call(
            functools.partial(last_body, groups[i], scales if final else None),
            [shape(panel.shape, bf16), shape((size, per * channels), bf16)] + [shape((width, per * channels), bf16)] * 2
            + [shape(v.shape, f32), shape((8, width), f32)],
            x, cols, low, low_t, b, c, rows, h["xr"], h["y"], h["err"], h["f"], mc,
            h.get("got", h["s"]), h["s"], h["d"], v, total, flops=4 * 10**8,
        )
        grad_x.append(gx)
        args = (b, c, h["xr"], ew, s_low, a_low, grads)
        (grads,) = call(project_body, [shape(grads.shape, f32)], *args, flops=2 * 10**8)
    spans = {axis: lax.axis_size(axis) for axis in ("seq", "ctx")}
    swaps = [(axis, 1 << k) for axis in ("seq", "ctx") for k in range(spans[axis].bit_length() - 1)]

    def swapped(value, axis, by):
        return lax.ppermute(value, axis, [(i, i ^ by) for i in range(spans[axis])])

    halves, sums = shape((2, cut, width), f32), shape(total.shape, f32)
    firsts = [total]
    if ("seq", 1) in swaps:
        swaps.remove(("seq", 1))
        firsts.append(swapped(total, "seq", 1))
    keep, send, total = call(cut_body, [halves, halves, sums], grads, *firsts)
    grad_x, grad_raw = call(
        functools.partial(output_body, chunks), [shape((heads, size, channels), bf16), shape(raw.shape, f32)],
        *grad_x, cols, rows, v, out_specs=[HBM, VMEM], scratch=[pltpu.SemaphoreType.DMA((chunks,))],
    )
    step = parts // 2
    while step >= 1:
        received = lax.ppermute(send, "head", [(i, i ^ step) for i in range(parts)])
        if swaps:
            got = swapped(total, *swaps.pop())
            keep, total = call(add_body, [shape(keep.shape, f32), sums], keep, total, received, got)
        else:
            keep = keep + received
        step //= 2
        if step >= 1:
            cut = keep.shape[1] // 2
            upper = (lax.axis_index("head") // step) % 2 == 1
            keep, send = (
                jnp.where(upper, keep[:, cut:], keep[:, :cut]),
                jnp.where(upper, keep[:, :cut], keep[:, cut:]),
            )
    while swaps:
        total = total + swapped(total, *swaps.pop())
    return (
        grad_x[None], keep[0][None], keep[1][None], grad_raw[None],
        total[0, :heads], total[1, :heads], total[2, :heads],
    )


def solution(mesh):
    return jax.shard_map(
        on_device,
        mesh=mesh,
        in_specs=(
            P("seq", "head", "ctx", None),
            P("seq", "head", "ctx", None),
            P("seq", "ctx", None),
            P("seq", "ctx", None),
            P("seq", "head", "ctx"),
            P("head"),
            P("head"),
            P("head"),
        ),
        out_specs=(
            P("seq", "head", "ctx", None),
            P("seq", ("ctx", "head"), None),
            P("seq", ("ctx", "head"), None),
            P("seq", "head", "ctx"),
            P("head"),
            P("head"),
            P("head"),
        ),
        check_vma=False,
    )
```

```python
import functools
import jax
import jax.numpy as jnp
from jax import lax
from jax.experimental import pallas as pl
from jax.experimental.pallas import tpu as pltpu
from jax.sharding import PartitionSpec as P

CHUNKS = 2
f32, bf16 = jnp.float32, jnp.bfloat16
highest = lax.Precision.HIGHEST
VMEM = pl.BlockSpec(memory_space=pltpu.VMEM)
HBM = pl.BlockSpec(memory_space=pltpu.HBM)
LIMIT = 48 * 1024 * 1024
shape = jax.ShapeDtypeStruct


def dot(a, b):
    return jnp.dot(a, b, preferred_element_type=f32)


def dot_nt(a, b):
    return lax.dot_general(a, b, (((1,), (1,)), ((), ())), preferred_element_type=f32)


def call(body, outs, *args, flops=10**8, ins=None, out_specs=None, scratch=()):
    return pl.pallas_call(
        body,
        out_shape=outs,
        in_specs=ins or [VMEM] * len(args),
        out_specs=out_specs or [VMEM] * len(outs),
        scratch_shapes=scratch,
        compiler_params=pltpu.CompilerParams(vmem_limit_bytes=LIMIT),
        cost_estimate=pl.CostEstimate(flops=flops // 10**5, bytes_accessed=1 << 8, transcendentals=0),
    )(*args)


def triangle(size, lower):
    rows = lax.broadcasted_iota(jnp.int32, (size, size), 0)
    cols = lax.broadcasted_iota(jnp.int32, (size, size), 1)
    return rows >= cols if lower else cols >= rows


def head_row(values, width):
    heads = values.shape[1]
    rows = lax.broadcasted_iota(jnp.int32, (heads, width), 0)
    cols = lax.broadcasted_iota(jnp.int32, (heads, width), 1)
    spread = jnp.where(rows == cols, 1.0, 0.0).astype(f32)
    return jnp.dot(values, spread, precision=highest, preferred_element_type=f32)


def steps_of(raw, bias, rate, width):
    heads, size = raw.shape
    columns = jnp.concatenate([raw, jnp.zeros((width - heads, size), f32)], axis=0).T
    shifted = columns + bias
    dt = jnp.maximum(shifted, 0.0) + jnp.log1p(jnp.exp(-jnp.abs(shifted)))
    lower = jnp.where(triangle(size, True), 1.0, 0.0).astype(f32)
    return shifted, dt, jnp.dot(lower, -rate * dt, precision=highest, preferred_element_type=f32)


def fetch(pairs, sems):
    copies = [pltpu.make_async_copy(src, dst, sems.at[i]) for i, (src, dst) in enumerate(pairs)]
    for copy in copies:
        copy.start()
    return copies


def own_body(c, raw, cv, rawv, own, sems):
    for copy in fetch(((c, cv), (raw, rawv)), sems):
        copy.wait()
    size, state = c.shape
    heads = raw.shape[0]
    own[:size, :] = cv[...].astype(f32)
    for s in range(size // state):
        own[size + s * heads : size + (s + 1) * heads, :] = rawv[:, s * state : (s + 1) * state]


def load_body(*refs):
    count = len(refs) // 2
    for copy in fetch(zip(refs[:count], refs[count : 2 * count]), refs[-1]):
        copy.wait()


def prepare_body(b, c, raw, a_log, skip, dt_bias, cols_out, low_out, low_t_out, b_t_out, c_t_out, sq_out, rows_out, sides_out):
    size, width = b.shape
    lanes = lax.broadcasted_iota(jnp.int32, (1, width), 1)
    rate = jnp.where(lanes < a_log.shape[1], jnp.exp(head_row(a_log[...], width)), 0.0)
    bias = head_row(dt_bias[...], width)
    shifted, dt, logs = steps_of(raw[...], bias, rate, width)
    mid = 0.5 * logs[size - 1 : size, :]
    cols_out[0] = jnp.exp(logs - mid)
    cols_out[1] = dt * jnp.exp(mid - logs)
    cols_out[2] = dt
    half = jnp.exp(mid)
    rows_out[...] = jnp.concatenate([half, half * half, rate, head_row(skip[...], width), bias, jnp.zeros((3, width), f32)], axis=0)
    sigma = 1.0 / (1.0 + jnp.exp(-shifted))
    cols_out[3] = sigma
    cols_out[4] = logs
    lower = jnp.where(triangle(size, True), 1.0, 0.0).astype(f32)
    cols_out[5] = jnp.dot(lower, rate * sigma, precision=highest, preferred_element_type=f32)
    sq_out[...] = jnp.exp(2.0 * logs).T
    sides_out[...] = jnp.concatenate([rate, bias, jnp.zeros((6, width), f32)], axis=0).T
    low_out[...] = jnp.where(triangle(size, True), dot_nt(c[...], b[...]), 0.0).astype(bf16)
    low_t_out[...] = jnp.where(triangle(size, False), dot_nt(b[...], c[...]), 0.0).astype(bf16)
    b_t_out[...] = b[...].T
    c_t_out[...] = c[...].T


def first_body(heads, x, t, cols, low, b_t, c_t, rows, f_out, p_out, xr_out, y_out, err_out):
    for k, h in enumerate(heads):
        xs = x[h].astype(f32)
        g, scale, skip = cols[0, :, h : h + 1], rows[0:1, h : h + 1], rows[3:4, h : h + 1]
        xr = (xs * cols[1, :, h : h + 1]).astype(bf16)
        y = dot(low[...], xr)
        err = g * y + skip * xs - t[h].astype(f32)
        ew = (err * g).astype(bf16)
        xr_out[k] = xr
        y_out[k] = y
        err_out[k] = err
        f_out[k] = scale * dot(b_t[...], xr)
        p_out[k] = scale * dot(c_t[...], ew)


def send_body(f, p, *refs):
    count = len(refs) // 2
    refs[count][...] = jnp.where(lax.axis_index("ctx") == 0, f[...], p[...])
    for relay, out in zip(refs[:count], refs[count + 1 :]):
        out[...] = relay[...]


def own_map_body(c, c_t, sq, m_out):
    wide = c_t[...].astype(f32)
    for h in range(m_out.shape[0]):
        m_out[h] = dot((wide * sq[h : h + 1, :]).astype(bf16), c[...])


def later_map_body(step, lowest, sides, got, *refs):
    before, (mc_out, factor_out) = refs[:-2], refs[-2:]
    heads, width = mc_out.shape[0], mc_out.shape[2]
    size = got.shape[0] * width // (width + heads)
    n, place = lax.axis_size("ctx"), lax.axis_index("ctx")
    needed = (place >= lowest) & (place < n - step)
    raw = jnp.concatenate([got[size + s * heads : size + (s + 1) * heads, :] for s in range(size // width)], axis=1)
    shifted = raw + sides[:heads, 1:2]
    dt = jnp.maximum(shifted, 0.0) + jnp.log1p(jnp.exp(-jnp.abs(shifted)))
    upper = jnp.where(triangle(size, False), 1.0, 0.0).astype(f32)
    logs = jnp.dot(-sides[:heads, 0:1] * dt, upper, precision=highest, preferred_element_type=f32)
    c = jnp.where(needed, got[:size, :], 0.0).astype(bf16)
    c_t = c.T.astype(f32)
    sq = jnp.exp(2.0 * logs)
    factor = before[1][:, 0:1] if before else jnp.ones((heads, 1), f32)
    for h in range(heads):
        added = factor[h : h + 1, :] * dot((c_t * sq[h : h + 1, :]).astype(bf16), c)
        mc_out[h] = before[0][h] + added if before else added
    factor_out[...] = jnp.broadcast_to(factor * sq[:, size - 1 : size], factor_out.shape)


def times(m, s):
    high = m.astype(bf16)
    low = (m - high.astype(f32)).astype(bf16)
    s_low = s.astype(bf16)
    return dot(high, s_low) + dot(low, s_low)


def round_body(heads, n, r, f, p, m, mc, rows, got, s_in, d_in, *refs):
    relays = (len(refs) - 3) // 2
    pay_out, s_out, d_out = refs[relays : relays + 3]
    for relay, out in zip(refs[:relays], refs[relays + 3 :]):
        out[...] = relay[...]
    place = lax.axis_index("ctx")
    came_up, came_down = place == r - 1, place == n - r
    for k, h in enumerate(heads):
        s = jnp.where(came_up, got[k], s_in[k])
        d = jnp.where(came_down, got[k], d_in[k])
        s_out[k] = s
        d_out[k] = d
        total = rows[1:2, h : h + 1]
        after = total * s + f[k]
        full = p[k] + times(m[h], s) + total * (d + times(mc[h], after))
        pay_out[k] = jnp.where(place == r - 1, after, full)


def last_body(heads, scales, *refs):
    (x, cols, low, low_t, b, c, rows, xr, y_in, err_in, f, mc, got, s_in, d_in, v_in, sums_in) = refs[:17]
    gx_out, ew_out, s_low_out, a_low_out, v_out, sums_out = refs[17:]
    n = lax.axis_size("ctx")
    place = lax.axis_index("ctx")
    size, width = b.shape
    channels = x.shape[2]
    lanes = lax.broadcasted_iota(jnp.int32, (1, width), 1)
    v_all, w_all = v_in[0], v_in[1]
    ends, skips = sums_in[0:1, :], sums_in[1:2, :]
    for k, h in enumerate(heads):
        g, r = cols[0, :, h : h + 1], cols[1, :, h : h + 1]
        scale, total, skip = rows[0:1, h : h + 1], rows[1:2, h : h + 1], rows[3:4, h : h + 1]
        s = jnp.where(place == n - 1, got[k], s_in[k]) if n > 1 else s_in[k]
        d = jnp.where(place == 0, got[k], d_in[k]) if n > 1 else d_in[k]
        after = total * s + f[k]
        adjoint = d + times(mc[h], after)
        s_low = (scale * s).astype(bf16)
        a_low = (scale * adjoint).astype(bf16)
        carried = dot(c[...], s_low)
        y = y_in[k] + carried
        err = err_in[k] + g * carried
        ew = (err * g).astype(bf16)
        z = dot(low_t[...], ew) + dot(b[...], a_low)
        gx_out[k] = (r * z + skip * err).astype(bf16)
        here = lanes == h
        v_all = jnp.where(here, jnp.sum(ew.astype(f32) * y, axis=1, keepdims=True), v_all)
        w_all = jnp.where(here, jnp.sum(xr[k].astype(f32) * z, axis=1, keepdims=True), w_all)
        ends = jnp.where(here, jnp.sum(jnp.sum(adjoint * after, axis=0, keepdims=True), axis=1, keepdims=True), ends)
        skips = jnp.where(here, jnp.sum(jnp.sum(err * x[h].astype(f32), axis=0, keepdims=True), axis=1, keepdims=True), skips)
        span = slice(k * channels, (k + 1) * channels)
        ew_out[:, span] = ew
        s_low_out[:, span] = s_low
        a_low_out[:, span] = a_low
    if scales is None:
        v_out[0] = v_all
        v_out[1] = w_all
        sums_out[...] = jnp.concatenate([ends, skips, jnp.zeros((6, width), f32)], axis=0)
        return
    last = lax.broadcasted_iota(jnp.int32, (size, width), 0) == size - 1
    grad_logs = v_all - w_all + jnp.where(last, ends, 0.0)
    by_step = w_all / cols[2]
    v_out[0] = grad_logs
    v_out[1] = by_step
    alog = jnp.sum(grad_logs * cols[4], axis=0, keepdims=True)
    bias = jnp.sum(by_step * cols[3] - grad_logs * cols[5], axis=0, keepdims=True)
    sums_out[...] = jnp.concatenate(
        [alog * scales[0], skips * scales[1], bias * scales[0], jnp.zeros((5, width), f32)], axis=0
    )


def project_body(chunks, b, c, *refs):
    size = b.shape[0]
    grads_out = refs[-1]
    parts = [refs[i * chunks : (i + 1) * chunks] for i in range(4)]
    wide = jnp.concatenate([xr[k] for xr in parts[0] for k in range(xr.shape[0])], axis=1)
    ew, s_low, a_low = [jnp.concatenate([ref[...] for ref in part], axis=1) for part in parts[1:]]
    score = jnp.where(triangle(size, True), dot_nt(ew, wide), 0.0).astype(bf16)
    score_t = jnp.where(triangle(size, False), dot_nt(wide, ew), 0.0).astype(bf16)
    grads_out[0] = dot(score_t, c[...]) + dot_nt(wide, a_low)
    grads_out[1] = dot(score, b[...]) + dot_nt(ew, s_low)


def cut_body(grads, *refs):
    *sums, keep_out, send_out, sums_out = refs
    cut, size = keep_out.shape[1], grads.shape[1]
    upper = lax.axis_index("head") >= lax.axis_size("head") // 2
    for i in range(2):
        grad = grads[i]
        keep_out[i] = jnp.where(upper, grad[size - cut :, :], grad[:cut, :])
        send_out[i] = jnp.where(upper, grad[:cut, :], grad[size - cut :, :])
    sums_out[...] = sums[0][...] + sums[1][...] if len(sums) > 1 else sums[0][...]


def output_body(chunks, *refs):
    parts, (cols, rows, v), (gx_out, raw_out, sems) = refs[:chunks], refs[chunks : chunks + 3], refs[chunks + 3 :]
    size, starts = v.shape[1], [0]
    for part in parts:
        starts.append(starts[-1] + part.shape[0])
    copies = fetch([(part, gx_out.at[pl.ds(start, part.shape[0])]) for part, start in zip(parts, starts)], sems)
    later = jnp.where(triangle(size, False), 1.0, 0.0).astype(f32)
    log_rate = jnp.dot(later, v[0], precision=highest, preferred_element_type=f32)
    raw_out[...] = ((v[1] - rows[2:3, :] * log_rate) * cols[3]).T[: raw_out.shape[0], :]
    for copy in copies:
        copy.wait()


def add_body(*refs):
    count = len(refs) // 3
    for a, b, out in zip(refs[:count], refs[count : 2 * count], refs[2 * count :]):
        out[...] = a[...] + b[...]


def on_device(x_heads, target, b_proj, c_proj, dt_raw, a_log, skip_gain, dt_bias):
    heads, size, channels = x_heads.shape[1:]
    width = b_proj.shape[2]
    n = lax.axis_size("ctx")
    parts = lax.axis_size("head")
    chunks = min(CHUNKS, heads)
    starts = [-(-heads * i // chunks) for i in range(chunks + 1)]
    groups = [tuple(range(start, end)) for start, end in zip(starts, starts[1:])]
    square, all_states = shape((size, size), bf16), shape((heads, width, width), f32)
    flat = shape((width, size), bf16)

    def held_in_hbm(*arrays):
        return [pltpu.with_memory_space_constraint(a, pltpu.HBM) for a in arrays]

    def like(*arrays):
        return [shape(a.shape, a.dtype) for a in arrays]

    shared = held_in_hbm(c_proj[0], dt_raw[0])
    c, raw, own = call(
        own_body, like(*shared) + [shape((size + heads * size // width, width), f32)], *shared,
        ins=[HBM] * 2, scratch=[pltpu.SemaphoreType.DMA((2,))], flops=10**6,
    )
    rest = held_in_hbm(a_log[None], skip_gain[None], dt_bias[None], b_proj[0], x_heads[0], target[0])
    a_log, skip_gain, dt_bias, b, x, t = call(
        load_body, like(*rest), *rest, ins=[HBM] * 6, scratch=[pltpu.SemaphoreType.DMA((6,))], flops=10**6
    )
    lowest = max(n // 2 - 1, 0)

    def exchange(value, links):
        to, width = dict(links), lax.axis_size("seq")
        if width % 2:
            return lax.ppermute(value, "ctx", links)
        places = [(i, j) for i in range(n) for j in range(width)]
        pairs = [(i * width + j, to[i] * width + j if i in to else i * width + (j ^ 1)) for i, j in places]
        return lax.ppermute(value, ("ctx", "seq"), pairs)

    def down(step, value):
        return exchange(value, [(i + 1, i) for i in range(lowest, n - step)] + [(lowest, n - step)])

    later = down(1, own) if n > 1 else own
    cols, low, low_t, b_t, c_t, sq, rows, sides = call(
        prepare_body,
        [shape((6, size, width), f32), square, square, flat, flat, shape((width, size), f32), shape((8, width), f32), shape((width, 8), f32)],
        b, c, raw, a_log, skip_gain, dt_bias,
    )
    held = []
    for group in groups:
        states, panel = shape((len(group), width, channels), f32), (len(group), size, channels)
        f, p, xr, y, err = call(
            functools.partial(first_body, group),
            [states, states, shape(panel, bf16), shape(panel, f32), shape(panel, f32)],
            x, t, cols, low, b_t, c_t, rows, flops=4 * 10**8,
        )
        zero = jnp.zeros(states.shape, f32)
        held.append(dict(f=f, p=p, xr=xr, y=y, err=err, s=zero, d=zero))
    held[0]["pay"], = call(send_body, like(held[0]["f"]), held[0]["f"], held[0]["p"])
    (m,) = call(own_map_body, [all_states], c, c_t, sq)
    for h in held[1:]:
        h["pay"], later = call(send_body, like(h["f"], later), h["f"], h["p"], later)
    layouts = [later]
    for step in range(2, n - lowest):
        layouts.append(down(step, layouts[-1]))

    def with_map(maps, layout):
        step = len(maps)
        mc, factor = call(
            functools.partial(later_map_body, step, lowest), [all_states, shape((heads, width), f32)], sides, layout,
            *(maps[-1] if step > 1 else ()),
        )
        return maps + [(mc, factor)]

    maps = [(jnp.zeros(all_states.shape, f32), None)]
    if n > 1:
        maps = with_map(maps, later)

    def swap(r):
        pairs = [(r - 1, r), (r, r - 1)]
        other = [(n - r, n - 1 - r), (n - 1 - r, n - r)]
        return pairs if r - 1 == n - 1 - r else pairs + other

    for stage in range(1, n - 1 + chunks):
        for i, h in enumerate(held):
            r = stage - i
            if not 1 <= r <= n - 1:
                continue
            if r > 1:
                relays = layouts[1:] if r == 2 and i == 0 else []
                h["pay"], h["s"], h["d"], *relays = call(
                    functools.partial(round_body, groups[i], n, r), like(h["f"]) * 3 + like(*relays),
                    h["f"], h["p"], m, maps[r - 1 if i == 0 and r < len(maps) else -1][0], rows, h["got"], h["s"], h["d"], *relays,
                )
                for relay in relays:
                    maps = with_map(maps, relay)
            h["got"] = exchange(h["pay"], swap(r))

    tokens = size * n * x_heads.shape[0] * lax.axis_size("seq")
    scales = (1.0 / tokens, 1.0 / (tokens * channels))
    cut = size if parts == 1 else size // 2
    v, total = jnp.zeros((2, size, width), f32), jnp.zeros((8, width), f32)
    grad_x = []
    for i, h in enumerate(held):
        final = i == chunks - 1
        gx, h["ew"], h["s_low"], h["a_low"], v, total = call(
            functools.partial(last_body, groups[i], scales if final else None),
            like(h["xr"]) + [shape((extent, len(groups[i]) * channels), bf16) for extent in (size, width, width)]
            + [shape(v.shape, f32), shape((8, width), f32)],
            x, cols, low, low_t, b, c, rows, h["xr"], h["y"], h["err"], h["f"], maps[-1][0],
            h.get("got", h["s"]), h["s"], h["d"], v, total, flops=4 * 10**8,
        )
        grad_x.append(gx)
    (grads,) = call(
        functools.partial(project_body, chunks), [shape((2, size, width), f32)], b, c,
        *[h[part] for part in ("xr", "ew", "s_low", "a_low") for h in held], flops=4 * 10**8,
    )
    spans = {axis: lax.axis_size(axis) for axis in ("seq", "ctx")}
    swaps = [(axis, 1 << k) for axis in ("seq", "ctx") for k in range(spans[axis].bit_length() - 1)]

    def swapped(value, axis, by):
        return lax.ppermute(value, axis, [(i, i ^ by) for i in range(spans[axis])])

    halves, sums = shape((2, cut, width), f32), shape(total.shape, f32)
    firsts = [total]
    if ("seq", 1) in swaps:
        swaps.remove(("seq", 1))
        firsts.append(swapped(total, "seq", 1))
    keep, send, total = call(cut_body, [halves, halves, sums], grads, *firsts)
    grad_x, grad_raw = call(
        functools.partial(output_body, chunks), [shape((heads, size, channels), bf16), shape(raw.shape, f32)],
        *grad_x, cols, rows, v, out_specs=[HBM, VMEM], scratch=[pltpu.SemaphoreType.DMA((chunks,))],
    )
    step = parts // 2
    while step >= 1:
        received = lax.ppermute(send, "head", [(i, i ^ step) for i in range(parts)])
        if swaps:
            got = swapped(total, *swaps.pop())
            keep, total = call(add_body, [shape(keep.shape, f32), sums], keep, total, received, got)
        else:
            keep = keep + received
        step //= 2
        if step >= 1:
            cut = keep.shape[1] // 2
            upper = (lax.axis_index("head") // step) % 2 == 1
            keep, send = (
                jnp.where(upper, keep[:, cut:], keep[:, :cut]),
                jnp.where(upper, keep[:, :cut], keep[:, cut:]),
            )
    while swaps:
        total = total + swapped(total, *swaps.pop())
    return (
        grad_x[None], keep[0][None], keep[1][None], grad_raw[None],
        total[0, :heads], total[1, :heads], total[2, :heads],
    )


def solution(mesh):
    return jax.shard_map(
        on_device,
        mesh=mesh,
        in_specs=(
            P("seq", "head", "ctx", None),
            P("seq", "head", "ctx", None),
            P("seq", "ctx", None),
            P("seq", "ctx", None),
            P("seq", "head", "ctx"),
            P("head"),
            P("head"),
            P("head"),
        ),
        out_specs=(
            P("seq", "head", "ctx", None),
            P("seq", ("ctx", "head"), None),
            P("seq", ("ctx", "head"), None),
            P("seq", "head", "ctx"),
            P("head"),
            P("head"),
            P("head"),
        ),
        check_vma=False,
    )
```

```python
import functools
import jax
import jax.numpy as jnp
from jax import lax
from jax.experimental import pallas as pl
from jax.experimental.pallas import tpu as pltpu
from jax.sharding import PartitionSpec as P

CHUNKS = 2
f32, bf16 = jnp.float32, jnp.bfloat16
highest = lax.Precision.HIGHEST
VMEM = pl.BlockSpec(memory_space=pltpu.VMEM)
HBM = pl.BlockSpec(memory_space=pltpu.HBM)
LIMIT = 48 * 1024 * 1024
shape = jax.ShapeDtypeStruct


def dot(a, b):
    return jnp.dot(a, b, preferred_element_type=f32)


def dot_nt(a, b):
    return lax.dot_general(a, b, (((1,), (1,)), ((), ())), preferred_element_type=f32)


def call(body, outs, *args, flops=10**8, ins=None, out_specs=None, scratch=()):
    return pl.pallas_call(
        body,
        out_shape=outs,
        in_specs=ins or [VMEM] * len(args),
        out_specs=out_specs or [VMEM] * len(outs),
        scratch_shapes=scratch,
        compiler_params=pltpu.CompilerParams(vmem_limit_bytes=LIMIT),
        cost_estimate=pl.CostEstimate(flops=flops // 10**5, bytes_accessed=1 << 8, transcendentals=0),
    )(*args)


def triangle(size, lower):
    rows = lax.broadcasted_iota(jnp.int32, (size, size), 0)
    cols = lax.broadcasted_iota(jnp.int32, (size, size), 1)
    return rows >= cols if lower else cols >= rows


def head_row(values, width):
    heads = values.shape[1]
    rows = lax.broadcasted_iota(jnp.int32, (heads, width), 0)
    cols = lax.broadcasted_iota(jnp.int32, (heads, width), 1)
    spread = jnp.where(rows == cols, 1.0, 0.0).astype(f32)
    return jnp.dot(values, spread, precision=highest, preferred_element_type=f32)


def steps_of(raw, bias, rate, width):
    heads, size = raw.shape
    columns = jnp.concatenate([raw, jnp.zeros((width - heads, size), f32)], axis=0).T
    shifted = columns + bias
    dt = jnp.maximum(shifted, 0.0) + jnp.log1p(jnp.exp(-jnp.abs(shifted)))
    lower = jnp.where(triangle(size, True), 1.0, 0.0).astype(f32)
    return shifted, dt, jnp.dot(lower, -rate * dt, precision=highest, preferred_element_type=f32)


def fetch(pairs, sems):
    copies = [pltpu.make_async_copy(src, dst, sems.at[i]) for i, (src, dst) in enumerate(pairs)]
    for copy in copies:
        copy.start()
    return copies


def own_body(c, raw, cv, rawv, own, sems):
    for copy in fetch(((c, cv), (raw, rawv)), sems):
        copy.wait()
    size, state = c.shape
    heads = raw.shape[0]
    own[:size, :] = cv[...].astype(f32)
    for s in range(size // state):
        own[size + s * heads : size + (s + 1) * heads, :] = rawv[:, s * state : (s + 1) * state]


def load_body(*refs):
    count = len(refs) // 2
    for copy in fetch(zip(refs[:count], refs[count : 2 * count]), refs[-1]):
        copy.wait()


def prepare_body(b, c, raw, a_log, skip, dt_bias, cols_out, low_out, b_t_out, c_t_out, rows_out, shifted_out):
    size, width = b.shape
    lanes = lax.broadcasted_iota(jnp.int32, (1, width), 1)
    rate = jnp.where(lanes < a_log.shape[1], jnp.exp(head_row(a_log[...], width)), 0.0)
    bias = head_row(dt_bias[...], width)
    shifted, dt, logs = steps_of(raw[...], bias, rate, width)
    mid = 0.5 * logs[size - 1 : size, :]
    cols_out[0] = jnp.exp(logs - mid)
    cols_out[1] = dt * jnp.exp(mid - logs)
    cols_out[2] = dt
    cols_out[3] = logs
    half = jnp.exp(mid)
    rows_out[...] = jnp.concatenate([half, half * half, rate, head_row(skip[...], width), bias, jnp.zeros((3, width), f32)], axis=0)
    shifted_out[...] = shifted
    low_out[...] = jnp.where(triangle(size, True), dot_nt(c[...], b[...]), 0.0).astype(bf16)
    b_t_out[...] = b[...].T
    c_t_out[...] = c[...].T


def prepare_more_body(b, c, cols, rows, shifted, low_t_out, sq_out, sides_out, sigmas_out):
    size = b.shape[0]
    low_t_out[...] = jnp.where(triangle(size, False), dot_nt(b[...], c[...]), 0.0).astype(bf16)
    sq_out[...] = jnp.exp(2.0 * cols[3]).T
    rate, bias = rows[2:3, :], rows[4:5, :]
    sides_out[...] = jnp.concatenate([rate, bias, jnp.zeros((6, rate.shape[1]), f32)], axis=0).T
    sigma = 1.0 / (1.0 + jnp.exp(-shifted[...]))
    lower = jnp.where(triangle(size, True), 1.0, 0.0).astype(f32)
    sigmas_out[0] = sigma
    sigmas_out[1] = jnp.dot(lower, rate * sigma, precision=highest, preferred_element_type=f32)


def side_by_side(parts):
    return jnp.concatenate(parts, axis=1)


def first_body(heads, x, t, cols, low, b_t, c_t, rows, f_out, p_out, xr_out, y_out, err_out):
    channels = x.shape[2]
    spans = [slice(k * channels, (k + 1) * channels) for k in range(len(heads))]
    for k, h in enumerate(heads):
        xr_out[k] = (x[h].astype(f32) * cols[1, :, h : h + 1]).astype(bf16)
    wide = side_by_side([xr_out[k] for k in range(len(heads))])
    y, contrib = dot(low[...], wide), dot(b_t[...], wide)
    weighted = []
    for k, h in enumerate(heads):
        g, skip = cols[0, :, h : h + 1], rows[3:4, h : h + 1]
        err = g * y[:, spans[k]] + skip * x[h].astype(f32) - t[h].astype(f32)
        y_out[k] = y[:, spans[k]]
        err_out[k] = err
        weighted.append((err * g).astype(bf16))
    pulled = dot(c_t[...], side_by_side(weighted))
    for k, h in enumerate(heads):
        scale = rows[0:1, h : h + 1]
        f_out[k] = scale * contrib[:, spans[k]]
        p_out[k] = scale * pulled[:, spans[k]]


def send_body(f, p, *refs):
    count = len(refs) // 2
    refs[count][...] = jnp.where(lax.axis_index("ctx") == 0, f[...], p[...])
    for relay, out in zip(refs[:count], refs[count + 1 :]):
        out[...] = relay[...]


def own_map_body(c, c_t, sq, m_out):
    wide = c_t[...].astype(f32)
    for h in range(m_out.shape[0]):
        m_out[h] = dot((wide * sq[h : h + 1, :]).astype(bf16), c[...])


def later_map_body(step, lowest, sides, got, *refs):
    before, (mc_out, factor_out) = refs[:-2], refs[-2:]
    heads, width = mc_out.shape[0], mc_out.shape[2]
    size = got.shape[0] * width // (width + heads)
    n, place = lax.axis_size("ctx"), lax.axis_index("ctx")
    needed = (place >= lowest) & (place < n - step)
    raw = jnp.concatenate([got[size + s * heads : size + (s + 1) * heads, :] for s in range(size // width)], axis=1)
    shifted = raw + sides[:heads, 1:2]
    dt = jnp.maximum(shifted, 0.0) + jnp.log1p(jnp.exp(-jnp.abs(shifted)))
    upper = jnp.where(triangle(size, False), 1.0, 0.0).astype(f32)
    logs = jnp.dot(-sides[:heads, 0:1] * dt, upper, precision=highest, preferred_element_type=f32)
    c = jnp.where(needed, got[:size, :], 0.0).astype(bf16)
    c_t = c.T.astype(f32)
    sq = jnp.exp(2.0 * logs)
    factor = before[1][:, 0:1] if before else jnp.ones((heads, 1), f32)
    for h in range(heads):
        added = factor[h : h + 1, :] * dot((c_t * sq[h : h + 1, :]).astype(bf16), c)
        mc_out[h] = before[0][h] + added if before else added
    factor_out[...] = jnp.broadcast_to(factor * sq[:, size - 1 : size], factor_out.shape)


def times(m, s):
    high = m.astype(bf16)
    low = (m - high.astype(f32)).astype(bf16)
    s_low = s.astype(bf16)
    return dot(side_by_side([high, low]), jnp.concatenate([s_low, s_low], axis=0))


def round_body(heads, n, r, f, p, m, mc, rows, got, s_in, d_in, *refs):
    relays = (len(refs) - 3) // 2
    pay_out, s_out, d_out = refs[relays : relays + 3]
    for relay, out in zip(refs[:relays], refs[relays + 3 :]):
        out[...] = relay[...]
    place = lax.axis_index("ctx")
    came_up, came_down = place == r - 1, place == n - r
    for k, h in enumerate(heads):
        s = jnp.where(came_up, got[k], s_in[k])
        d = jnp.where(came_down, got[k], d_in[k])
        s_out[k] = s
        d_out[k] = d
        total = rows[1:2, h : h + 1]
        after = total * s + f[k]
        full = p[k] + total * (d + times(mc[h], after))
        if n - r < r:
            full = full + times(m[h], s)
        pay_out[k] = jnp.where(place == r - 1, after, full)


def last_body(heads, scales, *refs):
    (x, cols, sigmas, low_t, b, c, rows, xr, y_in, err_in, f, mc, got, s_in, d_in, v_in, sums_in) = refs[:17]
    gx_out, ew_out, s_low_out, a_low_out, v_out, sums_out = refs[17:]
    n = lax.axis_size("ctx")
    place = lax.axis_index("ctx")
    size, width = b.shape
    channels = x.shape[2]
    lanes = lax.broadcasted_iota(jnp.int32, (1, width), 1)
    v_all, w_all = v_in[0], v_in[1]
    ends, skips = sums_in[0:1, :], sums_in[1:2, :]
    spans = [slice(k * channels, (k + 1) * channels) for k in range(len(heads))]
    states, adjoints = [], []
    for k, h in enumerate(heads):
        scale, total = rows[0:1, h : h + 1], rows[1:2, h : h + 1]
        s = jnp.where(place == n - 1, got[k], s_in[k]) if n > 1 else s_in[k]
        d = jnp.where(place == 0, got[k], d_in[k]) if n > 1 else d_in[k]
        after = total * s + f[k]
        adjoint = d + times(mc[h], after)
        states.append((scale * s).astype(bf16))
        adjoints.append((scale * adjoint).astype(bf16))
        ends = jnp.where(lanes == h, jnp.sum(jnp.sum(adjoint * after, axis=0, keepdims=True), axis=1, keepdims=True), ends)
    states, adjoints = side_by_side(states), side_by_side(adjoints)
    carried = dot(c[...], states)
    errs, weighted = [], []
    for k, h in enumerate(heads):
        g = cols[0, :, h : h + 1]
        errs.append(err_in[k] + g * carried[:, spans[k]])
        weighted.append((errs[k] * g).astype(bf16))
    wide = side_by_side(weighted)
    z = dot(low_t[...], wide) + dot(b[...], adjoints)
    for k, h in enumerate(heads):
        here, err, own = lanes == h, errs[k], z[:, spans[k]]
        y = y_in[k] + carried[:, spans[k]]
        gx_out[k] = (cols[1, :, h : h + 1] * own + rows[3:4, h : h + 1] * err).astype(bf16)
        v_all = jnp.where(here, jnp.sum(weighted[k].astype(f32) * y, axis=1, keepdims=True), v_all)
        w_all = jnp.where(here, jnp.sum(xr[k].astype(f32) * own, axis=1, keepdims=True), w_all)
        skips = jnp.where(here, jnp.sum(jnp.sum(err * x[h].astype(f32), axis=0, keepdims=True), axis=1, keepdims=True), skips)
    ew_out[...] = wide
    s_low_out[...] = states
    a_low_out[...] = adjoints
    if scales is None:
        v_out[0] = v_all
        v_out[1] = w_all
        sums_out[...] = jnp.concatenate([ends, skips, jnp.zeros((6, width), f32)], axis=0)
        return
    last = lax.broadcasted_iota(jnp.int32, (size, width), 0) == size - 1
    grad_logs = v_all - w_all + jnp.where(last, ends, 0.0)
    by_step = w_all / cols[2]
    v_out[0] = grad_logs
    v_out[1] = by_step
    alog = jnp.sum(grad_logs * cols[3], axis=0, keepdims=True)
    bias = jnp.sum(by_step * sigmas[0] - grad_logs * sigmas[1], axis=0, keepdims=True)
    sums_out[...] = jnp.concatenate(
        [alog * scales[0], skips * scales[1], bias * scales[0], jnp.zeros((5, width), f32)], axis=0
    )


def project_body(chunks, b, c, *refs):
    size = b.shape[0]
    grads_out = refs[-1]
    parts = [refs[i * chunks : (i + 1) * chunks] for i in range(4)]
    wide = jnp.concatenate([xr[k] for xr in parts[0] for k in range(xr.shape[0])], axis=1)
    ew, s_low, a_low = [jnp.concatenate([ref[...] for ref in part], axis=1) for part in parts[1:]]
    score = jnp.where(triangle(size, True), dot_nt(ew, wide), 0.0).astype(bf16)
    score_t = jnp.where(triangle(size, False), dot_nt(wide, ew), 0.0).astype(bf16)
    grads_out[0] = dot(score_t, c[...]) + dot_nt(wide, a_low)
    grads_out[1] = dot(score, b[...]) + dot_nt(ew, s_low)


def cut_body(grads, *refs):
    *sums, keep_out, send_out, sums_out = refs
    cut, size = keep_out.shape[1], grads.shape[1]
    upper = lax.axis_index("head") >= lax.axis_size("head") // 2
    for i in range(2):
        grad = grads[i]
        keep_out[i] = jnp.where(upper, grad[size - cut :, :], grad[:cut, :])
        send_out[i] = jnp.where(upper, grad[:cut, :], grad[size - cut :, :])
    sums_out[...] = sums[0][...] + sums[1][...] if len(sums) > 1 else sums[0][...]


def output_body(chunks, *refs):
    parts, (sigmas, rows, v), (gx_out, raw_out, sems) = refs[:chunks], refs[chunks : chunks + 3], refs[chunks + 3 :]
    size, starts = v.shape[1], [0]
    for part in parts:
        starts.append(starts[-1] + part.shape[0])
    copies = fetch([(part, gx_out.at[pl.ds(start, part.shape[0])]) for part, start in zip(parts, starts)], sems)
    later = jnp.where(triangle(size, False), 1.0, 0.0).astype(f32)
    log_rate = jnp.dot(later, v[0], precision=highest, preferred_element_type=f32)
    raw_out[...] = ((v[1] - rows[2:3, :] * log_rate) * sigmas[0]).T[: raw_out.shape[0], :]
    for copy in copies:
        copy.wait()


def add_body(*refs):
    count = len(refs) // 3
    for a, b, out in zip(refs[:count], refs[count : 2 * count], refs[2 * count :]):
        out[...] = a[...] + b[...]


def on_device(x_heads, target, b_proj, c_proj, dt_raw, a_log, skip_gain, dt_bias):
    heads, size, channels = x_heads.shape[1:]
    width = b_proj.shape[2]
    n = lax.axis_size("ctx")
    parts = lax.axis_size("head")
    chunks = min(CHUNKS, heads)
    starts = [-(-heads * i // chunks) for i in range(chunks + 1)]
    groups = [tuple(range(start, end)) for start, end in zip(starts, starts[1:])]
    square, all_states = shape((size, size), bf16), shape((heads, width, width), f32)
    flat = shape((width, size), bf16)

    def held_in_hbm(*arrays):
        return [pltpu.with_memory_space_constraint(a, pltpu.HBM) for a in arrays]

    def like(*arrays):
        return [shape(a.shape, a.dtype) for a in arrays]

    shared = held_in_hbm(c_proj[0], dt_raw[0])
    c, raw, own = call(
        own_body, like(*shared) + [shape((size + heads * size // width, width), f32)], *shared,
        ins=[HBM] * 2, scratch=[pltpu.SemaphoreType.DMA((2,))], flops=10**6,
    )
    rest = held_in_hbm(a_log[None], skip_gain[None], dt_bias[None], b_proj[0], x_heads[0], target[0])
    a_log, skip_gain, dt_bias, b, x, t = call(
        load_body, like(*rest), *rest, ins=[HBM] * 6, scratch=[pltpu.SemaphoreType.DMA((6,))], flops=10**6
    )
    lowest = max(n // 2 - 1, 0)

    def exchange(value, links):
        to, width = dict(links), lax.axis_size("seq")
        if width % 2:
            return lax.ppermute(value, "ctx", links)
        places = [(i, j) for i in range(n) for j in range(width)]
        pairs = [(i * width + j, to[i] * width + j if i in to else i * width + (j ^ 1)) for i, j in places]
        return lax.ppermute(value, ("ctx", "seq"), pairs)

    def down(step, value):
        return exchange(value, [(i + 1, i) for i in range(lowest, n - step)] + [(lowest, n - step)])

    later = down(1, own) if n > 1 else own
    row, sheet = shape((8, width), f32), shape((size, width), f32)
    cols, low, b_t, c_t, rows, shifted = call(
        prepare_body, [shape((4, size, width), f32), square, flat, flat, row, sheet], b, c, raw, a_log, skip_gain, dt_bias
    )
    low_t, sq, sides, sigmas = call(
        prepare_more_body, [square, shape((width, size), f32), shape((width, 8), f32), shape((2, size, width), f32)],
        b, c, cols, rows, shifted,
    )
    held = []
    for group in groups:
        states, panel = shape((len(group), width, channels), f32), (len(group), size, channels)
        f, p, xr, y, err = call(
            functools.partial(first_body, group),
            [states, states, shape(panel, bf16), shape(panel, f32), shape(panel, f32)],
            x, t, cols, low, b_t, c_t, rows, flops=4 * 10**8,
        )
        zero = jnp.zeros(states.shape, f32)
        held.append(dict(f=f, p=p, xr=xr, y=y, err=err, s=zero, d=zero))
    held[0]["pay"], = call(send_body, like(held[0]["f"]), held[0]["f"], held[0]["p"])
    (m,) = call(own_map_body, [all_states], c, c_t, sq)
    for h in held[1:]:
        h["pay"], later = call(send_body, like(h["f"], later), h["f"], h["p"], later)
    layouts = [later]
    for step in range(2, n - lowest):
        layouts.append(down(step, layouts[-1]))

    def with_map(maps, layout):
        step = len(maps)
        mc, factor = call(
            functools.partial(later_map_body, step, lowest), [all_states, shape((heads, width), f32)], sides, layout,
            *(maps[-1] if step > 1 else ()),
        )
        return maps + [(mc, factor)]

    maps = [(jnp.zeros(all_states.shape, f32), None)]
    if n > 1:
        maps = with_map(maps, later)

    def swap(r):
        pairs = [(r - 1, r), (r, r - 1)]
        other = [(n - r, n - 1 - r), (n - 1 - r, n - r)]
        return pairs if r - 1 == n - 1 - r else pairs + other

    for stage in range(1, n - 1 + chunks):
        for i, h in enumerate(held):
            r = stage - i
            if not 1 <= r <= n - 1:
                continue
            if r > 1:
                relays = layouts[1:] if r == 2 and i == 0 else []
                h["pay"], h["s"], h["d"], *relays = call(
                    functools.partial(round_body, groups[i], n, r), like(h["f"]) * 3 + like(*relays),
                    h["f"], h["p"], m, maps[r - 1 if i == 0 and r < len(maps) else -1][0], rows, h["got"], h["s"], h["d"], *relays,
                )
                for relay in relays:
                    maps = with_map(maps, relay)
            h["got"] = exchange(h["pay"], swap(r))

    tokens = size * n * x_heads.shape[0] * lax.axis_size("seq")
    scales = (1.0 / tokens, 1.0 / (tokens * channels))
    cut = size if parts == 1 else size // 2
    v, total = jnp.zeros((2, size, width), f32), jnp.zeros((8, width), f32)
    grad_x = []
    for i, h in enumerate(held):
        final = i == chunks - 1
        gx, h["ew"], h["s_low"], h["a_low"], v, total = call(
            functools.partial(last_body, groups[i], scales if final else None),
            like(h["xr"]) + [shape((extent, len(groups[i]) * channels), bf16) for extent in (size, width, width)]
            + [shape(v.shape, f32), shape((8, width), f32)],
            x, cols, sigmas, low_t, b, c, rows, h["xr"], h["y"], h["err"], h["f"], maps[-1][0],
            h.get("got", h["s"]), h["s"], h["d"], v, total, flops=4 * 10**8,
        )
        grad_x.append(gx)
    (grads,) = call(
        functools.partial(project_body, chunks), [shape((2, size, width), f32)], b, c,
        *[h[part] for part in ("xr", "ew", "s_low", "a_low") for h in held], flops=4 * 10**8,
    )
    spans = {axis: lax.axis_size(axis) for axis in ("seq", "ctx")}
    swaps = [(axis, 1 << k) for axis in ("seq", "ctx") for k in range(spans[axis].bit_length() - 1)]

    def swapped(value, axis, by):
        return lax.ppermute(value, axis, [(i, i ^ by) for i in range(spans[axis])])

    halves, sums = shape((2, cut, width), f32), shape(total.shape, f32)
    firsts = [total]
    if ("seq", 1) in swaps:
        swaps.remove(("seq", 1))
        firsts.append(swapped(total, "seq", 1))
    keep, send, total = call(cut_body, [halves, halves, sums], grads, *firsts)
    grad_x, grad_raw = call(
        functools.partial(output_body, chunks), [shape((heads, size, channels), bf16), shape(raw.shape, f32)],
        *grad_x, sigmas, rows, v, out_specs=[HBM, VMEM], scratch=[pltpu.SemaphoreType.DMA((chunks,))],
    )
    step = parts // 2
    while step >= 1:
        received = lax.ppermute(send, "head", [(i, i ^ step) for i in range(parts)])
        if swaps:
            got = swapped(total, *swaps.pop())
            keep, total = call(add_body, [shape(keep.shape, f32), sums], keep, total, received, got)
        else:
            keep = keep + received
        step //= 2
        if step >= 1:
            cut = keep.shape[1] // 2
            upper = (lax.axis_index("head") // step) % 2 == 1
            keep, send = (
                jnp.where(upper, keep[:, cut:], keep[:, :cut]),
                jnp.where(upper, keep[:, :cut], keep[:, cut:]),
            )
    while swaps:
        total = total + swapped(total, *swaps.pop())
    return (
        grad_x[None], keep[0][None], keep[1][None], grad_raw[None],
        total[0, :heads], total[1, :heads], total[2, :heads],
    )


def solution(mesh):
    return jax.shard_map(
        on_device,
        mesh=mesh,
        in_specs=(
            P("seq", "head", "ctx", None),
            P("seq", "head", "ctx", None),
            P("seq", "ctx", None),
            P("seq", "ctx", None),
            P("seq", "head", "ctx"),
            P("head"),
            P("head"),
            P("head"),
        ),
        out_specs=(
            P("seq", "head", "ctx", None),
            P("seq", ("ctx", "head"), None),
            P("seq", ("ctx", "head"), None),
            P("seq", "head", "ctx"),
            P("head"),
            P("head"),
            P("head"),
        ),
        check_vma=False,
    )
```

```python
import functools
import jax
import jax.numpy as jnp
from jax import lax
from jax.experimental import pallas as pl
from jax.experimental.pallas import tpu as pltpu
from jax.sharding import PartitionSpec as P

CHUNKS = 2
f32, bf16 = jnp.float32, jnp.bfloat16
highest = lax.Precision.HIGHEST
VMEM = pl.BlockSpec(memory_space=pltpu.VMEM)
HBM = pl.BlockSpec(memory_space=pltpu.HBM)
LIMIT = 48 * 1024 * 1024
shape = jax.ShapeDtypeStruct


def dot(a, b):
    return jnp.dot(a, b, preferred_element_type=f32)


def dot_nt(a, b):
    return lax.dot_general(a, b, (((1,), (1,)), ((), ())), preferred_element_type=f32)


def call(body, outs, *args, flops=10**8, ins=None, out_specs=None, scratch=()):
    return pl.pallas_call(
        body,
        out_shape=outs,
        in_specs=ins or [VMEM] * len(args),
        out_specs=out_specs or [VMEM] * len(outs),
        scratch_shapes=scratch,
        compiler_params=pltpu.CompilerParams(vmem_limit_bytes=LIMIT),
        cost_estimate=pl.CostEstimate(flops=flops // 10**5, bytes_accessed=1 << 8, transcendentals=0),
    )(*args)


def triangle(size, lower):
    rows = lax.broadcasted_iota(jnp.int32, (size, size), 0)
    cols = lax.broadcasted_iota(jnp.int32, (size, size), 1)
    return rows >= cols if lower else cols >= rows


def head_row(values, width):
    heads = values.shape[1]
    rows = lax.broadcasted_iota(jnp.int32, (heads, width), 0)
    cols = lax.broadcasted_iota(jnp.int32, (heads, width), 1)
    spread = jnp.where(rows == cols, 1.0, 0.0).astype(f32)
    return jnp.dot(values, spread, precision=highest, preferred_element_type=f32)


def steps_of(raw, bias, rate, width):
    heads, size = raw.shape
    columns = jnp.concatenate([raw, jnp.zeros((width - heads, size), f32)], axis=0).T
    shifted = columns + bias
    dt = jnp.maximum(shifted, 0.0) + jnp.log1p(jnp.exp(-jnp.abs(shifted)))
    lower = jnp.where(triangle(size, True), 1.0, 0.0).astype(f32)
    return shifted, dt, jnp.dot(lower, -rate * dt, precision=highest, preferred_element_type=f32)


def fetch(pairs, sems):
    copies = [pltpu.make_async_copy(src, dst, sems.at[i]) for i, (src, dst) in enumerate(pairs)]
    for copy in copies:
        copy.start()
    return copies


def load_body(*refs):
    count = len(refs) // 2 - 1
    copies = fetch(zip(refs[:count], refs[count : 2 * count]), refs[-1])
    for copy in copies[:2]:
        copy.wait()
    (c, raw), own = refs[count : count + 2], refs[-2]
    size, state = c.shape
    heads = raw.shape[0]
    own[:size, :] = c[...].astype(f32)
    for s in range(size // state):
        own[size + s * heads : size + (s + 1) * heads, :] = raw[:, s * state : (s + 1) * state]
    for copy in copies[2:]:
        copy.wait()


def prepare_body(b, c, raw, a_log, skip, dt_bias, cols_out, low_out, b_t_out, c_t_out, rows_out, shifted_out):
    size, width = b.shape
    lanes = lax.broadcasted_iota(jnp.int32, (1, width), 1)
    rate = jnp.where(lanes < a_log.shape[1], jnp.exp(head_row(a_log[...], width)), 0.0)
    bias = head_row(dt_bias[...], width)
    shifted, dt, logs = steps_of(raw[...], bias, rate, width)
    mid = 0.5 * logs[size - 1 : size, :]
    cols_out[0] = jnp.exp(logs - mid)
    cols_out[1] = dt * jnp.exp(mid - logs)
    cols_out[2] = dt
    cols_out[3] = logs
    half = jnp.exp(mid)
    rows_out[...] = jnp.concatenate([half, half * half, rate, head_row(skip[...], width), bias, jnp.zeros((3, width), f32)], axis=0)
    shifted_out[...] = shifted
    low_out[...] = jnp.where(triangle(size, True), dot_nt(c[...], b[...]), 0.0).astype(bf16)
    b_t_out[...] = b[...].T
    c_t_out[...] = c[...].T


def prepare_more_body(b, c, cols, rows, shifted, low_t_out, sq_out, sides_out, sigmas_out):
    size = b.shape[0]
    low_t_out[...] = jnp.where(triangle(size, False), dot_nt(b[...], c[...]), 0.0).astype(bf16)
    sq_out[...] = jnp.exp(2.0 * cols[3]).T
    rate, bias = rows[2:3, :], rows[4:5, :]
    sides_out[...] = jnp.concatenate([rate, bias, jnp.zeros((6, rate.shape[1]), f32)], axis=0).T
    sigma = 1.0 / (1.0 + jnp.exp(-shifted[...]))
    lower = jnp.where(triangle(size, True), 1.0, 0.0).astype(f32)
    sigmas_out[0] = sigma
    sigmas_out[1] = jnp.dot(lower, rate * sigma, precision=highest, preferred_element_type=f32)


def side_by_side(parts):
    return jnp.concatenate(parts, axis=1)


def first_body(heads, x, t, cols, low, b_t, c_t, rows, f_out, p_out, xr_out, y_out, err_out):
    channels = x.shape[2]
    spans = [slice(k * channels, (k + 1) * channels) for k in range(len(heads))]
    for k, h in enumerate(heads):
        xr_out[k] = (x[h].astype(f32) * cols[1, :, h : h + 1]).astype(bf16)
    wide = side_by_side([xr_out[k] for k in range(len(heads))])
    y, contrib = dot(low[...], wide), dot(b_t[...], wide)
    weighted = []
    for k, h in enumerate(heads):
        g, skip = cols[0, :, h : h + 1], rows[3:4, h : h + 1]
        err = g * y[:, spans[k]] + skip * x[h].astype(f32) - t[h].astype(f32)
        y_out[k] = y[:, spans[k]]
        err_out[k] = err
        weighted.append((err * g).astype(bf16))
    pulled = dot(c_t[...], side_by_side(weighted))
    for k, h in enumerate(heads):
        scale = rows[0:1, h : h + 1]
        f_out[k] = scale * contrib[:, spans[k]]
        p_out[k] = scale * pulled[:, spans[k]]


def send_body(f, p, *refs):
    count = len(refs) // 2
    refs[count][...] = jnp.where(lax.axis_index("ctx") == 0, f[...], p[...])
    for relay, out in zip(refs[:count], refs[count + 1 :]):
        out[...] = relay[...]


def own_map_body(c, c_t, sq, m_out):
    wide = c_t[...].astype(f32)
    for h in range(m_out.shape[0]):
        m_out[h] = dot((wide * sq[h : h + 1, :]).astype(bf16), c[...])


def later_map_body(step, lowest, sides, got, *refs):
    before, (mc_out, factor_out) = refs[:-2], refs[-2:]
    heads, width = mc_out.shape[0], mc_out.shape[2]
    size = got.shape[0] * width // (width + heads)
    n, place = lax.axis_size("ctx"), lax.axis_index("ctx")
    needed = (place >= lowest) & (place < n - step)
    raw = jnp.concatenate([got[size + s * heads : size + (s + 1) * heads, :] for s in range(size // width)], axis=1)
    shifted = raw + sides[:heads, 1:2]
    dt = jnp.maximum(shifted, 0.0) + jnp.log1p(jnp.exp(-jnp.abs(shifted)))
    upper = jnp.where(triangle(size, False), 1.0, 0.0).astype(f32)
    logs = jnp.dot(-sides[:heads, 0:1] * dt, upper, precision=highest, preferred_element_type=f32)
    c = jnp.where(needed, got[:size, :], 0.0).astype(bf16)
    c_t = c.T.astype(f32)
    sq = jnp.exp(2.0 * logs)
    factor = before[1][:, 0:1] if before else jnp.ones((heads, 1), f32)
    for h in range(heads):
        added = factor[h : h + 1, :] * dot((c_t * sq[h : h + 1, :]).astype(bf16), c)
        mc_out[h] = before[0][h] + added if before else added
    factor_out[...] = jnp.broadcast_to(factor * sq[:, size - 1 : size], factor_out.shape)


def times(m, s):
    high = m.astype(bf16)
    low = (m - high.astype(f32)).astype(bf16)
    s_low = s.astype(bf16)
    return dot(side_by_side([high, low]), jnp.concatenate([s_low, s_low], axis=0))


def round_body(heads, n, r, f, p, m, mc, rows, got, s_in, d_in, *refs):
    relays = (len(refs) - 3) // 2
    pay_out, s_out, d_out = refs[relays : relays + 3]
    for relay, out in zip(refs[:relays], refs[relays + 3 :]):
        out[...] = relay[...]
    place = lax.axis_index("ctx")
    came_up, came_down = place == r - 1, place == n - r
    for k, h in enumerate(heads):
        s = jnp.where(came_up, got[k], s_in[k])
        d = jnp.where(came_down, got[k], d_in[k])
        s_out[k] = s
        d_out[k] = d
        total = rows[1:2, h : h + 1]
        after = total * s + f[k]
        full = p[k] + total * (d + times(mc[h], after))
        if n - r < r:
            full = full + times(m[h], s)
        pay_out[k] = jnp.where(place == r - 1, after, full)


def last_body(heads, scales, *refs):
    (x, cols, sigmas, low_t, b, c, rows, xr, y_in, err_in, f, mc, got, s_in, d_in, v_in, sums_in) = refs[:17]
    gx_out, ew_out, s_low_out, a_low_out, v_out, sums_out = refs[17:]
    n = lax.axis_size("ctx")
    place = lax.axis_index("ctx")
    size, width = b.shape
    channels = x.shape[2]
    lanes = lax.broadcasted_iota(jnp.int32, (1, width), 1)
    v_all, w_all = v_in[0], v_in[1]
    ends, skips = sums_in[0:1, :], sums_in[1:2, :]
    spans = [slice(k * channels, (k + 1) * channels) for k in range(len(heads))]
    states, adjoints = [], []
    for k, h in enumerate(heads):
        scale, total = rows[0:1, h : h + 1], rows[1:2, h : h + 1]
        s = jnp.where(place == n - 1, got[k], s_in[k]) if n > 1 else s_in[k]
        d = jnp.where(place == 0, got[k], d_in[k]) if n > 1 else d_in[k]
        after = total * s + f[k]
        adjoint = d + times(mc[h], after)
        states.append((scale * s).astype(bf16))
        adjoints.append((scale * adjoint).astype(bf16))
        ends = jnp.where(lanes == h, jnp.sum(jnp.sum(adjoint * after, axis=0, keepdims=True), axis=1, keepdims=True), ends)
    states, adjoints = side_by_side(states), side_by_side(adjoints)
    carried = dot(c[...], states)
    errs, weighted = [], []
    for k, h in enumerate(heads):
        g = cols[0, :, h : h + 1]
        errs.append(err_in[k] + g * carried[:, spans[k]])
        weighted.append((errs[k] * g).astype(bf16))
    wide = side_by_side(weighted)
    z = dot(low_t[...], wide) + dot(b[...], adjoints)
    for k, h in enumerate(heads):
        here, err, own = lanes == h, errs[k], z[:, spans[k]]
        y = y_in[k] + carried[:, spans[k]]
        gx_out[k] = (cols[1, :, h : h + 1] * own + rows[3:4, h : h + 1] * err).astype(bf16)
        v_all = jnp.where(here, jnp.sum(weighted[k].astype(f32) * y, axis=1, keepdims=True), v_all)
        w_all = jnp.where(here, jnp.sum(xr[k].astype(f32) * own, axis=1, keepdims=True), w_all)
        skips = jnp.where(here, jnp.sum(jnp.sum(err * x[h].astype(f32), axis=0, keepdims=True), axis=1, keepdims=True), skips)
    ew_out[...] = wide
    s_low_out[...] = states
    a_low_out[...] = adjoints
    if scales is None:
        v_out[0] = v_all
        v_out[1] = w_all
        sums_out[...] = jnp.concatenate([ends, skips, jnp.zeros((6, width), f32)], axis=0)
        return
    last = lax.broadcasted_iota(jnp.int32, (size, width), 0) == size - 1
    grad_logs = v_all - w_all + jnp.where(last, ends, 0.0)
    by_step = w_all / cols[2]
    v_out[0] = grad_logs
    v_out[1] = by_step
    alog = jnp.sum(grad_logs * cols[3], axis=0, keepdims=True)
    bias = jnp.sum(by_step * sigmas[0] - grad_logs * sigmas[1], axis=0, keepdims=True)
    sums_out[...] = jnp.concatenate(
        [alog * scales[0], skips * scales[1], bias * scales[0], jnp.zeros((5, width), f32)], axis=0
    )


def project_body(chunks, b, c, *refs):
    size = b.shape[0]
    grads_out = refs[-1]
    parts = [refs[i * chunks : (i + 1) * chunks] for i in range(4)]
    wide = jnp.concatenate([xr[k] for xr in parts[0] for k in range(xr.shape[0])], axis=1)
    ew, s_low, a_low = [jnp.concatenate([ref[...] for ref in part], axis=1) for part in parts[1:]]
    score = jnp.where(triangle(size, True), dot_nt(ew, wide), 0.0).astype(bf16)
    score_t = jnp.where(triangle(size, False), dot_nt(wide, ew), 0.0).astype(bf16)
    grads_out[0] = dot(score_t, c[...]) + dot_nt(wide, a_low)
    grads_out[1] = dot(score, b[...]) + dot_nt(ew, s_low)


def cut_body(grads, *refs):
    *sums, keep_out, send_out, sums_out = refs
    cut, size = keep_out.shape[1], grads.shape[1]
    upper = lax.axis_index("head") >= lax.axis_size("head") // 2
    for i in range(2):
        grad = grads[i]
        keep_out[i] = jnp.where(upper, grad[size - cut :, :], grad[:cut, :])
        send_out[i] = jnp.where(upper, grad[:cut, :], grad[size - cut :, :])
    sums_out[...] = sums[0][...] + sums[1][...] if len(sums) > 1 else sums[0][...]


def output_body(chunks, *refs):
    parts, (sigmas, rows, v), (gx_out, raw_out, sems) = refs[:chunks], refs[chunks : chunks + 3], refs[chunks + 3 :]
    size, starts = v.shape[1], [0]
    for part in parts:
        starts.append(starts[-1] + part.shape[0])
    copies = fetch([(part, gx_out.at[pl.ds(start, part.shape[0])]) for part, start in zip(parts, starts)], sems)
    later = jnp.where(triangle(size, False), 1.0, 0.0).astype(f32)
    log_rate = jnp.dot(later, v[0], precision=highest, preferred_element_type=f32)
    raw_out[...] = ((v[1] - rows[2:3, :] * log_rate) * sigmas[0]).T[: raw_out.shape[0], :]
    for copy in copies:
        copy.wait()


def add_body(*refs):
    count = len(refs) // 3
    for a, b, out in zip(refs[:count], refs[count : 2 * count], refs[2 * count :]):
        out[...] = a[...] + b[...]


def on_device(x_heads, target, b_proj, c_proj, dt_raw, a_log, skip_gain, dt_bias):
    heads, size, channels = x_heads.shape[1:]
    width = b_proj.shape[2]
    n = lax.axis_size("ctx")
    parts = lax.axis_size("head")
    chunks = min(CHUNKS, heads)
    starts = [-(-heads * i // chunks) for i in range(chunks + 1)]
    groups = [tuple(range(start, end)) for start, end in zip(starts, starts[1:])]
    square, all_states = shape((size, size), bf16), shape((heads, width, width), f32)
    flat = shape((width, size), bf16)

    def held_in_hbm(*arrays):
        return [pltpu.with_memory_space_constraint(a, pltpu.HBM) for a in arrays]

    def like(*arrays):
        return [shape(a.shape, a.dtype) for a in arrays]

    arrays = held_in_hbm(
        c_proj[0], dt_raw[0], a_log[None], skip_gain[None], dt_bias[None], b_proj[0], x_heads[0], target[0]
    )
    c, raw, a_log, skip_gain, dt_bias, b, x, t, own = call(
        load_body, like(*arrays) + [shape((size + heads * size // width, width), f32)], *arrays,
        ins=[HBM] * len(arrays), scratch=[pltpu.SemaphoreType.DMA((len(arrays),))], flops=10**6,
    )
    lowest = max(n // 2 - 1, 0)

    def exchange(value, links):
        to, width = dict(links), lax.axis_size("seq")
        if width % 2:
            return lax.ppermute(value, "ctx", links)
        places = [(i, j) for i in range(n) for j in range(width)]
        pairs = [(i * width + j, to[i] * width + j if i in to else i * width + (j ^ 1)) for i, j in places]
        return lax.ppermute(value, ("ctx", "seq"), pairs)

    def down(step, value):
        return exchange(value, [(i + 1, i) for i in range(lowest, n - step)] + [(lowest, n - step)])

    later = down(1, own) if n > 1 else own
    row, sheet = shape((8, width), f32), shape((size, width), f32)
    cols, low, b_t, c_t, rows, shifted = call(
        prepare_body, [shape((4, size, width), f32), square, flat, flat, row, sheet], b, c, raw, a_log, skip_gain, dt_bias
    )
    low_t, sq, sides, sigmas = call(
        prepare_more_body, [square, shape((width, size), f32), shape((width, 8), f32), shape((2, size, width), f32)],
        b, c, cols, rows, shifted,
    )
    held = []
    for group in groups:
        states, panel = shape((len(group), width, channels), f32), (len(group), size, channels)
        f, p, xr, y, err = call(
            functools.partial(first_body, group),
            [states, states, shape(panel, bf16), shape(panel, f32), shape(panel, f32)],
            x, t, cols, low, b_t, c_t, rows, flops=4 * 10**8,
        )
        zero = jnp.zeros(states.shape, f32)
        held.append(dict(f=f, p=p, xr=xr, y=y, err=err, s=zero, d=zero))
    held[0]["pay"], = call(send_body, like(held[0]["f"]), held[0]["f"], held[0]["p"])
    (m,) = call(own_map_body, [all_states], c, c_t, sq)
    for h in held[1:]:
        h["pay"], later = call(send_body, like(h["f"], later), h["f"], h["p"], later)
    layouts = [later]
    for step in range(2, n - lowest):
        layouts.append(down(step, layouts[-1]))

    def with_map(maps, layout):
        step = len(maps)
        mc, factor = call(
            functools.partial(later_map_body, step, lowest), [all_states, shape((heads, width), f32)], sides, layout,
            *(maps[-1] if step > 1 else ()),
        )
        return maps + [(mc, factor)]

    maps = [(jnp.zeros(all_states.shape, f32), None)]
    if n > 1:
        maps = with_map(maps, later)

    def swap(r):
        pairs = [(r - 1, r), (r, r - 1)]
        other = [(n - r, n - 1 - r), (n - 1 - r, n - r)]
        return pairs if r - 1 == n - 1 - r else pairs + other

    for stage in range(1, n - 1 + chunks):
        for i, h in enumerate(held):
            r = stage - i
            if not 1 <= r <= n - 1:
                continue
            if r > 1:
                relays = layouts[1:] if r == 2 and i == 0 else []
                h["pay"], h["s"], h["d"], *relays = call(
                    functools.partial(round_body, groups[i], n, r), like(h["f"]) * 3 + like(*relays),
                    h["f"], h["p"], m, maps[r - 1 if i == 0 and r < len(maps) else -1][0], rows, h["got"], h["s"], h["d"], *relays,
                )
                for relay in relays:
                    maps = with_map(maps, relay)
            h["got"] = exchange(h["pay"], swap(r))

    tokens = size * n * x_heads.shape[0] * lax.axis_size("seq")
    scales = (1.0 / tokens, 1.0 / (tokens * channels))
    cut = size if parts == 1 else size // 2
    v, total = jnp.zeros((2, size, width), f32), jnp.zeros((8, width), f32)
    grad_x = []
    for i, h in enumerate(held):
        final = i == chunks - 1
        gx, h["ew"], h["s_low"], h["a_low"], v, total = call(
            functools.partial(last_body, groups[i], scales if final else None),
            like(h["xr"]) + [shape((extent, len(groups[i]) * channels), bf16) for extent in (size, width, width)]
            + [shape(v.shape, f32), shape((8, width), f32)],
            x, cols, sigmas, low_t, b, c, rows, h["xr"], h["y"], h["err"], h["f"], maps[-1][0],
            h.get("got", h["s"]), h["s"], h["d"], v, total, flops=4 * 10**8,
        )
        grad_x.append(gx)
    (grads,) = call(
        functools.partial(project_body, chunks), [shape((2, size, width), f32)], b, c,
        *[h[part] for part in ("xr", "ew", "s_low", "a_low") for h in held], flops=4 * 10**8,
    )
    spans = {axis: lax.axis_size(axis) for axis in ("seq", "ctx")}
    swaps = [(axis, 1 << k) for axis in ("seq", "ctx") for k in range(spans[axis].bit_length() - 1)]

    def swapped(value, axis, by):
        return lax.ppermute(value, axis, [(i, i ^ by) for i in range(spans[axis])])

    halves, sums = shape((2, cut, width), f32), shape(total.shape, f32)
    firsts = [total]
    if ("seq", 1) in swaps:
        swaps.remove(("seq", 1))
        firsts.append(swapped(total, "seq", 1))
    keep, send, total = call(cut_body, [halves, halves, sums], grads, *firsts)
    grad_x, grad_raw = call(
        functools.partial(output_body, chunks), [shape((heads, size, channels), bf16), shape(raw.shape, f32)],
        *grad_x, sigmas, rows, v, out_specs=[HBM, VMEM], scratch=[pltpu.SemaphoreType.DMA((chunks,))],
    )
    step = parts // 2
    while step >= 1:
        received = lax.ppermute(send, "head", [(i, i ^ step) for i in range(parts)])
        if swaps:
            got = swapped(total, *swaps.pop())
            keep, total = call(add_body, [shape(keep.shape, f32), sums], keep, total, received, got)
        else:
            keep = keep + received
        step //= 2
        if step >= 1:
            cut = keep.shape[1] // 2
            upper = (lax.axis_index("head") // step) % 2 == 1
            keep, send = (
                jnp.where(upper, keep[:, cut:], keep[:, :cut]),
                jnp.where(upper, keep[:, :cut], keep[:, cut:]),
            )
    while swaps:
        total = total + swapped(total, *swaps.pop())
    return (
        grad_x[None], keep[0][None], keep[1][None], grad_raw[None],
        total[0, :heads], total[1, :heads], total[2, :heads],
    )


def solution(mesh):
    return jax.shard_map(
        on_device,
        mesh=mesh,
        in_specs=(
            P("seq", "head", "ctx", None),
            P("seq", "head", "ctx", None),
            P("seq", "ctx", None),
            P("seq", "ctx", None),
            P("seq", "head", "ctx"),
            P("head"),
            P("head"),
            P("head"),
        ),
        out_specs=(
            P("seq", "head", "ctx", None),
            P("seq", ("ctx", "head"), None),
            P("seq", ("ctx", "head"), None),
            P("seq", "head", "ctx"),
            P("head"),
            P("head"),
            P("head"),
        ),
        check_vma=False,
    )
```

```python
import functools
import jax
import jax.numpy as jnp
from jax import lax
from jax.experimental import pallas as pl
from jax.experimental.pallas import tpu as pltpu
from jax.sharding import PartitionSpec as P

CHUNKS = 2
f32, bf16 = jnp.float32, jnp.bfloat16
highest = lax.Precision.HIGHEST
VMEM = pl.BlockSpec(memory_space=pltpu.VMEM)
HBM = pl.BlockSpec(memory_space=pltpu.HBM)
LIMIT = 48 * 1024 * 1024
shape = jax.ShapeDtypeStruct


def dot(a, b):
    return jnp.dot(a, b, preferred_element_type=f32)


def dot_nt(a, b):
    return lax.dot_general(a, b, (((1,), (1,)), ((), ())), preferred_element_type=f32)


def call(body, outs, *args, flops=10**8, ins=None, out_specs=None, scratch=()):
    return pl.pallas_call(
        body,
        out_shape=outs,
        in_specs=ins or [VMEM] * len(args),
        out_specs=out_specs or [VMEM] * len(outs),
        scratch_shapes=scratch,
        compiler_params=pltpu.CompilerParams(vmem_limit_bytes=LIMIT),
        cost_estimate=pl.CostEstimate(flops=flops // 10**5, bytes_accessed=1 << 8, transcendentals=0),
    )(*args)


def triangle(size, lower):
    rows = lax.broadcasted_iota(jnp.int32, (size, size), 0)
    cols = lax.broadcasted_iota(jnp.int32, (size, size), 1)
    return rows >= cols if lower else cols >= rows


def head_row(values, width):
    heads = values.shape[1]
    rows = lax.broadcasted_iota(jnp.int32, (heads, width), 0)
    cols = lax.broadcasted_iota(jnp.int32, (heads, width), 1)
    spread = jnp.where(rows == cols, 1.0, 0.0).astype(f32)
    return jnp.dot(values, spread, precision=highest, preferred_element_type=f32)


def steps_of(raw, bias, rate, width):
    heads, size = raw.shape
    columns = jnp.concatenate([raw, jnp.zeros((width - heads, size), f32)], axis=0).T
    shifted = columns + bias
    dt = jnp.maximum(shifted, 0.0) + jnp.log1p(jnp.exp(-jnp.abs(shifted)))
    lower = jnp.where(triangle(size, True), 1.0, 0.0).astype(f32)
    return shifted, dt, jnp.dot(lower, -rate * dt, precision=highest, preferred_element_type=f32)


def fetch(pairs, sems):
    copies = [pltpu.make_async_copy(src, dst, sems.at[i]) for i, (src, dst) in enumerate(pairs)]
    for copy in copies:
        copy.start()
    return copies


def load_body(*refs):
    count = len(refs) // 2 - 1
    copies = fetch(zip(refs[:count], refs[count : 2 * count]), refs[-1])
    for copy in copies[:2]:
        copy.wait()
    (c, raw), own = refs[count : count + 2], refs[-2]
    size, state = c.shape
    heads = raw.shape[0]
    own[:size, :] = c[...].astype(f32)
    for s in range(size // state):
        own[size + s * heads : size + (s + 1) * heads, :] = raw[:, s * state : (s + 1) * state]
    for copy in copies[2:]:
        copy.wait()


def prepare_body(b, c, raw, a_log, skip, dt_bias, cols_out, low_out, b_t_out, c_t_out, rows_out, shifted_out):
    size, width = b.shape
    lanes = lax.broadcasted_iota(jnp.int32, (1, width), 1)
    rate = jnp.where(lanes < a_log.shape[1], jnp.exp(head_row(a_log[...], width)), 0.0)
    bias = head_row(dt_bias[...], width)
    shifted, dt, logs = steps_of(raw[...], bias, rate, width)
    mid = 0.5 * logs[size - 1 : size, :]
    cols_out[0] = jnp.exp(logs - mid)
    cols_out[1] = dt * jnp.exp(mid - logs)
    cols_out[2] = dt
    cols_out[3] = logs
    half = jnp.exp(mid)
    rows_out[...] = jnp.concatenate([half, half * half, rate, head_row(skip[...], width), bias, jnp.zeros((3, width), f32)], axis=0)
    shifted_out[...] = shifted
    low_out[...] = jnp.where(triangle(size, True), dot_nt(c[...], b[...]), 0.0).astype(bf16)
    b_t_out[...] = b[...].T
    c_t_out[...] = c[...].T


def prepare_more_body(b, c, cols, rows, shifted, low_t_out, sq_out, sides_out, sigmas_out):
    size = b.shape[0]
    low_t_out[...] = jnp.where(triangle(size, False), dot_nt(b[...], c[...]), 0.0).astype(bf16)
    sq_out[...] = jnp.exp(2.0 * cols[3]).T
    rate, bias = rows[2:3, :], rows[4:5, :]
    sides_out[...] = jnp.concatenate([rate, bias, jnp.zeros((6, rate.shape[1]), f32)], axis=0).T
    sigma = 1.0 / (1.0 + jnp.exp(-shifted[...]))
    lower = jnp.where(triangle(size, True), 1.0, 0.0).astype(f32)
    sigmas_out[0] = sigma
    sigmas_out[1] = jnp.dot(lower, rate * sigma, precision=highest, preferred_element_type=f32)


def side_by_side(parts):
    return jnp.concatenate(parts, axis=1)


def first_body(heads, x, t, cols, low, b_t, c_t, rows, f_out, p_out, pay_out, xr_out, y_out, err_out):
    first = lax.axis_index("ctx") == 0
    channels = x.shape[2]
    spans = [slice(k * channels, (k + 1) * channels) for k in range(len(heads))]
    for k, h in enumerate(heads):
        xr_out[k] = (x[h].astype(f32) * cols[1, :, h : h + 1]).astype(bf16)
    wide = side_by_side([xr_out[k] for k in range(len(heads))])
    y, contrib = dot(low[...], wide), dot(b_t[...], wide)
    weighted = []
    for k, h in enumerate(heads):
        g, skip = cols[0, :, h : h + 1], rows[3:4, h : h + 1]
        err = g * y[:, spans[k]] + skip * x[h].astype(f32) - t[h].astype(f32)
        y_out[k] = y[:, spans[k]]
        err_out[k] = err
        weighted.append((err * g).astype(bf16))
    pulled = dot(c_t[...], side_by_side(weighted))
    for k, h in enumerate(heads):
        scale = rows[0:1, h : h + 1]
        f, p = scale * contrib[:, spans[k]], scale * pulled[:, spans[k]]
        f_out[k] = f
        p_out[k] = p
        pay_out[k] = jnp.where(first, f, p)


def own_map_body(c, c_t, sq, m_out):
    wide = c_t[...].astype(f32)
    for h in range(m_out.shape[0]):
        m_out[h] = dot((wide * sq[h : h + 1, :]).astype(bf16), c[...])


def later_map_body(step, lowest, sides, got, *refs):
    before, (mc_out, factor_out) = refs[:-2], refs[-2:]
    heads, width = mc_out.shape[0], mc_out.shape[2]
    size = got.shape[0] * width // (width + heads)
    n, place = lax.axis_size("ctx"), lax.axis_index("ctx")
    needed = (place >= lowest) & (place < n - step)
    raw = jnp.concatenate([got[size + s * heads : size + (s + 1) * heads, :] for s in range(size // width)], axis=1)
    shifted = raw + sides[:heads, 1:2]
    dt = jnp.maximum(shifted, 0.0) + jnp.log1p(jnp.exp(-jnp.abs(shifted)))
    upper = jnp.where(triangle(size, False), 1.0, 0.0).astype(f32)
    logs = jnp.dot(-sides[:heads, 0:1] * dt, upper, precision=highest, preferred_element_type=f32)
    c = jnp.where(needed, got[:size, :], 0.0).astype(bf16)
    c_t = c.T.astype(f32)
    sq = jnp.exp(2.0 * logs)
    factor = before[1][:, 0:1] if before else jnp.ones((heads, 1), f32)
    for h in range(heads):
        added = factor[h : h + 1, :] * dot((c_t * sq[h : h + 1, :]).astype(bf16), c)
        mc_out[h] = before[0][h] + added if before else added
    factor_out[...] = jnp.broadcast_to(factor * sq[:, size - 1 : size], factor_out.shape)


def times(m, s):
    high = m.astype(bf16)
    low = (m - high.astype(f32)).astype(bf16)
    s_low = s.astype(bf16)
    return dot(side_by_side([high, low]), jnp.concatenate([s_low, s_low], axis=0))


def round_body(heads, n, r, f, p, m, mc, rows, got, s_in, d_in, *refs):
    relays = (len(refs) - 3) // 2
    pay_out, s_out, d_out = refs[relays : relays + 3]
    for relay, out in zip(refs[:relays], refs[relays + 3 :]):
        out[...] = relay[...]
    place = lax.axis_index("ctx")
    came_up, came_down = place == r - 1, place == n - r
    for k, h in enumerate(heads):
        s = jnp.where(came_up, got[k], s_in[k])
        d = jnp.where(came_down, got[k], d_in[k])
        s_out[k] = s
        d_out[k] = d
        total = rows[1:2, h : h + 1]
        after = total * s + f[k]
        full = p[k] + total * (d + times(mc[h], after))
        if n - r < r:
            full = full + times(m[h], s)
        pay_out[k] = jnp.where(place == r - 1, after, full)


def last_body(heads, scales, *refs):
    (x, cols, sigmas, low_t, b, c, rows, xr, y_in, err_in, f, mc, got, s_in, d_in, v_in, sums_in) = refs[:17]
    gx_out, ew_out, s_low_out, a_low_out, v_out, sums_out = refs[17:]
    n = lax.axis_size("ctx")
    place = lax.axis_index("ctx")
    size, width = b.shape
    channels = x.shape[2]
    lanes = lax.broadcasted_iota(jnp.int32, (1, width), 1)
    v_all, w_all = v_in[0], v_in[1]
    ends, skips = sums_in[0:1, :], sums_in[1:2, :]
    spans = [slice(k * channels, (k + 1) * channels) for k in range(len(heads))]
    states, adjoints = [], []
    for k, h in enumerate(heads):
        scale, total = rows[0:1, h : h + 1], rows[1:2, h : h + 1]
        s = jnp.where(place == n - 1, got[k], s_in[k]) if n > 1 else s_in[k]
        d = jnp.where(place == 0, got[k], d_in[k]) if n > 1 else d_in[k]
        after = total * s + f[k]
        adjoint = d + times(mc[h], after)
        states.append((scale * s).astype(bf16))
        adjoints.append((scale * adjoint).astype(bf16))
        ends = jnp.where(lanes == h, jnp.sum(jnp.sum(adjoint * after, axis=0, keepdims=True), axis=1, keepdims=True), ends)
    states, adjoints = side_by_side(states), side_by_side(adjoints)
    carried = dot(c[...], states)
    errs, weighted = [], []
    for k, h in enumerate(heads):
        g = cols[0, :, h : h + 1]
        errs.append(err_in[k] + g * carried[:, spans[k]])
        weighted.append((errs[k] * g).astype(bf16))
    wide = side_by_side(weighted)
    z = dot(low_t[...], wide) + dot(b[...], adjoints)
    for k, h in enumerate(heads):
        here, err, own = lanes == h, errs[k], z[:, spans[k]]
        y = y_in[k] + carried[:, spans[k]]
        gx_out[k] = (cols[1, :, h : h + 1] * own + rows[3:4, h : h + 1] * err).astype(bf16)
        v_all = jnp.where(here, jnp.sum(weighted[k].astype(f32) * y, axis=1, keepdims=True), v_all)
        w_all = jnp.where(here, jnp.sum(xr[k].astype(f32) * own, axis=1, keepdims=True), w_all)
        skips = jnp.where(here, jnp.sum(jnp.sum(err * x[h].astype(f32), axis=0, keepdims=True), axis=1, keepdims=True), skips)
    ew_out[...] = wide
    s_low_out[...] = states
    a_low_out[...] = adjoints
    if scales is None:
        v_out[0] = v_all
        v_out[1] = w_all
        sums_out[...] = jnp.concatenate([ends, skips, jnp.zeros((6, width), f32)], axis=0)
        return
    last = lax.broadcasted_iota(jnp.int32, (size, width), 0) == size - 1
    grad_logs = v_all - w_all + jnp.where(last, ends, 0.0)
    by_step = w_all / cols[2]
    v_out[0] = grad_logs
    v_out[1] = by_step
    alog = jnp.sum(grad_logs * cols[3], axis=0, keepdims=True)
    bias = jnp.sum(by_step * sigmas[0] - grad_logs * sigmas[1], axis=0, keepdims=True)
    sums_out[...] = jnp.concatenate(
        [alog * scales[0], skips * scales[1], bias * scales[0], jnp.zeros((5, width), f32)], axis=0
    )


def project_body(chunks, b, c, *refs):
    size = b.shape[0]
    grads_out = refs[-1]
    parts = [refs[i * chunks : (i + 1) * chunks] for i in range(4)]
    wide = jnp.concatenate([xr[k] for xr in parts[0] for k in range(xr.shape[0])], axis=1)
    ew, s_low, a_low = [jnp.concatenate([ref[...] for ref in part], axis=1) for part in parts[1:]]
    score = jnp.where(triangle(size, True), dot_nt(ew, wide), 0.0).astype(bf16)
    score_t = jnp.where(triangle(size, False), dot_nt(wide, ew), 0.0).astype(bf16)
    grads_out[0] = dot(score_t, c[...]) + dot_nt(wide, a_low)
    grads_out[1] = dot(score, b[...]) + dot_nt(ew, s_low)


def cut_body(grads, *refs):
    *sums, keep_out, send_out, sums_out = refs
    cut, size = keep_out.shape[1], grads.shape[1]
    upper = lax.axis_index("head") >= lax.axis_size("head") // 2
    for i in range(2):
        grad = grads[i]
        keep_out[i] = jnp.where(upper, grad[size - cut :, :], grad[:cut, :])
        send_out[i] = jnp.where(upper, grad[:cut, :], grad[size - cut :, :])
    sums_out[...] = sums[0][...] + sums[1][...] if len(sums) > 1 else sums[0][...]


def output_body(chunks, *refs):
    parts, (sigmas, rows, v), (gx_out, raw_out, sems) = refs[:chunks], refs[chunks : chunks + 3], refs[chunks + 3 :]
    size, starts = v.shape[1], [0]
    for part in parts:
        starts.append(starts[-1] + part.shape[0])
    copies = fetch([(part, gx_out.at[pl.ds(start, part.shape[0])]) for part, start in zip(parts, starts)], sems)
    later = jnp.where(triangle(size, False), 1.0, 0.0).astype(f32)
    log_rate = jnp.dot(later, v[0], precision=highest, preferred_element_type=f32)
    raw_out[...] = ((v[1] - rows[2:3, :] * log_rate) * sigmas[0]).T[: raw_out.shape[0], :]
    for copy in copies:
        copy.wait()


def add_body(*refs):
    count = len(refs) // 3
    for a, b, out in zip(refs[:count], refs[count : 2 * count], refs[2 * count :]):
        out[...] = a[...] + b[...]


def on_device(x_heads, target, b_proj, c_proj, dt_raw, a_log, skip_gain, dt_bias):
    heads, size, channels = x_heads.shape[1:]
    width = b_proj.shape[2]
    n = lax.axis_size("ctx")
    parts = lax.axis_size("head")
    chunks = min(CHUNKS, heads)
    starts = [-(-heads * i // chunks) for i in range(chunks + 1)]
    groups = [tuple(range(start, end)) for start, end in zip(starts, starts[1:])]
    square, all_states = shape((size, size), bf16), shape((heads, width, width), f32)
    flat = shape((width, size), bf16)

    def held_in_hbm(*arrays):
        return [pltpu.with_memory_space_constraint(a, pltpu.HBM) for a in arrays]

    def like(*arrays):
        return [shape(a.shape, a.dtype) for a in arrays]

    arrays = held_in_hbm(
        c_proj[0], dt_raw[0], a_log[None], skip_gain[None], dt_bias[None], b_proj[0], x_heads[0], target[0]
    )
    c, raw, a_log, skip_gain, dt_bias, b, x, t, own = call(
        load_body, like(*arrays) + [shape((size + heads * size // width, width), f32)], *arrays,
        ins=[HBM] * len(arrays), scratch=[pltpu.SemaphoreType.DMA((len(arrays),))], flops=10**6,
    )
    lowest = max(n // 2 - 1, 0)

    def exchange(value, links):
        to, width = dict(links), lax.axis_size("seq")
        if width % 2:
            return lax.ppermute(value, "ctx", links)
        places = [(i, j) for i in range(n) for j in range(width)]
        pairs = [(i * width + j, to[i] * width + j if i in to else i * width + (j ^ 1)) for i, j in places]
        return lax.ppermute(value, ("ctx", "seq"), pairs)

    def down(step, value):
        return exchange(value, [(i + 1, i) for i in range(lowest, n - step)] + [(lowest, n - step)])

    later = down(1, own) if n > 1 else own
    row, sheet = shape((8, width), f32), shape((size, width), f32)
    cols, low, b_t, c_t, rows, shifted = call(
        prepare_body, [shape((4, size, width), f32), square, flat, flat, row, sheet], b, c, raw, a_log, skip_gain, dt_bias
    )
    low_t, sq, sides, sigmas = call(
        prepare_more_body, [square, shape((width, size), f32), shape((width, 8), f32), shape((2, size, width), f32)],
        b, c, cols, rows, shifted,
    )
    held = []
    for group in groups:
        states, panel = shape((len(group), width, channels), f32), (len(group), size, channels)
        f, p, pay, xr, y, err = call(
            functools.partial(first_body, group),
            [states, states, states, shape(panel, bf16), shape(panel, f32), shape(panel, f32)],
            x, t, cols, low, b_t, c_t, rows, flops=4 * 10**8,
        )
        zero = jnp.zeros(states.shape, f32)
        held.append(dict(f=f, p=p, pay=pay, xr=xr, y=y, err=err, s=zero, d=zero))
    (m,) = call(own_map_body, [all_states], c, c_t, sq)
    layouts = [later]
    for step in range(2, n - lowest):
        layouts.append(down(step, layouts[-1]))

    def with_map(maps, layout):
        step = len(maps)
        mc, factor = call(
            functools.partial(later_map_body, step, lowest), [all_states, shape((heads, width), f32)], sides, layout,
            *(maps[-1] if step > 1 else ()),
        )
        return maps + [(mc, factor)]

    maps = [(jnp.zeros(all_states.shape, f32), None)]
    if n > 1:
        maps = with_map(maps, later)

    def swap(r):
        pairs = [(r - 1, r), (r, r - 1)]
        other = [(n - r, n - 1 - r), (n - 1 - r, n - r)]
        return pairs if r - 1 == n - 1 - r else pairs + other

    for stage in range(1, n - 1 + chunks):
        for i, h in enumerate(held):
            r = stage - i
            if not 1 <= r <= n - 1:
                continue
            if r > 1:
                relays = layouts[1:] if r == 2 and i == 0 else []
                h["pay"], h["s"], h["d"], *relays = call(
                    functools.partial(round_body, groups[i], n, r), like(h["f"]) * 3 + like(*relays),
                    h["f"], h["p"], m, maps[r - 1 if i == 0 and r < len(maps) else -1][0], rows, h["got"], h["s"], h["d"], *relays,
                )
                for relay in relays:
                    maps = with_map(maps, relay)
            h["got"] = exchange(h["pay"], swap(r))

    tokens = size * n * x_heads.shape[0] * lax.axis_size("seq")
    scales = (1.0 / tokens, 1.0 / (tokens * channels))
    cut = size if parts == 1 else size // 2
    v, total = jnp.zeros((2, size, width), f32), jnp.zeros((8, width), f32)
    grad_x = []
    for i, h in enumerate(held):
        final = i == chunks - 1
        gx, h["ew"], h["s_low"], h["a_low"], v, total = call(
            functools.partial(last_body, groups[i], scales if final else None),
            like(h["xr"]) + [shape((extent, len(groups[i]) * channels), bf16) for extent in (size, width, width)]
            + [shape(v.shape, f32), shape((8, width), f32)],
            x, cols, sigmas, low_t, b, c, rows, h["xr"], h["y"], h["err"], h["f"], maps[-1][0],
            h.get("got", h["s"]), h["s"], h["d"], v, total, flops=4 * 10**8,
        )
        grad_x.append(gx)
    (grads,) = call(
        functools.partial(project_body, chunks), [shape((2, size, width), f32)], b, c,
        *[h[part] for part in ("xr", "ew", "s_low", "a_low") for h in held], flops=4 * 10**8,
    )
    spans = {axis: lax.axis_size(axis) for axis in ("seq", "ctx")}
    swaps = [(axis, 1 << k) for axis in ("seq", "ctx") for k in range(spans[axis].bit_length() - 1)]

    def swapped(value, axis, by):
        return lax.ppermute(value, axis, [(i, i ^ by) for i in range(spans[axis])])

    halves, sums = shape((2, cut, width), f32), shape(total.shape, f32)
    firsts = [total]
    if ("seq", 1) in swaps:
        swaps.remove(("seq", 1))
        firsts.append(swapped(total, "seq", 1))
    keep, send, total = call(cut_body, [halves, halves, sums], grads, *firsts)
    grad_x, grad_raw = call(
        functools.partial(output_body, chunks), [shape((heads, size, channels), bf16), shape(raw.shape, f32)],
        *grad_x, sigmas, rows, v, out_specs=[HBM, VMEM], scratch=[pltpu.SemaphoreType.DMA((chunks,))],
    )
    step = parts // 2
    while step >= 1:
        received = lax.ppermute(send, "head", [(i, i ^ step) for i in range(parts)])
        if swaps:
            got = swapped(total, *swaps.pop())
            keep, total = call(add_body, [shape(keep.shape, f32), sums], keep, total, received, got)
        else:
            keep = keep + received
        step //= 2
        if step >= 1:
            cut = keep.shape[1] // 2
            upper = (lax.axis_index("head") // step) % 2 == 1
            keep, send = (
                jnp.where(upper, keep[:, cut:], keep[:, :cut]),
                jnp.where(upper, keep[:, :cut], keep[:, cut:]),
            )
    while swaps:
        total = total + swapped(total, *swaps.pop())
    return (
        grad_x[None], keep[0][None], keep[1][None], grad_raw[None],
        total[0, :heads], total[1, :heads], total[2, :heads],
    )


def solution(mesh):
    return jax.shard_map(
        on_device,
        mesh=mesh,
        in_specs=(
            P("seq", "head", "ctx", None),
            P("seq", "head", "ctx", None),
            P("seq", "ctx", None),
            P("seq", "ctx", None),
            P("seq", "head", "ctx"),
            P("head"),
            P("head"),
            P("head"),
        ),
        out_specs=(
            P("seq", "head", "ctx", None),
            P("seq", ("ctx", "head"), None),
            P("seq", ("ctx", "head"), None),
            P("seq", "head", "ctx"),
            P("head"),
            P("head"),
            P("head"),
        ),
        check_vma=False,
    )
```

```python
import functools
import jax
import jax.numpy as jnp
from jax import lax
from jax.experimental import pallas as pl
from jax.experimental.pallas import tpu as pltpu
from jax.sharding import PartitionSpec as P

CHUNKS = 2
f32, bf16 = jnp.float32, jnp.bfloat16
highest = lax.Precision.HIGHEST
VMEM = pl.BlockSpec(memory_space=pltpu.VMEM)
HBM = pl.BlockSpec(memory_space=pltpu.HBM)
LIMIT = 48 * 1024 * 1024
shape = jax.ShapeDtypeStruct


def dot(a, b):
    return jnp.dot(a, b, preferred_element_type=f32)


def dot_nt(a, b):
    return lax.dot_general(a, b, (((1,), (1,)), ((), ())), preferred_element_type=f32)


def call(body, outs, *args, flops=10**8, ins=None, out_specs=None, scratch=()):
    return pl.pallas_call(
        body,
        out_shape=outs,
        in_specs=ins or [VMEM] * len(args),
        out_specs=out_specs or [VMEM] * len(outs),
        scratch_shapes=scratch,
        compiler_params=pltpu.CompilerParams(vmem_limit_bytes=LIMIT),
        cost_estimate=pl.CostEstimate(flops=flops // 10**5, bytes_accessed=1 << 8, transcendentals=0),
    )(*args)


def triangle(size, lower):
    rows = lax.broadcasted_iota(jnp.int32, (size, size), 0)
    cols = lax.broadcasted_iota(jnp.int32, (size, size), 1)
    return rows >= cols if lower else cols >= rows


def head_row(values, width):
    heads = values.shape[1]
    rows = lax.broadcasted_iota(jnp.int32, (heads, width), 0)
    cols = lax.broadcasted_iota(jnp.int32, (heads, width), 1)
    spread = jnp.where(rows == cols, 1.0, 0.0).astype(f32)
    return jnp.dot(values, spread, precision=highest, preferred_element_type=f32)


def steps_of(raw, bias, rate, width):
    heads, size = raw.shape
    columns = jnp.concatenate([raw, jnp.zeros((width - heads, size), f32)], axis=0).T
    shifted = columns + bias
    dt = jnp.maximum(shifted, 0.0) + jnp.log1p(jnp.exp(-jnp.abs(shifted)))
    lower = jnp.where(triangle(size, True), 1.0, 0.0).astype(f32)
    return shifted, dt, jnp.dot(lower, -rate * dt, precision=highest, preferred_element_type=f32)


def fetch(pairs, sems):
    copies = [pltpu.make_async_copy(src, dst, sems.at[i]) for i, (src, dst) in enumerate(pairs)]
    for copy in copies:
        copy.start()
    return copies


def load_body(*refs):
    count = len(refs) // 2 - 1
    copies = fetch(zip(refs[:count], refs[count : 2 * count]), refs[-1])
    for copy in copies[:2]:
        copy.wait()
    (c, raw), own = refs[count : count + 2], refs[-2]
    size, state = c.shape
    heads = raw.shape[0]
    own[:size, :] = c[...].astype(f32)
    for s in range(size // state):
        own[size + s * heads : size + (s + 1) * heads, :] = raw[:, s * state : (s + 1) * state]
    for copy in copies[2:]:
        copy.wait()


def prepare_body(b, c, raw, a_log, skip, dt_bias, cols_out, low_out, b_t_out, c_t_out, rows_out, shifted_out):
    size, width = b.shape
    lanes = lax.broadcasted_iota(jnp.int32, (1, width), 1)
    rate = jnp.where(lanes < a_log.shape[1], jnp.exp(head_row(a_log[...], width)), 0.0)
    bias = head_row(dt_bias[...], width)
    shifted, dt, logs = steps_of(raw[...], bias, rate, width)
    mid = 0.5 * logs[size - 1 : size, :]
    cols_out[0] = jnp.exp(logs - mid)
    cols_out[1] = dt * jnp.exp(mid - logs)
    cols_out[2] = dt
    cols_out[3] = logs
    half = jnp.exp(mid)
    rows_out[...] = jnp.concatenate([half, half * half, rate, head_row(skip[...], width), bias, jnp.zeros((3, width), f32)], axis=0)
    shifted_out[...] = shifted
    low_out[...] = jnp.where(triangle(size, True), dot_nt(c[...], b[...]), 0.0).astype(bf16)
    b_t_out[...] = b[...].T
    c_t_out[...] = c[...].T


def prepare_more_body(b, c, cols, rows, shifted, low_t_out, sq_out, sides_out, sigmas_out):
    size = b.shape[0]
    low_t_out[...] = jnp.where(triangle(size, False), dot_nt(b[...], c[...]), 0.0).astype(bf16)
    sq_out[...] = jnp.exp(2.0 * cols[3]).T
    rate, bias = rows[2:3, :], rows[4:5, :]
    sides_out[...] = jnp.concatenate([rate, bias, jnp.zeros((6, rate.shape[1]), f32)], axis=0).T
    sigma = 1.0 / (1.0 + jnp.exp(-shifted[...]))
    lower = jnp.where(triangle(size, True), 1.0, 0.0).astype(f32)
    sigmas_out[0] = sigma
    sigmas_out[1] = jnp.dot(lower, rate * sigma, precision=highest, preferred_element_type=f32)


def side_by_side(parts):
    return jnp.concatenate(parts, axis=1)


def first_body(heads, x, t, cols, low, b_t, c_t, rows, f_out, p_out, pay_out, xr_out, y_out, err_out):
    first = lax.axis_index("ctx") == 0
    channels = x.shape[2]
    spans = [slice(k * channels, (k + 1) * channels) for k in range(len(heads))]
    for k, h in enumerate(heads):
        xr_out[k] = (x[h].astype(f32) * cols[1, :, h : h + 1]).astype(bf16)
    wide = side_by_side([xr_out[k] for k in range(len(heads))])
    y, contrib = dot(low[...], wide), dot(b_t[...], wide)
    weighted = []
    for k, h in enumerate(heads):
        g, skip = cols[0, :, h : h + 1], rows[3:4, h : h + 1]
        err = g * y[:, spans[k]] + skip * x[h].astype(f32) - t[h].astype(f32)
        y_out[k] = y[:, spans[k]]
        err_out[k] = err
        weighted.append((err * g).astype(bf16))
    pulled = dot(c_t[...], side_by_side(weighted))
    for k, h in enumerate(heads):
        scale = rows[0:1, h : h + 1]
        f, p = scale * contrib[:, spans[k]], scale * pulled[:, spans[k]]
        f_out[k] = f
        p_out[k] = p
        pay_out[k] = jnp.where(first, f, p)


def own_map_body(c, c_t, sq, m_out):
    wide = c_t[...].astype(f32)
    for h in range(m_out.shape[0]):
        m_out[h] = dot((wide * sq[h : h + 1, :]).astype(bf16), c[...])


def later_map_body(step, lowest, sides, got, *refs):
    before, (mc_out, factor_out) = refs[:-2], refs[-2:]
    heads, width = mc_out.shape[0], mc_out.shape[2]
    size = got.shape[0] * width // (width + heads)
    n, place = lax.axis_size("ctx"), lax.axis_index("ctx")
    needed = (place >= lowest) & (place < n - step)
    raw = jnp.concatenate([got[size + s * heads : size + (s + 1) * heads, :] for s in range(size // width)], axis=1)
    shifted = raw + sides[:heads, 1:2]
    dt = jnp.maximum(shifted, 0.0) + jnp.log1p(jnp.exp(-jnp.abs(shifted)))
    upper = jnp.where(triangle(size, False), 1.0, 0.0).astype(f32)
    logs = jnp.dot(-sides[:heads, 0:1] * dt, upper, precision=highest, preferred_element_type=f32)
    c = jnp.where(needed, got[:size, :], 0.0).astype(bf16)
    c_t = c.T.astype(f32)
    sq = jnp.exp(2.0 * logs)
    factor = before[1][:, 0:1] if before else jnp.ones((heads, 1), f32)
    for h in range(heads):
        added = factor[h : h + 1, :] * dot((c_t * sq[h : h + 1, :]).astype(bf16), c)
        mc_out[h] = before[0][h] + added if before else added
    factor_out[...] = jnp.broadcast_to(factor * sq[:, size - 1 : size], factor_out.shape)


def times(m, s):
    high = m.astype(bf16)
    low = (m - high.astype(f32)).astype(bf16)
    s_low = s.astype(bf16)
    return dot(side_by_side([high, low]), jnp.concatenate([s_low, s_low], axis=0))


def round_body(heads, n, r, f, p, m, mc, rows, got, s_in, d_in, *refs):
    relays = (len(refs) - 3) // 2
    pay_out, s_out, d_out = refs[relays : relays + 3]
    for relay, out in zip(refs[:relays], refs[relays + 3 :]):
        out[...] = relay[...]
    place = lax.axis_index("ctx")
    came_up, came_down = place == r - 1, place == n - r
    for k, h in enumerate(heads):
        s = jnp.where(came_up, got[k], s_in[k])
        d = jnp.where(came_down, got[k], d_in[k])
        s_out[k] = s
        d_out[k] = d
        total = rows[1:2, h : h + 1]
        after = total * s + f[k]
        full = p[k] + total * (d + times(mc[h], after))
        if n - r < r:
            full = full + times(m[h], s)
        pay_out[k] = jnp.where(place == r - 1, after, full)


def last_body(heads, scales, *refs):
    (x, cols, sigmas, low_t, b, c, rows, xr, y_in, err_in, f, mc, got, s_in, d_in, v_in, sums_in) = refs[:17]
    gx_out, ew_out, s_low_out, a_low_out, v_out, sums_out = refs[17:]
    n = lax.axis_size("ctx")
    place = lax.axis_index("ctx")
    size, width = b.shape
    channels = x.shape[2]
    lanes = lax.broadcasted_iota(jnp.int32, (1, width), 1)
    v_all, w_all = v_in[0], v_in[1]
    ends, skips = sums_in[0:1, :], sums_in[1:2, :]
    spans = [slice(k * channels, (k + 1) * channels) for k in range(len(heads))]
    states, adjoints = [], []
    for k, h in enumerate(heads):
        scale, total = rows[0:1, h : h + 1], rows[1:2, h : h + 1]
        s = jnp.where(place == n - 1, got[k], s_in[k]) if n > 1 else s_in[k]
        d = jnp.where(place == 0, got[k], d_in[k]) if n > 1 else d_in[k]
        after = total * s + f[k]
        adjoint = d + times(mc[h], after)
        states.append((scale * s).astype(bf16))
        adjoints.append((scale * adjoint).astype(bf16))
        ends = jnp.where(lanes == h, jnp.sum(jnp.sum(adjoint * after, axis=0, keepdims=True), axis=1, keepdims=True), ends)
    states, adjoints = side_by_side(states), side_by_side(adjoints)
    carried = dot(c[...], states)
    errs, weighted = [], []
    for k, h in enumerate(heads):
        g = cols[0, :, h : h + 1]
        errs.append(err_in[k] + g * carried[:, spans[k]])
        weighted.append((errs[k] * g).astype(bf16))
    wide = side_by_side(weighted)
    z = dot(low_t[...], wide) + dot(b[...], adjoints)
    for k, h in enumerate(heads):
        here, err, own = lanes == h, errs[k], z[:, spans[k]]
        y = y_in[k] + carried[:, spans[k]]
        gx_out[k] = (cols[1, :, h : h + 1] * own + rows[3:4, h : h + 1] * err).astype(bf16)
        v_all = jnp.where(here, jnp.sum(weighted[k].astype(f32) * y, axis=1, keepdims=True), v_all)
        w_all = jnp.where(here, jnp.sum(xr[k].astype(f32) * own, axis=1, keepdims=True), w_all)
        skips = jnp.where(here, jnp.sum(jnp.sum(err * x[h].astype(f32), axis=0, keepdims=True), axis=1, keepdims=True), skips)
    ew_out[...] = wide
    s_low_out[...] = states
    a_low_out[...] = adjoints
    if scales is None:
        v_out[0] = v_all
        v_out[1] = w_all
        sums_out[...] = jnp.concatenate([ends, skips, jnp.zeros((6, width), f32)], axis=0)
        return
    last = lax.broadcasted_iota(jnp.int32, (size, width), 0) == size - 1
    grad_logs = v_all - w_all + jnp.where(last, ends, 0.0)
    by_step = w_all / cols[2]
    v_out[0] = grad_logs
    v_out[1] = by_step
    alog = jnp.sum(grad_logs * cols[3], axis=0, keepdims=True)
    bias = jnp.sum(by_step * sigmas[0] - grad_logs * sigmas[1], axis=0, keepdims=True)
    sums_out[...] = jnp.concatenate(
        [alog * scales[0], skips * scales[1], bias * scales[0], jnp.zeros((5, width), f32)], axis=0
    )


def project_body(chunks, b, c, *refs):
    size = b.shape[0]
    grads_out = refs[-1]
    parts = [refs[i * chunks : (i + 1) * chunks] for i in range(4)]
    wide = jnp.concatenate([xr[k] for xr in parts[0] for k in range(xr.shape[0])], axis=1)
    ew, s_low, a_low = [jnp.concatenate([ref[...] for ref in part], axis=1) for part in parts[1:]]
    score = jnp.where(triangle(size, True), dot_nt(ew, wide), 0.0).astype(bf16)
    score_t = jnp.where(triangle(size, False), dot_nt(wide, ew), 0.0).astype(bf16)
    grads_out[0] = dot(score_t, c[...]) + dot_nt(wide, a_low)
    grads_out[1] = dot(score, b[...]) + dot_nt(ew, s_low)


def cut_body(grads, *refs):
    *sums, keep_out, send_out, sums_out = refs
    cut, size = keep_out.shape[1], grads.shape[1]
    upper = lax.axis_index("head") >= lax.axis_size("head") // 2
    for i in range(2):
        grad = grads[i]
        keep_out[i] = jnp.where(upper, grad[size - cut :, :], grad[:cut, :])
        send_out[i] = jnp.where(upper, grad[:cut, :], grad[size - cut :, :])
    sums_out[...] = sums[0][...] + sums[1][...] if len(sums) > 1 else sums[0][...]


def output_body(chunks, *refs):
    parts, (sigmas, rows, v), (gx_out, raw_out, sems) = refs[:chunks], refs[chunks : chunks + 3], refs[chunks + 3 :]
    size, starts = v.shape[1], [0]
    for part in parts:
        starts.append(starts[-1] + part.shape[0])
    copies = fetch([(part, gx_out.at[pl.ds(start, part.shape[0])]) for part, start in zip(parts, starts)], sems)
    later = jnp.where(triangle(size, False), 1.0, 0.0).astype(f32)
    log_rate = jnp.dot(later, v[0], precision=highest, preferred_element_type=f32)
    raw_out[...] = ((v[1] - rows[2:3, :] * log_rate) * sigmas[0]).T[: raw_out.shape[0], :]
    for copy in copies:
        copy.wait()


def add_body(*refs):
    count = len(refs) // 3
    for a, b, out in zip(refs[:count], refs[count : 2 * count], refs[2 * count :]):
        out[...] = a[...] + b[...]


def on_device(x_heads, target, b_proj, c_proj, dt_raw, a_log, skip_gain, dt_bias):
    heads, size, channels = x_heads.shape[1:]
    width = b_proj.shape[2]
    n = lax.axis_size("ctx")
    parts = lax.axis_size("head")
    chunks = min(CHUNKS, heads)
    starts = [-(-heads * i // chunks) for i in range(chunks + 1)]
    groups = [tuple(range(start, end)) for start, end in zip(starts, starts[1:])]
    square, all_states = shape((size, size), bf16), shape((heads, width, width), f32)
    flat = shape((width, size), bf16)

    def held_in_hbm(*arrays):
        return [pltpu.with_memory_space_constraint(a, pltpu.HBM) for a in arrays]

    def like(*arrays):
        return [shape(a.shape, a.dtype) for a in arrays]

    arrays = held_in_hbm(
        c_proj[0], dt_raw[0], a_log[None], skip_gain[None], dt_bias[None], b_proj[0], x_heads[0], target[0]
    )
    c, raw, a_log, skip_gain, dt_bias, b, x, t, own = call(
        load_body, like(*arrays) + [shape((size + heads * size // width, width), f32)], *arrays,
        ins=[HBM] * len(arrays), scratch=[pltpu.SemaphoreType.DMA((len(arrays),))], flops=10**6,
    )
    lowest = max(n // 2 - 1, 0)

    def exchange(value, links):
        to, width = dict(links), lax.axis_size("seq")
        if width % 2:
            return lax.ppermute(value, "ctx", links)
        places = [(i, j) for i in range(n) for j in range(width)]
        pairs = [(i * width + j, to[i] * width + j if i in to else i * width + (j ^ 1)) for i, j in places]
        return lax.ppermute(value, ("ctx", "seq"), pairs)

    def down(step, value):
        return exchange(value, [(i + 1, i) for i in range(lowest, n - step)] + [(lowest, n - step)])

    later = down(1, own) if n > 1 else own
    row, sheet = shape((8, width), f32), shape((size, width), f32)
    cols, low, b_t, c_t, rows, shifted = call(
        prepare_body, [shape((4, size, width), f32), square, flat, flat, row, sheet], b, c, raw, a_log, skip_gain, dt_bias
    )
    low_t, sq, sides, sigmas = call(
        prepare_more_body, [square, shape((width, size), f32), shape((width, 8), f32), shape((2, size, width), f32)],
        b, c, cols, rows, shifted,
    )
    held = []
    for group in groups:
        states, panel = shape((len(group), width, channels), f32), (len(group), size, channels)
        f, p, pay, xr, y, err = call(
            functools.partial(first_body, group),
            [states, states, states, shape(panel, bf16), shape(panel, f32), shape(panel, f32)],
            x, t, cols, low, b_t, c_t, rows, flops=4 * 10**8,
        )
        zero = jnp.zeros(states.shape, f32)
        held.append(dict(f=f, p=p, pay=pay, xr=xr, y=y, err=err, s=zero, d=zero))
    (m,) = call(own_map_body, [all_states], c, c_t, sq)
    layouts = [later]
    for step in range(2, n - lowest):
        layouts.append(down(step, layouts[-1]))

    def with_map(maps, layout):
        step = len(maps)
        mc, factor = call(
            functools.partial(later_map_body, step, lowest), [all_states, shape((heads, width), f32)], sides, layout,
            *(maps[-1] if step > 1 else ()),
        )
        return maps + [(mc, factor)]

    maps = [(jnp.zeros(all_states.shape, f32), None)]
    if n > 1:
        maps = with_map(maps, later)

    def swap(r):
        pairs = [(r - 1, r), (r, r - 1)]
        other = [(n - r, n - 1 - r), (n - 1 - r, n - r)]
        return pairs if r - 1 == n - 1 - r else pairs + other

    for stage in range(1, n - 1 + chunks):
        for i, h in enumerate(held):
            r = stage - i
            if not 1 <= r <= n - 1:
                continue
            if r > 1:
                relays = layouts[1:] if r == 2 and i == 0 else []
                h["pay"], h["s"], h["d"], *relays = call(
                    functools.partial(round_body, groups[i], n, r), like(h["f"]) * 3 + like(*relays),
                    h["f"], h["p"], m, maps[r - 1 if i == 0 and r < len(maps) else -1][0], rows, h["got"], h["s"], h["d"], *relays,
                )
                for relay in relays:
                    maps = with_map(maps, relay)
            if r == 1 and i and len(groups[i]) > 1:
                half = len(groups[i]) // 2
                one_way = sorted({(r - 1, r), (n - r, n - 1 - r)})
                parts_of = (h["pay"][:half], h["pay"][half:])
                h["got"] = jnp.concatenate([lax.ppermute(part, "ctx", one_way) for part in parts_of], axis=0)
            else:
                h["got"] = exchange(h["pay"], swap(r))

    tokens = size * n * x_heads.shape[0] * lax.axis_size("seq")
    scales = (1.0 / tokens, 1.0 / (tokens * channels))
    cut = size if parts == 1 else size // 2
    v, total = jnp.zeros((2, size, width), f32), jnp.zeros((8, width), f32)
    grad_x = []
    for i, h in enumerate(held):
        final = i == chunks - 1
        gx, h["ew"], h["s_low"], h["a_low"], v, total = call(
            functools.partial(last_body, groups[i], scales if final else None),
            like(h["xr"]) + [shape((extent, len(groups[i]) * channels), bf16) for extent in (size, width, width)]
            + [shape(v.shape, f32), shape((8, width), f32)],
            x, cols, sigmas, low_t, b, c, rows, h["xr"], h["y"], h["err"], h["f"], maps[-1][0],
            h.get("got", h["s"]), h["s"], h["d"], v, total, flops=4 * 10**8,
        )
        grad_x.append(gx)
    (grads,) = call(
        functools.partial(project_body, chunks), [shape((2, size, width), f32)], b, c,
        *[h[part] for part in ("xr", "ew", "s_low", "a_low") for h in held], flops=4 * 10**8,
    )
    spans = {axis: lax.axis_size(axis) for axis in ("seq", "ctx")}
    swaps = [(axis, 1 << k) for axis in ("seq", "ctx") for k in range(spans[axis].bit_length() - 1)]

    def swapped(value, axis, by):
        return lax.ppermute(value, axis, [(i, i ^ by) for i in range(spans[axis])])

    halves, sums = shape((2, cut, width), f32), shape(total.shape, f32)
    firsts = [total]
    if ("seq", 1) in swaps:
        swaps.remove(("seq", 1))
        firsts.append(swapped(total, "seq", 1))
    keep, send, total = call(cut_body, [halves, halves, sums], grads, *firsts)
    grad_x, grad_raw = call(
        functools.partial(output_body, chunks), [shape((heads, size, channels), bf16), shape(raw.shape, f32)],
        *grad_x, sigmas, rows, v, out_specs=[HBM, VMEM], scratch=[pltpu.SemaphoreType.DMA((chunks,))],
    )
    step = parts // 2
    while step >= 1:
        received = lax.ppermute(send, "head", [(i, i ^ step) for i in range(parts)])
        if swaps:
            got = swapped(total, *swaps.pop())
            keep, total = call(add_body, [shape(keep.shape, f32), sums], keep, total, received, got)
        else:
            keep = keep + received
        step //= 2
        if step >= 1:
            cut = keep.shape[1] // 2
            upper = (lax.axis_index("head") // step) % 2 == 1
            keep, send = (
                jnp.where(upper, keep[:, cut:], keep[:, :cut]),
                jnp.where(upper, keep[:, :cut], keep[:, cut:]),
            )
    while swaps:
        total = total + swapped(total, *swaps.pop())
    return (
        grad_x[None], keep[0][None], keep[1][None], grad_raw[None],
        total[0, :heads], total[1, :heads], total[2, :heads],
    )


def solution(mesh):
    return jax.shard_map(
        on_device,
        mesh=mesh,
        in_specs=(
            P("seq", "head", "ctx", None),
            P("seq", "head", "ctx", None),
            P("seq", "ctx", None),
            P("seq", "ctx", None),
            P("seq", "head", "ctx"),
            P("head"),
            P("head"),
            P("head"),
        ),
        out_specs=(
            P("seq", "head", "ctx", None),
            P("seq", ("ctx", "head"), None),
            P("seq", ("ctx", "head"), None),
            P("seq", "head", "ctx"),
            P("head"),
            P("head"),
            P("head"),
        ),
        check_vma=False,
    )
```
